32 devices in a mesh: ctx: 8 (over z, core), fsdp: 4 (over y, x).
Axes of the slice: x: 2, y: 2, z: 4, core: 2. Of those that a mesh axis runs over, the one named last changes fastest.
Arguments:
- hidden_in: bfloat16 [4, 2048, 2048], P('fsdp', 'ctx'), may hold values from -6 to 6
- out_grad: bfloat16 [4, 2048, 2048], P('fsdp', 'ctx'), may hold values from -6 to 6
- lengths: int32 [4, 2], P('fsdp'), may hold values from 682 to 1024, as said below
- block_order: int32 [4, 16], P('fsdp'), may hold values from 0 to 15, as said below
- ln_gain: bfloat16 [2048], P('fsdp'), may hold values from 0.25 to 1.75
- ln_bias: bfloat16 [2048], P('fsdp'), may hold values from -2 to 2
- w_qkv: bfloat16 [2048, 6144], P('fsdp'), may hold values from -0.125 to 0.125
- b_qkv: bfloat16 [6144], P('fsdp'), may hold values from -2 to 2
- w_out: bfloat16 [2048, 2048], P('fsdp'), may hold values from -2 to 2
- w_gate: bfloat16 [2048, 5632], P('fsdp'), may hold values from -0.125 to 0.125
- w_up: bfloat16 [2048, 5632], P('fsdp'), may hold values from -0.125 to 0.125
- w_down: bfloat16 [5632, 2048], P('fsdp'), may hold values from -0.078125 to 0.078125
Outputs:
- output: bfloat16 [4, 2048, 2048], P('fsdp', 'ctx')
- input_grad: bfloat16 [4, 2048, 2048], P('fsdp', 'ctx')
- grad_ln_gain: float32 [2048], P('fsdp')
- grad_ln_bias: float32 [2048], P('fsdp')
- grad_w_qkv: float32 [2048, 6144], P('fsdp')
- grad_b_qkv: float32 [6144], P('fsdp')
- grad_w_out: float32 [2048, 2048], P('fsdp')
- grad_w_gate: float32 [2048, 5632], P('fsdp')
- grad_w_up: float32 [2048, 5632], P('fsdp')
- grad_w_down: float32 [5632, 2048], P('fsdp')
The draws below stay inside these ranges and needn't reach their ends.
Inputs may be any that keep to these rules, and one draw needn't show every extreme that they name: Each group's 2 lengths sum to 2048; each is at least 682; in every group at least one sequence has the greatest length, at a position that varies. `block_order`: each group's row is a permutation of 0 to 15 whose entries 2 c and 2 c + 1 sum to 15.
All inputs are finite; a program needn't handle non-finite values.
Results may differ from the reference program's by a relative error of at most 0.012.
Values may be sent and summed in bfloat16 or wider, within the bound.
No kernel may reach another device: no remote copies, remote signals or barrier semaphores. Data moves between devices by JAX's collectives and lax.ppermute only.
A program may use at most 576 MiB of HBM per device.

```python
from functools import partial
import jax
import jax.numpy as jnp
from jax import lax

D = 2048
H = 32
HD = 64
ROT = 16
FF = 5632
BLOCK = 128
GROUP_TOK = 2048
GROUPS = 4
GROUP_BLOCKS = 16
SEQS = 2
SHORTEST = 682


def draw_lengths(key, part):
    key = jax.random.fold_in(key, 7)
    cut_key, place_key = jax.random.split(key, 2)
    spare = GROUP_TOK - SEQS * SHORTEST
    long_extra = (spare + 1) // 2
    rest_spare = spare - long_extra
    cuts = jnp.sort(jax.random.randint(cut_key, (GROUPS, SEQS - 2), 0, rest_spare + 1), axis=1).astype(jnp.int32)
    zeros_col = jnp.zeros((GROUPS, 1), jnp.int32)
    spare_col = jnp.full((GROUPS, 1), rest_spare, jnp.int32)
    edges = jnp.concatenate([zeros_col, cuts, spare_col], axis=1)
    others = (SHORTEST + edges[:, 1:] - edges[:, :-1]).astype(jnp.int32)
    longest_col = jnp.full((GROUPS, 1), SHORTEST + long_extra, jnp.int32)
    ordered = jnp.concatenate([longest_col, others], axis=1).astype(jnp.int32)
    shifts = jax.random.randint(place_key, (GROUPS, 1), 0, SEQS).astype(jnp.int32)
    picks = ((jnp.arange(SEQS, dtype=jnp.int32)[None, :] + shifts) % SEQS).astype(jnp.int32)
    return jnp.take_along_axis(ordered, picks, axis=1).astype(jnp.int32)


def draw_block_order(key, part):
    key = jax.random.fold_in(key, 13)
    pair_count = GROUP_BLOCKS // 2
    first_key, second_key = jax.random.split(key, 2)
    scores = jax.random.randint(first_key, (GROUPS, pair_count), 0, 1 << 20)
    scores = scores * pair_count + jnp.arange(pair_count, dtype=jnp.int32)[None, :]
    pairs = jnp.argsort(scores, axis=1, stable=True).astype(jnp.int32)
    flips = jax.random.randint(second_key, (GROUPS, pair_count), 0, 2)
    leading = jnp.where(flips == 1, GROUP_BLOCKS - 1 - pairs, pairs).astype(jnp.int32)
    trailing = (GROUP_BLOCKS - 1 - leading).astype(jnp.int32)
    return jnp.stack([leading, trailing], axis=2).reshape(GROUPS, GROUP_BLOCKS).astype(jnp.int32)


def steps_of(own_key, shape, cuts, low, top_value):
    def one(position, shards_of):
        draws = jax.random.uniform(jax.random.fold_in(jax.random.fold_in(own_key, 6), position), (shards_of,), jnp.float32, low / len(cuts), top_value / len(cuts))
        return jnp.repeat(jnp.exp(draws), shape[position] // shards_of).reshape((-1,) + (1,) * (len(shape) - position - 1))

    loudness = one(*cuts[0])
    for cut in cuts[1:]:
        loudness = loudness * one(*cut)
    return loudness


def bell_draw(key, extent, width, limit, cuts=(), kind=jnp.bfloat16):
    gain = steps_of(key, extent, cuts, -0.22, 0.18) if cuts else 1.0
    values = jax.random.normal(key, extent, jnp.float32) * width * gain
    return jnp.minimum(jnp.maximum(values, -limit), limit).astype(kind)


def setup_inputs(seed: int = 0) -> dict:
    arg_keys = jax.random.split(jax.random.key(seed), 13)
    hidden_in = bell_draw(arg_keys[0], (GROUPS, GROUP_TOK, D), 1.0, 6.0, ((0, 4), (1, 8)))
    out_grad = bell_draw(arg_keys[1], (GROUPS, GROUP_TOK, D), 1.0, 6.0, ((0, 4), (1, 8)))
    lengths = draw_lengths(jax.random.fold_in(arg_keys[12], 71), 0)
    block_order = draw_block_order(jax.random.fold_in(arg_keys[12], 71), 0)
    ln_gain = jnp.clip(1.0 + 0.15 * jax.random.normal(arg_keys[4], (D,), jnp.float32), 0.25, 1.75).astype(jnp.bfloat16)
    ln_bias = bell_draw(arg_keys[5], (D,), 0.3, 2.0, ((0, 4),))
    w_qkv = bell_draw(arg_keys[6], (D, 3 * D), D ** -0.5, 0.125, ((0, 4),))
    b_qkv = bell_draw(arg_keys[7], (3 * D,), 0.3, 2.0, ((0, 4),))
    w_out = bell_draw(arg_keys[8], (D, D), (max(1, D // 256)) ** -0.5, 2.0, ((0, 4),))
    w_gate = bell_draw(arg_keys[9], (D, FF), D ** -0.5, 0.125, ((0, 4),))
    w_up = bell_draw(arg_keys[10], (D, FF), D ** -0.5, 0.125, ((0, 4),))
    w_down = bell_draw(arg_keys[11], (FF, D), FF ** -0.5, 0.078125, ((0, 4),))
    return {"hidden_in": hidden_in, "out_grad": out_grad, "lengths": lengths, "block_order": block_order, "ln_gain": ln_gain, "ln_bias": ln_bias, "w_qkv": w_qkv, "b_qkv": b_qkv, "w_out": w_out, "w_gate": w_gate, "w_up": w_up, "w_down": w_down}


@jax.custom_vjp
def low(v):
    return lax.optimization_barrier(v.astype(jnp.bfloat16)).astype(jnp.float32)

@jax.custom_vjp
def low_back(v):
    return v

def low_keep(v):
    return (low(v), None)

def low_pass(kept, grad):
    return (grad,)

def back_keep(v):
    return (v, None)

def back_low(kept, grad):
    return (low(grad),)
low.defvjp(low_keep, low_pass)
low_back.defvjp(back_keep, back_low)

def highest(left, right):
    return jnp.dot(left, right, precision=lax.Precision.HIGHEST, preferred_element_type=jnp.float32)

def stream_places(order_row, length_row):
    places = (order_row[:, None] * BLOCK + jnp.arange(BLOCK, dtype=jnp.int32)[None, :]).reshape(-1).astype(jnp.int32)
    ends = jnp.cumsum(length_row).astype(jnp.int32)
    starts = (ends - length_row).astype(jnp.int32)
    begins = lax.optimization_barrier(jnp.max(jnp.where(starts[None, :] <= places[:, None], starts[None, :], 0), axis=1)).astype(jnp.int32)
    return (places, begins)

def rotary_tables(places, begins):
    offsets = (places - begins).astype(jnp.float32)
    inverse = 1.0 / 10000.0 ** (jnp.arange(0, ROT, 2).astype(jnp.float32) / ROT)
    angles = offsets[:, None, None] * inverse[None, None, :]
    return (jnp.cos(angles), jnp.sin(angles))

def rotate(values, cosine, sine_table, direction):
    half_rot = ROT // 2
    lead_half = values[..., :half_rot]
    tail_half = values[..., half_rot:ROT]
    return jnp.concatenate([lead_half * cosine - direction * tail_half * sine_table, tail_half * cosine + direction * lead_half * sine_table, values[..., ROT:]], axis=-1)

def layer_pack(weights, packed):
    gain_full, bias_full, w_attn, b_attn, w_proj, w_gating, w_rising, w_lower = weights
    float_in, places, begins = packed
    row_count = float_in.shape[0]
    centre = lax.optimization_barrier(jnp.mean(float_in, axis=1, keepdims=True))
    deviation = float_in - centre
    inverse_std = lax.rsqrt(lax.optimization_barrier(jnp.mean(deviation * deviation, axis=1, keepdims=True)) + 1e-05)
    normed = low(deviation * inverse_std * gain_full + bias_full)
    merged_proj = low_back(highest(normed, w_attn) + b_attn)
    cosine, sine_table = rotary_tables(places, begins)
    query_all = low(rotate(merged_proj[:, :D].reshape(row_count, H, HD), cosine, sine_table, 1.0))
    key_all = low(rotate(merged_proj[:, D:2 * D].reshape(row_count, H, HD), cosine, sine_table, 1.0))
    value_all = low(merged_proj[:, 2 * D:].reshape(row_count, H, HD))
    allowed = (places[None, :] <= places[:, None]) & (places[None, :] >= begins[:, None])

    def one_head(triple):
        query_head, key_head, value_head = triple
        scores = low_back(highest(query_head, key_head.T) * HD ** (-0.5))
        scores = jnp.where(allowed, scores, -1e+30)
        row_max = lax.optimization_barrier(jnp.max(scores, axis=1, keepdims=True))
        log_total = row_max + jnp.log(lax.optimization_barrier(jnp.sum(jnp.exp(scores - row_max), axis=1, keepdims=True)))
        return highest(low(jnp.exp(scores - log_total)), value_head)
    heads_out = lax.map(jax.checkpoint(one_head), (jnp.transpose(query_all, (1, 0, 2)), jnp.transpose(key_all, (1, 0, 2)), jnp.transpose(value_all, (1, 0, 2))))
    attn_mixed = low_back(low(jnp.transpose(heads_out, (1, 0, 2)).reshape(row_count, D)))
    gating = low_back(highest(normed, w_gating))
    rising = low_back(highest(normed, w_rising))
    activated = low(jax.nn.silu(gating) * rising)
    return float_in + highest(attn_mixed, w_proj) + highest(activated, w_lower)

def reference(hidden_in, out_grad, lengths, block_order, ln_gain, ln_bias, w_qkv, b_qkv, w_out, w_gate, w_up, w_down):
    places, begins = jax.vmap(stream_places)(block_order, lengths)

    def forward(float_in, gain_full, bias_full, w_attn, b_attn, w_proj, w_gating, w_rising, w_lower):
        weights = (gain_full, bias_full, w_attn, b_attn, w_proj, w_gating, w_rising, w_lower)
        return lax.map(partial(layer_pack, weights), (float_in, places, begins))
    summed, pullback = jax.vjp(forward, hidden_in.astype(jnp.float32), ln_gain.astype(jnp.float32), ln_bias.astype(jnp.float32), w_qkv.astype(jnp.float32), b_qkv.astype(jnp.float32), w_out.astype(jnp.float32), w_gate.astype(jnp.float32), w_up.astype(jnp.float32), w_down.astype(jnp.float32))
    grads = pullback(out_grad.astype(jnp.float32))
    return (summed.astype(jnp.bfloat16), grads[0].astype(jnp.bfloat16), grads[1], grads[2], grads[3], grads[4], grads[5], grads[6], grads[7], grads[8])
```

```python
import functools

import jax
import jax.numpy as jnp
from jax import lax
from jax.experimental import pallas as pl
from jax.experimental.pallas import tpu as pltpu
from jax.sharding import PartitionSpec as P

HD = 64
ROT = 16
BLOCK = 128
CHUNK = 256
BF = jnp.bfloat16
F32 = jnp.float32
MASKED = -1e30


def matmul(left, right):
    return jnp.dot(left, right, preferred_element_type=F32)


def matmul_nt(left, right):
    return lax.dot_general(left, right, (((1,), (1,)), ((), ())), preferred_element_type=F32)


def matmul_tn(left, right):
    return lax.dot_general(left, right, (((0,), (0,)), ((), ())), preferred_element_type=F32)


def flip(values, axis, bit):
    count = lax.axis_size(axis)
    return lax.ppermute(values, axis, [(i, i ^ (1 << bit)) for i in range(count)])


def bits_of(count):
    bits = count.bit_length() - 1
    assert count == 1 << bits
    return bits


def gather_rows(values, axis, order):
    me = lax.axis_index(axis)
    count = lax.axis_size(axis)
    held = values[None]
    steps = [0]
    for bit in order:
        other = flip(held, axis, bit)
        held = jnp.concatenate([held, other], axis=0)
        steps = steps + [s ^ (1 << bit) for s in steps]
    rows = values.shape[0]
    out = jnp.zeros((count * rows,) + values.shape[1:], values.dtype)
    for place, step in enumerate(steps):
        out = lax.dynamic_update_slice_in_dim(out, held[place], (me ^ step) * rows, 0)
    return out


def gather_fsdp(values):
    bits = bits_of(lax.axis_size("fsdp"))
    half = values.shape[1] // 2 // 128 * 128
    first = list(range(bits))
    second = first[1:] + first[:1]
    return jnp.concatenate(
        [gather_rows(values[:, :half], "fsdp", first), gather_rows(values[:, half:], "fsdp", second)],
        axis=1,
    )


def scatter_rows(values, axis, order):
    me = lax.axis_index(axis)
    count = lax.axis_size(axis)
    bits = bits_of(count)
    rows = values.shape[0] // count
    held = values.reshape((2,) * bits + (rows,) + values.shape[1:])
    left = list(range(bits))
    for bit in order:
        at = len(left) - 1 - left.index(bit)
        mine = (me >> bit) & 1
        sent = lax.dynamic_index_in_dim(held, 1 - mine, at, keepdims=False).astype(BF)
        kept = lax.dynamic_index_in_dim(held, mine, at, keepdims=False)
        held = kept.astype(F32) + flip(sent, axis, bit).astype(F32)
        left.remove(bit)
    return held


def scatter_fsdp(values):
    bits = bits_of(lax.axis_size("fsdp"))
    half = values.shape[1] // 2 // 128 * 128
    first = list(range(bits))
    second = first[1:] + first[:1]
    return jnp.concatenate(
        [scatter_rows(values[:, :half], "fsdp", first), scatter_rows(values[:, half:], "fsdp", second)],
        axis=1,
    )


def gather_ctx(values):
    return lax.all_gather(values, "ctx", axis=0, tiled=True)


def scatter_ctx(values):
    return lax.psum_scatter(values.astype(BF), "ctx", scatter_dimension=0, tiled=True)


def attention_kernel(
    heads,
    slot_ref,
    low_ref,
    merged_ref,
    grad_mixed_ref,
    cos_ref,
    lead_ref,
    tail_ref,
    begin_ref,
    mixed_ref,
    grad_merged_ref,
    q_ref,
    k_ref,
    v_ref,
    g_ref,
    kt_ref,
    vt_ref,
    qm_ref,
    gm_ref,
    s_ref,
    d_ref,
    p_ref,
    ot_ref,
    dqt_ref,
    dk_ref,
    dv_ref,
):
    width = heads * HD
    tokens = merged_ref.shape[0]
    chunks = tokens // CHUNK
    blocks = tokens // BLOCK
    scale = HD ** (-0.5)

    def tables(rows):
        repeat = width // 128
        return tuple(
            jnp.concatenate([ref[rows, :]] * repeat, axis=1) for ref in (cos_ref, lead_ref, tail_ref)
        )

    def turn(values, rows, direction):
        cosine, lead, tail = tables(rows)
        ahead = pltpu.roll(values, width - ROT // 2, 1)
        behind = pltpu.roll(values, ROT // 2, 1)
        return values * cosine + direction * (ahead * lead + behind * tail)

    def rows_at(index, size):
        return pl.ds(pl.multiple_of(index * size, size), size)

    def prepare(block, carry):
        source = rows_at(slot_ref[block], BLOCK)
        target = rows_at(block, BLOCK)
        query = turn(merged_ref[source, 0:width], source, 1.0).astype(BF)
        key = turn(merged_ref[source, width : 2 * width], source, 1.0).astype(BF)
        value = merged_ref[source, 2 * width : 3 * width].astype(BF)
        q_ref[target, :] = query * jnp.asarray(scale, BF)
        k_ref[target, :] = key
        v_ref[target, :] = value
        kt_ref[:, target] = key.T
        vt_ref[:, target] = value.T
        g_ref[target, :] = grad_mixed_ref[source, :]
        dk_ref[target, :] = jnp.zeros((BLOCK, width), F32)
        dv_ref[target, :] = jnp.zeros((BLOCK, width), F32)
        return carry

    lax.fori_loop(0, blocks, prepare, 0)
    head_of = lax.broadcasted_iota(jnp.int32, (CHUNK, width), 1) // HD
    behind_by = lax.broadcasted_iota(jnp.int32, (CHUNK, CHUNK), 0) - lax.broadcasted_iota(
        jnp.int32, (CHUNK, CHUNK), 1
    )
    row_at = lax.broadcasted_iota(jnp.int32, (CHUNK, CHUNK), 0)

    def query_chunk(i, carry):
        here = rows_at(i, CHUNK)
        query = q_ref[here, :]
        grad = g_ref[here, :]
        zero = jnp.zeros_like(query)
        for h in range(heads):
            qm_ref[h * CHUNK : (h + 1) * CHUNK, :] = jnp.where(head_of == h, query, zero)
            gm_ref[h * CHUNK : (h + 1) * CHUNK, :] = jnp.where(head_of == h, grad, zero)
        ot_ref[...] = jnp.zeros_like(ot_ref)
        dqt_ref[...] = jnp.zeros_like(dqt_ref)
        low = low_ref[i]
        begin = begin_ref[i]

        def score(j, tops):
            there = rows_at(j, CHUNK)
            key = k_ref[there, :]
            allowed = (behind_by <= (i - j) * CHUNK) & (row_at >= begin - j * CHUNK)
            out = []
            for h in range(heads):
                s = matmul_nt(key, qm_ref[h * CHUNK : (h + 1) * CHUNK, :])
                s = jnp.where(allowed, s, MASKED)
                s_ref[h, there, :] = s
                out.append(jnp.maximum(tops[h], jnp.max(s, axis=0, keepdims=True)))
            return tuple(out)

        tops = lax.fori_loop(
            low, i + 1, score, tuple(jnp.full((1, CHUNK), MASKED, F32) for _ in range(heads))
        )

        def total(j, sums):
            there = rows_at(j, CHUNK)
            out = []
            for h in range(heads):
                e = jnp.exp(s_ref[h, there, :] - tops[h])
                s_ref[h, there, :] = e
                out.append(sums[h] + jnp.sum(e, axis=0, keepdims=True))
            return tuple(out)

        zeros = tuple(jnp.zeros((1, CHUNK), F32) for _ in range(heads))
        sums = lax.fori_loop(low, i + 1, total, zeros)
        shares = [1.0 / s for s in sums]

        def value_side(j, dots):
            there = rows_at(j, CHUNK)
            value = v_ref[there, :]
            out = []
            for h in range(heads):
                span = slice(h * HD, (h + 1) * HD)
                probs = s_ref[h, there, :] * shares[h]
                rounded = probs.astype(BF)
                p_ref[:, h * CHUNK : (h + 1) * CHUNK] = rounded
                ot_ref[span, :] += matmul(vt_ref[span, there], rounded)
                d = matmul_nt(value, gm_ref[h * CHUNK : (h + 1) * CHUNK, :])
                d_ref[h, there, :] = d
                out.append(dots[h] + jnp.sum(probs * d, axis=0, keepdims=True))
            dv_ref[there, :] += matmul(p_ref[...], gm_ref[...])
            return tuple(out)

        dots = lax.fori_loop(low, i + 1, value_side, zeros)

        def score_side(j, carry):
            there = rows_at(j, CHUNK)
            for h in range(heads):
                span = slice(h * HD, (h + 1) * HD)
                probs = s_ref[h, there, :] * shares[h]
                ds = (probs * (d_ref[h, there, :] - dots[h])).astype(BF)
                p_ref[:, h * CHUNK : (h + 1) * CHUNK] = ds
                dqt_ref[span, :] += matmul(kt_ref[span, there], ds)
            dk_ref[there, :] += matmul(p_ref[...], qm_ref[...])
            return carry

        lax.fori_loop(low, i + 1, score_side, 0)
        mixed = ot_ref[...].T.astype(BF)
        grad_query = dqt_ref[...].T * scale
        for part in range(CHUNK // BLOCK):
            target = rows_at(slot_ref[i * (CHUNK // BLOCK) + part], BLOCK)
            rows = slice(part * BLOCK, (part + 1) * BLOCK)
            mixed_ref[target, :] = mixed[rows]
            grad_merged_ref[target, 0:width] = turn(grad_query[rows], target, -1.0).astype(BF)
        return carry

    lax.fori_loop(0, chunks, query_chunk, 0)

    def finish(block, carry):
        source = rows_at(block, BLOCK)
        target = rows_at(slot_ref[block], BLOCK)
        grad_merged_ref[target, width : 2 * width] = turn(dk_ref[source, :], target, -1.0).astype(BF)
        grad_merged_ref[target, 2 * width : 3 * width] = dv_ref[source, :].astype(BF)
        return carry

    lax.fori_loop(0, blocks, finish, 0)


def attention(heads, slots, lows, merged, grad_mixed, tables, begins):
    tokens = merged.shape[0]
    width = heads * HD
    whole = pl.BlockSpec(memory_space=pltpu.VMEM)
    scalar = pl.BlockSpec(memory_space=pltpu.SMEM)
    return pl.pallas_call(
        functools.partial(attention_kernel, heads),
        out_shape=(
            jax.ShapeDtypeStruct((tokens, width), BF),
            jax.ShapeDtypeStruct((tokens, 3 * width), BF),
        ),
        in_specs=[scalar, scalar] + [whole] * 6,
        out_specs=(whole, whole),
        scratch_shapes=[
            pltpu.VMEM((tokens, width), BF),
            pltpu.VMEM((tokens, width), BF),
            pltpu.VMEM((tokens, width), BF),
            pltpu.VMEM((tokens, width), BF),
            pltpu.VMEM((width, tokens), BF),
            pltpu.VMEM((width, tokens), BF),
            pltpu.VMEM((heads * CHUNK, width), BF),
            pltpu.VMEM((heads * CHUNK, width), BF),
            pltpu.VMEM((heads, tokens, CHUNK), F32),
            pltpu.VMEM((heads, tokens, CHUNK), F32),
            pltpu.VMEM((CHUNK, heads * CHUNK), BF),
            pltpu.VMEM((width, CHUNK), F32),
            pltpu.VMEM((width, CHUNK), F32),
            pltpu.VMEM((tokens, width), F32),
            pltpu.VMEM((tokens, width), F32),
        ],
        compiler_params=pltpu.CompilerParams(vmem_limit_bytes=56 * 1024 * 1024),
        name="attention",
    )(slots, lows, merged, grad_mixed, *tables, begins)


def assemble_kernel(plan, source_ref, *targets):
    for target, pieces in zip(targets, plan):
        at = 0
        for part, offset, width in pieces:
            target[:, at : at + width] = source_ref[part, :, offset : offset + width].astype(F32)
            at += width


def assemble(gathered, plan):
    parts, rows, columns = gathered.shape
    step = 64
    widths = [sum(piece[2] for piece in pieces) for pieces in plan]
    return pl.pallas_call(
        functools.partial(assemble_kernel, plan),
        grid=(rows // step,),
        out_shape=tuple(jax.ShapeDtypeStruct((rows, w), F32) for w in widths),
        in_specs=[pl.BlockSpec((parts, step, columns), lambda i: (0, i, 0))],
        out_specs=tuple(pl.BlockSpec((step, w), lambda i: (i, 0)) for w in widths),
        compiler_params=pltpu.CompilerParams(vmem_limit_bytes=40 * 1024 * 1024),
        name="assemble",
    )(gathered)


def stream_places(order_row, length_row):
    places = (order_row[:, None] * BLOCK + jnp.arange(BLOCK, dtype=jnp.int32)[None, :]).reshape(-1)
    return places, stream_begins(places, length_row)


def stream_begins(places, length_row):
    ends = jnp.cumsum(length_row)
    starts = ends - length_row
    return jnp.max(jnp.where(starts[None, :] <= places[:, None], starts[None, :], 0), axis=1)


def rotary_tables(places, begins):
    entry = jnp.arange(128) % HD
    turned = entry < ROT
    index = jnp.where(entry < ROT // 2, entry, entry - ROT // 2)
    inverse = 1.0 / 10000.0 ** ((2 * index).astype(F32) / ROT)
    angles = (places - begins).astype(F32)[:, None] * jnp.where(turned, inverse, 0.0)[None, :]
    cosine, sine = jnp.cos(angles), jnp.sin(angles)
    lead = jnp.where((entry < ROT // 2)[None, :], -sine, 0.0)
    tail = jnp.where((turned & (entry >= ROT // 2))[None, :], sine, 0.0)
    return cosine, lead, tail


def take_columns(array, starts, width):
    return [lax.dynamic_slice_in_dim(array, s, width, 1) for s in starts]


def normalise(rows):
    centre = jnp.mean(rows, axis=1, keepdims=True)
    deviation = rows - centre
    inverse_std = lax.rsqrt(jnp.mean(deviation * deviation, axis=1, keepdims=True) + 1e-05)
    return deviation * inverse_std, inverse_std


def shards(
    hidden_in,
    out_grad,
    lengths,
    block_order,
    ln_gain,
    ln_bias,
    w_qkv,
    b_qkv,
    w_out,
    w_gate,
    w_up,
    w_down,
):
    parts = lax.axis_size("ctx")
    shard_count = lax.axis_size("fsdp")
    ctx_at = lax.axis_index("ctx")
    fsdp_at = lax.axis_index("fsdp")
    rows = hidden_in.shape[1]
    model = w_out.shape[1]
    hidden = w_gate.shape[1]
    tokens = rows * parts
    heads = model // HD // parts
    width = heads * HD
    shard_rows = w_qkv.shape[0]

    hidden_all = gather_ctx(hidden_in[0])
    grad_all = gather_ctx(out_grad[0])
    vectors = lax.all_gather(jnp.concatenate([ln_gain, ln_bias, b_qkv]), "fsdp", axis=0)
    gain_full = vectors[:, :shard_rows].reshape(-1).astype(F32)
    bias_full = vectors[:, shard_rows : 2 * shard_rows].reshape(-1).astype(F32)
    b_attn = vectors[:, 2 * shard_rows :].reshape(-1).astype(F32)

    spread = (model // HD) % (shard_count * parts) == 0
    pieces = shard_count if spread else 1
    head_span = model // pieces
    head_width = head_span // parts
    head_starts = [
        s * model + p * head_span + ctx_at * head_width for s in range(3) for p in range(pieces)
    ]
    unit_span = hidden // shard_count
    unit_width = unit_span // parts
    unit_starts = [p * unit_span + ctx_at * unit_width for p in range(shard_count)]

    w_pair_own = jnp.concatenate(
        take_columns(w_gate, unit_starts, unit_width) + take_columns(w_up, unit_starts, unit_width), axis=1
    )
    w_attn_own = jnp.concatenate(take_columns(w_qkv, head_starts, head_width), axis=1)
    b_attn_own = jnp.concatenate([lax.dynamic_slice_in_dim(b_attn, s, head_width, 0) for s in head_starts])
    w_down_own = lax.dynamic_slice_in_dim(w_down, ctx_at * unit_width, unit_width, 0)
    w_attn = gather_fsdp(w_attn_own)
    w_pair = gather_fsdp(w_pair_own)
    w_lower = gather_fsdp(w_down_own)
    if spread:
        w_proj = gather_fsdp(lax.dynamic_slice_in_dim(w_out, ctx_at * head_width, head_width, 0))
    else:
        w_proj = lax.dynamic_slice_in_dim(
            lax.all_gather(w_out, "fsdp", axis=0, tiled=True), ctx_at * width, width, 0
        )

    order_row = block_order[0]
    places, begins = stream_places(order_row, lengths[0])
    tables = rotary_tables(places, begins)
    blocks = order_row.shape[0]
    slots = jnp.sum(
        jnp.where(
            order_row[None, :] == jnp.arange(blocks, dtype=jnp.int32)[:, None],
            jnp.arange(blocks, dtype=jnp.int32)[None, :],
            0,
        ),
        axis=1,
    ).astype(jnp.int32)
    stream_starts = stream_begins(jnp.arange(tokens, dtype=jnp.int32), lengths[0]).astype(jnp.int32)
    lows = stream_starts[::CHUNK] // CHUNK
    stream_starts = stream_starts.reshape(tokens // CHUNK, 1, CHUNK)

    normal_all, _ = normalise(hidden_all.astype(F32))
    normed = (normal_all * gain_full + bias_full).astype(BF)
    merged = matmul(normed, w_attn) + b_attn_own
    pair = matmul(normed, w_pair)
    units = shard_count * unit_width
    gating, rising = pair[:, :units], pair[:, units:]
    sigma = jax.nn.sigmoid(gating)
    silu_gate = gating * sigma
    activated = (silu_gate * rising).astype(BF)

    grad_mixed = matmul_nt(grad_all, w_proj).astype(BF)
    grad_act = matmul_nt(grad_all, w_lower)
    grad_pair = jnp.concatenate(
        [
            (grad_act * rising * sigma * (1.0 + gating * (1.0 - sigma))).astype(BF),
            (grad_act * silu_gate).astype(BF),
        ],
        axis=1,
    )
    pair_sum = scatter_fsdp(matmul_tn(normed, grad_pair))
    down_sum = scatter_fsdp(matmul_tn(activated, grad_all))
    pair_all = gather_ctx(pair_sum.astype(BF)[None])
    down_all = gather_ctx(down_sum.astype(BF))

    mixed, grad_merged = attention(heads, slots, lows, merged, grad_mixed, tables, stream_starts)

    out_rows = scatter_ctx(matmul(mixed, w_proj) + matmul(activated, w_lower))
    float_in = hidden_in[0].astype(F32)
    output = (float_in + out_rows.astype(F32)).astype(BF)[None]

    grad_normed = scatter_ctx(matmul_nt(grad_pair, w_pair) + matmul_nt(grad_merged, w_attn)).astype(F32)

    attn_sum = scatter_fsdp(matmul_tn(normed, grad_merged))
    attn_all = gather_ctx(attn_sum.astype(BF)[None])
    proj_part = matmul_tn(mixed, grad_all)
    if spread:
        proj_all = gather_ctx(scatter_fsdp(proj_part).astype(BF)).astype(F32)
    else:
        proj_all = lax.dynamic_slice_in_dim(
            gather_ctx(lax.psum(proj_part, "fsdp")), fsdp_at * shard_rows, shard_rows, 0
        )

    pair_plan = [
        [
            (c, side * units + p * unit_width, unit_width)
            for p in range(shard_count)
            for c in range(parts)
        ]
        for side in range(2)
    ]
    attn_plan = [
        [
            (c, (s * pieces + p) * head_width, head_width)
            for s in range(3)
            for p in range(pieces)
            for c in range(parts)
        ]
    ]
    grad_gate_w, grad_up_w = assemble(pair_all, pair_plan)
    (grad_attn_w,) = assemble(attn_all, attn_plan)

    normal_hat, inverse_std = normalise(float_in)
    merged_term = jnp.sum(grad_merged, axis=0, dtype=F32)
    merged_terms = jnp.sum(lax.all_gather(merged_term, ("ctx", "fsdp"), axis=0).reshape(parts, shard_count, -1), axis=1)
    merged_full = jnp.moveaxis(merged_terms.reshape(parts, 3, pieces, head_width), 0, 2).reshape(-1)
    b_rows = b_qkv.shape[0]
    grad_b = lax.dynamic_slice_in_dim(merged_full, fsdp_at * b_rows, b_rows, 0)
    terms = jnp.stack([jnp.sum(grad_normed * normal_hat, axis=0), jnp.sum(grad_normed, axis=0)])
    terms = jnp.sum(lax.all_gather(terms, ("ctx", "fsdp"), axis=0), axis=0)
    terms = lax.dynamic_slice_in_dim(terms, fsdp_at * shard_rows, shard_rows, 1)

    grad_hat = grad_normed * gain_full
    grad_in = out_grad[0].astype(F32) + inverse_std * (
        grad_hat
        - jnp.mean(grad_hat, axis=1, keepdims=True)
        - normal_hat * jnp.mean(grad_hat * normal_hat, axis=1, keepdims=True)
    )
    return (
        output,
        grad_in.astype(BF)[None],
        terms[0],
        terms[1],
        grad_attn_w,
        grad_b,
        proj_all,
        grad_gate_w,
        grad_up_w,
        down_all.astype(F32),
    )


def solution(mesh):
    return jax.shard_map(
        shards,
        mesh=mesh,
        in_specs=(
            P("fsdp", "ctx", None),
            P("fsdp", "ctx", None),
            P("fsdp", None),
            P("fsdp", None),
            P("fsdp"),
            P("fsdp"),
            P("fsdp", None),
            P("fsdp"),
            P("fsdp", None),
            P("fsdp", None),
            P("fsdp", None),
            P("fsdp", None),
        ),
        out_specs=(
            P("fsdp", "ctx", None),
            P("fsdp", "ctx", None),
            P("fsdp"),
            P("fsdp"),
            P("fsdp", None),
            P("fsdp"),
            P("fsdp", None),
            P("fsdp", None),
            P("fsdp", None),
            P("fsdp", None),
        ),
        check_vma=False,
    )
```

```python
import functools

import jax
import jax.numpy as jnp
from jax import lax
from jax.experimental import pallas as pl
from jax.experimental.pallas import tpu as pltpu
from jax.sharding import PartitionSpec as P

HD = 64
ROT = 16
BLOCK = 128
CHUNK = 256
BF = jnp.bfloat16
F32 = jnp.float32
MASKED = -1e30


def matmul(left, right):
    return jnp.dot(left, right, preferred_element_type=F32)


def matmul_nt(left, right):
    return lax.dot_general(left, right, (((1,), (1,)), ((), ())), preferred_element_type=F32)


def matmul_tn(left, right):
    return lax.dot_general(left, right, (((0,), (0,)), ((), ())), preferred_element_type=F32)


def flip(values, axis, bit):
    count = lax.axis_size(axis)
    return lax.ppermute(values, axis, [(i, i ^ (1 << bit)) for i in range(count)])


def bits_of(count):
    bits = count.bit_length() - 1
    assert count == 1 << bits
    return bits


def gather_rows(values, axis, order):
    me = lax.axis_index(axis)
    count = lax.axis_size(axis)
    held = values[None]
    steps = [0]
    for bit in order:
        other = flip(held, axis, bit)
        held = jnp.concatenate([held, other], axis=0)
        steps = steps + [s ^ (1 << bit) for s in steps]
    rows = values.shape[0]
    out = jnp.zeros((count * rows,) + values.shape[1:], values.dtype)
    for place, step in enumerate(steps):
        out = lax.dynamic_update_slice_in_dim(out, held[place], (me ^ step) * rows, 0)
    return out


def placed(pieces, places, total):
    out = jnp.zeros((total,) + pieces[0].shape[1:], pieces[0].dtype)
    for piece, place in zip(pieces, places):
        out = lax.dynamic_update_slice_in_dim(out, piece, place, 0)
    return out


def gather_first(values):
    if lax.axis_size("fsdp") != 4:
        return [gather_rows(values, "fsdp", list(range(bits_of(lax.axis_size("fsdp")))))]
    return [flip(values, "fsdp", 0), flip(values, "fsdp", 1)]


def gather_second(values, first):
    if lax.axis_size("fsdp") != 4:
        return []
    half = values.shape[0] // 2 // 16 * 16
    return [flip(first[0][:half], "fsdp", 1), flip(first[1][half:], "fsdp", 0)]


def gathered_pieces(values, first, second, rows):
    count = lax.axis_size("fsdp")
    shard = values.shape[0]
    if count != 4:
        return [(first[0], i * shard, rows, i * rows) for i in range(count)]
    me = lax.axis_index("fsdp")
    half = shard // 2 // 16 * 16
    return [
        (values, 0, rows, me * rows),
        (first[0], 0, rows, (me ^ 1) * rows),
        (first[1], 0, rows, (me ^ 2) * rows),
        (second[0], 0, half, (me ^ 3) * rows),
        (second[1], 0, rows - half, (me ^ 3) * rows + half),
    ]


def gathered_rest(values, first, second, rows):
    count = lax.axis_size("fsdp")
    shard = values.shape[0]
    if count != 4:
        return first[0].reshape(count, shard, -1)[:, rows:]
    me = lax.axis_index("fsdp")
    half = shard // 2 // 16 * 16
    tails = [values[rows:], first[0][rows:], first[1][rows:], second[1][rows - half :]]
    return placed([t[None] for t in tails], [me, me ^ 1, me ^ 2, me ^ 3], count)


def others_of(values, axis, stride, count):
    size = lax.axis_size(axis)
    digit = lax.axis_index(axis) // stride % count

    def moved(i, by):
        at = i // stride % count
        return i + ((at + by) % count - at) * stride

    return [lax.ppermute(values, axis, [(i, moved(i, by)) for i in range(size)]) for by in range(1, count)], digit


def sum_of(values, others, digit):
    count = len(others) + 1
    out = jnp.zeros((count,) + values.shape, values.dtype)
    for by, piece in enumerate([values] + others):
        out = lax.dynamic_update_slice_in_dim(out, piece[None], (digit + count - by) % count, 0)
    total = out[0]
    for at in range(1, count):
        total = total + out[at]
    return total


def scatter_rows(values, axis, order):
    me = lax.axis_index(axis)
    count = lax.axis_size(axis)
    bits = bits_of(count)
    rows = values.shape[0] // count
    held = values.reshape((2,) * bits + (rows,) + values.shape[1:])
    left = list(range(bits))
    for bit in order:
        at = len(left) - 1 - left.index(bit)
        mine = (me >> bit) & 1
        sent = lax.dynamic_index_in_dim(held, 1 - mine, at, keepdims=False).astype(BF)
        kept = lax.dynamic_index_in_dim(held, mine, at, keepdims=False)
        held = kept.astype(F32) + flip(sent, axis, bit).astype(F32)
        left.remove(bit)
    return held


def fsdp_block(part, index):
    rows = part.shape[0] // lax.axis_size("fsdp")
    return lax.dynamic_slice_in_dim(part, index * rows, rows, 0)


def halves(part):
    half = part.shape[1] // 2 // 128 * 128
    return part[:, :half], part[:, half:]


def scatter_first(sides):
    if lax.axis_size("fsdp") != 4:
        return [scatter_rows(part, "fsdp", list(range(bits_of(lax.axis_size("fsdp"))))) for part in sides]
    me = lax.axis_index("fsdp")
    return [
        flip(fsdp_block(sides[1], me ^ 3), "fsdp", 0),
        flip(fsdp_block(sides[0], me ^ 3), "fsdp", 1),
        flip(fsdp_block(sides[1], me ^ 1), "fsdp", 0),
        flip(fsdp_block(sides[0], me ^ 2), "fsdp", 1),
    ]


def scatter_second(sides, first):
    if lax.axis_size("fsdp") != 4:
        return []
    me = lax.axis_index("fsdp")
    across = fsdp_block(sides[0], me ^ 1).astype(F32) + first[1].astype(F32)
    along = fsdp_block(sides[1], me ^ 2).astype(F32) + first[0].astype(F32)
    return [flip(across.astype(BF), "fsdp", 0), flip(along.astype(BF), "fsdp", 1)]


def scatter_last(sides, first, second):
    if lax.axis_size("fsdp") != 4:
        return first[0].astype(BF), first[1].astype(BF)
    me = lax.axis_index("fsdp")
    left = fsdp_block(sides[0], me).astype(F32) + first[3].astype(F32) + second[0].astype(F32)
    right = fsdp_block(sides[1], me).astype(F32) + first[2].astype(F32) + second[1].astype(F32)
    return left.astype(BF), right.astype(BF)


def gather_ctx(values):
    return lax.all_gather(values, "ctx", axis=0, tiled=True)


def scatter_ctx(values):
    return lax.psum_scatter(values, "ctx", scatter_dimension=0, tiled=True)


def split_cores(part):
    parts = lax.axis_size("ctx")
    core = lax.axis_index("ctx") % 2
    blocks = part.reshape(parts // 2, 2, part.shape[0] // parts, part.shape[1])
    return [lax.dynamic_index_in_dim(blocks, k, 1, keepdims=False) for k in (core, 1 - core)]


def scatter_places(values):
    places, rows, columns = values.shape
    lines = [[2 * p + k for p in range(places)] for k in range(2)]
    return lax.psum_scatter(
        values.reshape(places * rows, columns), "ctx", scatter_dimension=0, axis_index_groups=lines, tiled=True
    )


def nothing_kernel(*refs):
    return None


def tie(values, after):
    anywhere = pl.BlockSpec(memory_space=pl.ANY)
    return pl.pallas_call(
        nothing_kernel,
        out_shape=tuple(jax.ShapeDtypeStruct(v.shape, v.dtype) for v in values),
        in_specs=[anywhere] * (len(values) + len(after)),
        out_specs=tuple([anywhere] * len(values)),
        input_output_aliases={i: i for i in range(len(values))},
        name="tie",
    )(*values, *after)


def stage(*groups):
    leaves, tree = jax.tree.flatten(groups)
    return jax.tree.unflatten(tree, tie(leaves, []))


def rows_at(index, size):
    return pl.ds(pl.multiple_of(index * size, size), size)


def turn(values, tables, rows, direction):
    width = values.shape[1]
    cosine, lead, tail = (jnp.concatenate([ref[rows, :]] * (width // 128), axis=1) for ref in tables)
    ahead = pltpu.roll(values, width - ROT // 2, 1)
    behind = pltpu.roll(values, ROT // 2, 1)
    return values * cosine + direction * (ahead * lead + behind * tail)


def split_heads(target, values, heads):
    head_of = lax.broadcasted_iota(jnp.int32, values.shape, 1) // HD
    for h in range(heads):
        target[h * CHUNK : (h + 1) * CHUNK, :] = jnp.where(head_of == h, values, jnp.zeros_like(values))


def visible(i, j, begin):
    key_at = lax.broadcasted_iota(jnp.int32, (CHUNK, CHUNK), 0)
    query_at = lax.broadcasted_iota(jnp.int32, (CHUNK, CHUNK), 1)
    return (key_at - query_at <= (i - j) * CHUNK) & (key_at >= begin - j * CHUNK)


def forward_kernel(
    heads,
    slot_ref,
    low_ref,
    merged_ref,
    cos_ref,
    lead_ref,
    tail_ref,
    begin_ref,
    mixed_ref,
    q_ref,
    k_ref,
    v_ref,
    total_ref,
    ot_ref,
    vt_ref,
    qm_ref,
    s_ref,
):
    width = heads * HD
    tokens = merged_ref.shape[0]
    tables = (cos_ref, lead_ref, tail_ref)

    def prepare(block, carry):
        source = rows_at(slot_ref[block], BLOCK)
        target = rows_at(block, BLOCK)
        query = turn(merged_ref[source, 0:width], tables, source, 1.0).astype(BF)
        key = turn(merged_ref[source, width : 2 * width], tables, source, 1.0).astype(BF)
        value = merged_ref[source, 2 * width : 3 * width].astype(BF)
        q_ref[target, :] = query * jnp.asarray(HD ** (-0.5), BF)
        k_ref[target, :] = key
        v_ref[target, :] = value
        vt_ref[:, target] = value.T
        return carry

    lax.fori_loop(0, tokens // BLOCK, prepare, 0)

    def query_chunk(i, carry):
        here = rows_at(i, CHUNK)
        split_heads(qm_ref, q_ref[here, :], heads)
        ot_ref[:, here] = jnp.zeros((width, CHUNK), F32)
        low = low_ref[i]
        begin = begin_ref[i]

        def score(j, tops):
            there = rows_at(j, CHUNK)
            key = k_ref[there, :]
            allowed = visible(i, j, begin)
            out = []
            for h in range(heads):
                s = matmul_nt(key, qm_ref[h * CHUNK : (h + 1) * CHUNK, :])
                s = jnp.where(allowed, s, MASKED)
                s_ref[h, there, :] = s
                out.append(jnp.maximum(tops[h], jnp.max(s, axis=0, keepdims=True)))
            return tuple(out)

        tops = lax.fori_loop(
            low, i + 1, score, tuple(jnp.full((1, CHUNK), MASKED, F32) for _ in range(heads))
        )

        def value_side(j, sums):
            there = rows_at(j, CHUNK)
            out = []
            for h in range(heads):
                span = slice(h * HD, (h + 1) * HD)
                e = jnp.exp(s_ref[h, there, :] - tops[h])
                out.append(sums[h] + jnp.sum(e, axis=0, keepdims=True))
                ot_ref[span, here] += matmul(vt_ref[span, there], e.astype(BF))
            return tuple(out)

        sums = lax.fori_loop(low, i + 1, value_side, tuple(jnp.zeros((1, CHUNK), F32) for _ in range(heads)))
        for h in range(heads):
            span = slice(h * HD, (h + 1) * HD)
            ot_ref[span, here] = ot_ref[span, here] * (1.0 / sums[h])
            total_ref[i, h : h + 1, :] = tops[h] + jnp.log(sums[h])
        mixed = ot_ref[:, here].T.astype(BF)
        for part in range(CHUNK // BLOCK):
            target = rows_at(slot_ref[i * (CHUNK // BLOCK) + part], BLOCK)
            mixed_ref[target, :] = mixed[part * BLOCK : (part + 1) * BLOCK]
        return carry

    lax.fori_loop(0, tokens // CHUNK, query_chunk, 0)


def backward_kernel(
    heads,
    slot_ref,
    low_ref,
    q_ref,
    k_ref,
    v_ref,
    total_ref,
    ot_ref,
    grad_mixed_ref,
    cos_ref,
    lead_ref,
    tail_ref,
    begin_ref,
    grad_merged_ref,
    kt_ref,
    qm_ref,
    gm_ref,
    p_ref,
    ds_ref,
    dqt_ref,
    dk_ref,
    dv_ref,
):
    width = heads * HD
    tokens = q_ref.shape[0]
    tables = (cos_ref, lead_ref, tail_ref)

    def prepare(block, carry):
        here = rows_at(block, BLOCK)
        kt_ref[:, here] = k_ref[here, :].T
        dk_ref[here, :] = jnp.zeros((BLOCK, width), F32)
        dv_ref[here, :] = jnp.zeros((BLOCK, width), F32)
        return carry

    lax.fori_loop(0, tokens // BLOCK, prepare, 0)

    def query_chunk(i, carry):
        here = rows_at(i, CHUNK)
        targets = [rows_at(slot_ref[i * (CHUNK // BLOCK) + part], BLOCK) for part in range(CHUNK // BLOCK)]
        grad = jnp.concatenate([grad_mixed_ref[target, :] for target in targets], axis=0)
        split_heads(qm_ref, q_ref[here, :], heads)
        split_heads(gm_ref, grad, heads)
        dqt_ref[...] = jnp.zeros_like(dqt_ref)
        product = grad.T.astype(F32) * ot_ref[:, here]
        dots = [jnp.sum(product[h * HD : (h + 1) * HD], axis=0, keepdims=True) for h in range(heads)]
        totals = [total_ref[i, h : h + 1, :] for h in range(heads)]
        begin = begin_ref[i]

        def key_chunk(j, carry):
            there = rows_at(j, CHUNK)
            key = k_ref[there, :]
            value = v_ref[there, :]
            allowed = visible(i, j, begin)
            for h in range(heads):
                span = slice(h * HD, (h + 1) * HD)
                part = slice(h * CHUNK, (h + 1) * CHUNK)
                s = matmul_nt(key, qm_ref[part, :])
                probs = jnp.exp(jnp.where(allowed, s, MASKED) - totals[h])
                p_ref[:, part] = probs.astype(BF)
                ds = (probs * (matmul_nt(value, gm_ref[part, :]) - dots[h])).astype(BF)
                ds_ref[:, part] = ds
                dqt_ref[span, :] += matmul(kt_ref[span, there], ds)
            dv_ref[there, :] += matmul(p_ref[...], gm_ref[...])
            dk_ref[there, :] += matmul(ds_ref[...], qm_ref[...])
            return carry

        lax.fori_loop(low_ref[i], i + 1, key_chunk, 0)
        grad_query = dqt_ref[...].T * HD ** (-0.5)
        for part, target in enumerate(targets):
            rows = slice(part * BLOCK, (part + 1) * BLOCK)
            grad_merged_ref[target, 0:width] = turn(grad_query[rows], tables, target, -1.0).astype(BF)
        return carry

    lax.fori_loop(0, tokens // CHUNK, query_chunk, 0)

    def finish(block, carry):
        source = rows_at(block, BLOCK)
        target = rows_at(slot_ref[block], BLOCK)
        grad_merged_ref[target, width : 2 * width] = turn(dk_ref[source, :], tables, target, -1.0).astype(BF)
        grad_merged_ref[target, 2 * width : 3 * width] = dv_ref[source, :].astype(BF)
        return carry

    lax.fori_loop(0, tokens // BLOCK, finish, 0)


WHOLE = pl.BlockSpec(memory_space=pltpu.VMEM)
SCALAR = pl.BlockSpec(memory_space=pltpu.SMEM)
ANYWHERE = pl.BlockSpec(memory_space=pl.ANY)


def attention_forward(heads, slots, lows, merged, tables, begins):
    tokens = merged.shape[0]
    width = heads * HD
    rows = jax.ShapeDtypeStruct((tokens, width), BF)
    return pl.pallas_call(
        functools.partial(forward_kernel, heads),
        out_shape=(
            rows,
            rows,
            rows,
            rows,
            jax.ShapeDtypeStruct((tokens // CHUNK, heads, CHUNK), F32),
            jax.ShapeDtypeStruct((width, tokens), F32),
        ),
        in_specs=[SCALAR, SCALAR] + [WHOLE] * 5,
        out_specs=(WHOLE,) * 6,
        scratch_shapes=[
            pltpu.VMEM((width, tokens), BF),
            pltpu.VMEM((heads * CHUNK, width), BF),
            pltpu.VMEM((heads, tokens, CHUNK), F32),
        ],
        compiler_params=pltpu.CompilerParams(vmem_limit_bytes=48 * 1024 * 1024),
        cost_estimate=pl.CostEstimate(flops=25_000_000_000, transcendentals=0, bytes_accessed=0),
        name="attention_forward",
    )(slots, lows, merged, *tables, begins)


def attention_backward(heads, slots, lows, kept, grad_mixed, tables, begins):
    tokens, width = grad_mixed.shape
    return pl.pallas_call(
        functools.partial(backward_kernel, heads),
        out_shape=jax.ShapeDtypeStruct((tokens, 3 * width), BF),
        in_specs=[SCALAR, SCALAR] + [WHOLE] * 10,
        out_specs=WHOLE,
        scratch_shapes=[
            pltpu.VMEM((width, tokens), BF),
            pltpu.VMEM((heads * CHUNK, width), BF),
            pltpu.VMEM((heads * CHUNK, width), BF),
            pltpu.VMEM((CHUNK, heads * CHUNK), BF),
            pltpu.VMEM((CHUNK, heads * CHUNK), BF),
            pltpu.VMEM((width, CHUNK), F32),
            pltpu.VMEM((tokens, width), F32),
            pltpu.VMEM((tokens, width), F32),
        ],
        compiler_params=pltpu.CompilerParams(vmem_limit_bytes=48 * 1024 * 1024),
        cost_estimate=pl.CostEstimate(flops=40_000_000_000, transcendentals=0, bytes_accessed=0),
        name="attention_backward",
    )(slots, lows, *kept, grad_mixed, *tables, begins)


def fetch(at_ref, pieces, spans, target, sem):
    copies = []
    for n, (piece, (first, rows)) in enumerate(zip(pieces, spans)):
        place = pl.ds(pl.multiple_of(at_ref[n], 16), rows)
        copies.append(pltpu.make_async_copy(piece.at[pl.ds(first, rows), :], target.at[place, :], sem.at[n]))
    for copy in copies:
        copy.start()
    return copies


def attn_kernel(spans, at_ref, hidden_ref, gain_ref, bias_ref, shift_ref, *refs):
    n = len(spans)
    normed_ref, merged_ref, w_attn, sem = refs[n:]

    @pl.when(pl.program_id(0) == 0)
    def _():
        for copy in fetch(at_ref, refs[:n], spans, w_attn, sem):
            copy.wait()

    normal, _ = normalise(hidden_ref[...].astype(F32))
    normed = (normal * gain_ref[...] + bias_ref[...]).astype(BF)
    normed_ref[...] = normed
    merged_ref[...] = matmul(normed, w_attn[...]) + shift_ref[...]


def pair_kernel(spans, at_ref, normed_ref, *refs):
    n = len(spans)
    gate_pieces, up_pieces = refs[:n], refs[n : 2 * n]
    act_ref, slope_ref, silu_ref, w_gate, w_up, *sems = refs[2 * n :]

    @pl.when(pl.program_id(0) == 0)
    def _():
        copies = fetch(at_ref, gate_pieces, spans, w_gate, sems[0])
        copies += fetch(at_ref, up_pieces, spans, w_up, sems[1])
        for copy in copies:
            copy.wait()

    normed = normed_ref[...]
    gating = matmul(normed, w_gate[...])
    rising = matmul(normed, w_up[...])
    sigma = jax.nn.sigmoid(gating)
    silu = gating * sigma
    act_ref[...] = (silu * rising).astype(BF)
    slope_ref[...] = (rising * sigma * (1.0 + gating * (1.0 - sigma))).astype(BF)
    silu_ref[...] = silu.astype(BF)


def row_block(width):
    return pl.BlockSpec((CHUNK, width), lambda i: (i, 0))


def full_block(array):
    return pl.BlockSpec(array.shape, lambda i: (0, 0))


def split_pieces(pieces):
    at = jnp.stack([jnp.asarray(piece[3], jnp.int32) for piece in pieces])
    return at, [piece[0] for piece in pieces], tuple((piece[1], piece[2]) for piece in pieces)


def attn_side(hidden, gain, bias, shift, pieces):
    tokens, model = hidden.shape
    at, arrays, spans = split_pieces(pieces)
    n = len(spans)
    width = arrays[0].shape[1]
    return pl.pallas_call(
        functools.partial(attn_kernel, spans),
        grid=(tokens // CHUNK,),
        out_shape=(jax.ShapeDtypeStruct((tokens, model), BF), jax.ShapeDtypeStruct((tokens, width), F32)),
        in_specs=[SCALAR, row_block(model), full_block(gain), full_block(bias), full_block(shift)] + [ANYWHERE] * n,
        out_specs=(row_block(model), row_block(width)),
        scratch_shapes=[pltpu.VMEM((model, width), BF), pltpu.SemaphoreType.DMA((n,))],
        compiler_params=pltpu.CompilerParams(vmem_limit_bytes=56 * 1024 * 1024),
        cost_estimate=pl.CostEstimate(flops=18_000_000_000, transcendentals=0, bytes_accessed=0),
        name="attn_side",
    )(at, hidden, gain, bias, shift, *arrays)


def pair_side(normed, gate_pieces, up_pieces):
    tokens, model = normed.shape
    at, gates, spans = split_pieces(gate_pieces)
    ups = split_pieces(up_pieces)[1]
    n = len(spans)
    units = gates[0].shape[1]
    return pl.pallas_call(
        functools.partial(pair_kernel, spans),
        grid=(tokens // CHUNK,),
        out_shape=(jax.ShapeDtypeStruct((tokens, units), BF),) * 3,
        in_specs=[SCALAR, row_block(model)] + [ANYWHERE] * (2 * n),
        out_specs=(row_block(units),) * 3,
        scratch_shapes=[
            pltpu.VMEM((model, units), BF),
            pltpu.VMEM((model, units), BF),
            pltpu.SemaphoreType.DMA((n,)),
            pltpu.SemaphoreType.DMA((n,)),
        ],
        compiler_params=pltpu.CompilerParams(vmem_limit_bytes=56 * 1024 * 1024),
        cost_estimate=pl.CostEstimate(flops=28_000_000_000, transcendentals=0, bytes_accessed=0),
        name="pair_side",
    )(at, normed, *gates, *ups)


def grad_kernel(grad_ref, slope_ref, silu_ref, lower_ref, proj_ref, gate_ref, up_ref, mixed_ref):
    grad = grad_ref[...]
    act = matmul_nt(grad, lower_ref[...])
    mixed_ref[...] = matmul_nt(grad, proj_ref[...]).astype(BF)
    gate_ref[...] = (act * slope_ref[...].astype(F32)).astype(BF)
    up_ref[...] = (act * silu_ref[...].astype(F32)).astype(BF)


def grad_side(grad, slope, silu, lower, proj):
    tokens, model = grad.shape
    units, width = slope.shape[1], proj.shape[0]
    return pl.pallas_call(
        grad_kernel,
        grid=(tokens // CHUNK,),
        out_shape=(
            jax.ShapeDtypeStruct((tokens, units), BF),
            jax.ShapeDtypeStruct((tokens, units), BF),
            jax.ShapeDtypeStruct((tokens, width), BF),
        ),
        in_specs=[
            row_block(model),
            row_block(units),
            row_block(units),
            full_block(lower),
            full_block(proj),
        ],
        out_specs=(row_block(units), row_block(units), row_block(width)),
        compiler_params=pltpu.CompilerParams(vmem_limit_bytes=56 * 1024 * 1024),
        cost_estimate=pl.CostEstimate(flops=18_000_000_000, transcendentals=0, bytes_accessed=0),
        name="grad_side",
    )(grad, slope, silu, lower, proj)


def out_kernel(mixed_ref, act_ref, proj_ref, lower_ref, out_ref):
    out_ref[...] = (matmul(mixed_ref[...], proj_ref[...]) + matmul(act_ref[...], lower_ref[...])).astype(BF)


def out_side(mixed, act, proj, lower):
    tokens, model = mixed.shape[0], proj.shape[1]
    return pl.pallas_call(
        out_kernel,
        grid=(tokens // CHUNK,),
        out_shape=jax.ShapeDtypeStruct((tokens, model), BF),
        in_specs=[row_block(mixed.shape[1]), row_block(act.shape[1]), full_block(proj), full_block(lower)],
        out_specs=row_block(model),
        compiler_params=pltpu.CompilerParams(vmem_limit_bytes=56 * 1024 * 1024),
        cost_estimate=pl.CostEstimate(flops=15_000_000_000, transcendentals=0, bytes_accessed=0),
        name="out_side",
    )(mixed, act, proj, lower)


def input_kernel(spans, at_ref, gate_ref, up_ref, merged_ref, hidden_ref, *refs):
    n = len(spans)
    gate_pieces, up_pieces, attn_pieces = refs[:n], refs[n : 2 * n], refs[2 * n : 3 * n]
    part_ref, terms_ref, w_gate, w_up, w_attn, *sems = refs[3 * n :]

    @pl.when(pl.program_id(0) == 0)
    def _():
        copies = fetch(at_ref, gate_pieces, spans, w_gate, sems[0])
        copies += fetch(at_ref, up_pieces, spans, w_up, sems[1])
        copies += fetch(at_ref, attn_pieces, spans, w_attn, sems[2])
        terms_ref[...] = jnp.zeros_like(terms_ref)
        for copy in copies:
            copy.wait()

    part = matmul_nt(gate_ref[...], w_gate[...]) + matmul_nt(up_ref[...], w_up[...])
    part = part + matmul_nt(merged_ref[...], w_attn[...])
    part_ref[...] = part.astype(BF)
    normal, _ = normalise(hidden_ref[...].astype(F32))
    terms_ref[0:1, :] += jnp.sum(part * normal, axis=0, keepdims=True)
    terms_ref[1:2, :] += jnp.sum(part, axis=0, keepdims=True)


def input_side(grad_gate, grad_up, grad_merged, hidden, gate_pieces, up_pieces, attn_pieces):
    tokens, model = hidden.shape
    at, gates, spans = split_pieces(gate_pieces)
    ups, attns = split_pieces(up_pieces)[1], split_pieces(attn_pieces)[1]
    n = len(spans)
    units, width = grad_gate.shape[1], grad_merged.shape[1]
    return pl.pallas_call(
        functools.partial(input_kernel, spans),
        grid=(tokens // CHUNK,),
        out_shape=(jax.ShapeDtypeStruct((tokens, model), BF), jax.ShapeDtypeStruct((2, model), F32)),
        in_specs=[SCALAR, row_block(units), row_block(units), row_block(width), row_block(model)]
        + [ANYWHERE] * (3 * n),
        out_specs=(row_block(model), pl.BlockSpec((2, model), lambda i: (0, 0))),
        scratch_shapes=[
            pltpu.VMEM((model, units), BF),
            pltpu.VMEM((model, units), BF),
            pltpu.VMEM((model, width), BF),
            pltpu.SemaphoreType.DMA((n,)),
            pltpu.SemaphoreType.DMA((n,)),
            pltpu.SemaphoreType.DMA((n,)),
        ],
        compiler_params=pltpu.CompilerParams(vmem_limit_bytes=56 * 1024 * 1024),
        cost_estimate=pl.CostEstimate(flops=30_000_000_000, transcendentals=0, bytes_accessed=0),
        name="input_side",
    )(at, grad_gate, grad_up, grad_merged, hidden, *gates, *ups, *attns)


def assemble_kernel(plan, source_ref, *targets):
    for target, pieces in zip(targets, plan):
        at = 0
        for part, offset, width in pieces:
            target[:, at : at + width] = source_ref[part, :, offset : offset + width].astype(F32)
            at += width


def assemble(gathered, plan):
    parts, rows, columns = gathered.shape
    step = 64
    widths = [sum(piece[2] for piece in pieces) for pieces in plan]
    return pl.pallas_call(
        functools.partial(assemble_kernel, plan),
        grid=(rows // step,),
        out_shape=tuple(jax.ShapeDtypeStruct((rows, w), F32) for w in widths),
        in_specs=[pl.BlockSpec((parts, step, columns), lambda i: (0, i, 0))],
        out_specs=tuple(pl.BlockSpec((step, w), lambda i: (i, 0)) for w in widths),
        compiler_params=pltpu.CompilerParams(vmem_limit_bytes=40 * 1024 * 1024),
        name="assemble",
    )(gathered)


def stream_places(order_row, length_row):
    places = (order_row[:, None] * BLOCK + jnp.arange(BLOCK, dtype=jnp.int32)[None, :]).reshape(-1)
    return places, stream_begins(places, length_row)


def stream_begins(places, length_row):
    ends = jnp.cumsum(length_row)
    starts = ends - length_row
    return jnp.max(jnp.where(starts[None, :] <= places[:, None], starts[None, :], 0), axis=1)


def rotary_tables(places, begins):
    entry = jnp.arange(128) % HD
    turned = entry < ROT
    index = jnp.where(entry < ROT // 2, entry, entry - ROT // 2)
    inverse = 1.0 / 10000.0 ** ((2 * index).astype(F32) / ROT)
    angles = (places - begins).astype(F32)[:, None] * jnp.where(turned, inverse, 0.0)[None, :]
    cosine, sine = jnp.cos(angles), jnp.sin(angles)
    lead = jnp.where((entry < ROT // 2)[None, :], -sine, 0.0)
    tail = jnp.where((turned & (entry >= ROT // 2))[None, :], sine, 0.0)
    return cosine, lead, tail


def take_columns(array, starts, width):
    return [lax.dynamic_slice_in_dim(array, s, width, 1) for s in starts]


def normalise(rows):
    centre = jnp.mean(rows, axis=1, keepdims=True)
    deviation = rows - centre
    inverse_std = lax.rsqrt(jnp.mean(deviation * deviation, axis=1, keepdims=True) + 1e-05)
    return deviation * inverse_std, inverse_std


def shards(
    hidden_in,
    out_grad,
    lengths,
    block_order,
    ln_gain,
    ln_bias,
    w_qkv,
    b_qkv,
    w_out,
    w_gate,
    w_up,
    w_down,
):
    parts = lax.axis_size("ctx")
    shard_count = lax.axis_size("fsdp")
    ctx_at = lax.axis_index("ctx")
    fsdp_at = lax.axis_index("fsdp")
    rows = hidden_in.shape[1]
    model = w_out.shape[1]
    hidden = w_gate.shape[1]
    tokens = rows * parts
    heads = model // HD // parts
    width = heads * HD
    shard_rows = w_qkv.shape[0]

    hidden_all = gather_ctx(hidden_in[0])
    grad_all = gather_ctx(out_grad[0])

    spread = (model // HD) % (shard_count * parts) == 0
    pieces = shard_count if spread else 1
    head_span = model // pieces
    head_width = head_span // parts
    head_starts = [
        s * model + p * head_span + ctx_at * head_width for s in range(3) for p in range(pieces)
    ]
    unit_span = hidden // shard_count
    unit_width = unit_span // parts
    unit_starts = [p * unit_span + ctx_at * unit_width for p in range(shard_count)]

    units = shard_count * unit_width
    spare = -units % 128
    empty = jnp.zeros((shard_rows, spare), BF)
    vectors = jnp.concatenate([ln_gain, ln_bias, b_qkv])
    vector_rows = -(-vectors.shape[0] // (3 * width)) + 15
    vector_rows = vector_rows // 16 * 16
    vectors = jnp.pad(vectors, (0, vector_rows * 3 * width - vectors.shape[0])).reshape(vector_rows, 3 * width)
    w_attn_own = jnp.concatenate(take_columns(w_qkv, head_starts, head_width), axis=1)
    w_attn_own = jnp.concatenate([w_attn_own, vectors], axis=0)
    attn_near = gather_first(w_attn_own)
    w_gate_own = jnp.concatenate(take_columns(w_gate, unit_starts, unit_width) + [empty], axis=1)
    gate_near = gather_first(w_gate_own)
    w_up_own = jnp.concatenate(take_columns(w_up, unit_starts, unit_width) + [empty], axis=1)
    attn_near, w_up_own = stage(attn_near, w_up_own)
    attn_far = gather_second(w_attn_own, attn_near)
    up_near = gather_first(w_up_own)
    gate_near, attn_far = stage(gate_near, attn_far)
    gate_far = gather_second(w_gate_own, gate_near)
    w_down_own = lax.dynamic_slice_in_dim(w_down, ctx_at * unit_width, unit_width, 0)
    if spread:
        w_out_own = lax.dynamic_slice_in_dim(w_out, ctx_at * head_width, head_width, 0)
        w_rest_own = jnp.concatenate([w_down_own, w_out_own], axis=0)
    else:
        w_rest_own = w_down_own
    attn_pieces = gathered_pieces(w_attn_own, attn_near, attn_far, shard_rows)
    vectors = gathered_rest(w_attn_own, attn_near, attn_far, shard_rows).reshape(shard_count, -1)
    gain_full = vectors[:, :shard_rows].reshape(-1).astype(F32)
    bias_full = vectors[:, shard_rows : 2 * shard_rows].reshape(-1).astype(F32)
    b_attn = vectors[:, 2 * shard_rows : 2 * shard_rows + b_qkv.shape[0]].reshape(-1).astype(F32)
    b_attn_own = jnp.concatenate([lax.dynamic_slice_in_dim(b_attn, s, head_width, 0) for s in head_starts])

    order_row = block_order[0]
    blocks = order_row.shape[0]
    places, begins = stream_places(order_row, lengths[0])
    tables = rotary_tables(places, begins)
    slots = jnp.sum(
        jnp.where(
            order_row[None, :] == jnp.arange(blocks, dtype=jnp.int32)[:, None],
            jnp.arange(blocks, dtype=jnp.int32)[None, :],
            0,
        ),
        axis=1,
    ).astype(jnp.int32)
    stream_starts = stream_begins(jnp.arange(tokens, dtype=jnp.int32), lengths[0]).astype(jnp.int32)
    lows = stream_starts[::CHUNK] // CHUNK
    stream_starts = stream_starts.reshape(tokens // CHUNK, 1, CHUNK)

    normed, merged = attn_side(hidden_all, gain_full[None], bias_full[None], b_attn_own[None], attn_pieces)
    merged, up_near, w_rest_own = stage(merged, up_near, w_rest_own)
    up_far = gather_second(w_up_own, up_near)
    rest_near = gather_first(w_rest_own)
    mixed, *kept = attention_forward(heads, slots, lows, merged, tables, stream_starts)
    mixed, gate_far, up_far, rest_near = stage(mixed, gate_far, up_far, rest_near)
    gate_pieces = gathered_pieces(w_gate_own, gate_near, gate_far, shard_rows)
    up_pieces = gathered_pieces(w_up_own, up_near, up_far, shard_rows)
    rest_far = gather_second(w_rest_own, rest_near)
    act, slope, silu = pair_side(normed, gate_pieces, up_pieces)
    if spread:
        me = lax.axis_index("fsdp")
        if shard_count == 4:
            rest_pieces = [w_rest_own, rest_near[0], rest_near[1], jnp.concatenate(rest_far, axis=0)]
            origin = [me, me ^ 1, me ^ 2, me ^ 3]
        else:
            rest_pieces = [rest_near[0].reshape(shard_count, -1, model)[i] for i in range(shard_count)]
            origin = list(range(shard_count))
        w_lower = placed([p[:unit_width] for p in rest_pieces], [o * unit_width for o in origin], units + spare)
        w_proj = placed([p[unit_width:] for p in rest_pieces], [o * head_width for o in origin], width)
    else:
        w_lower = placed(rest_near, [0], units + spare)
        w_proj = lax.dynamic_slice_in_dim(
            lax.all_gather(w_out, "fsdp", axis=0, tiled=True), ctx_at * width, width, 0
        )
    out_part = out_side(mixed, act, w_proj, w_lower)
    out_rows = scatter_ctx(out_part)

    (grad_all,) = tie([grad_all], [out_part])
    down_part = matmul_tn(act, grad_all).astype(BF)
    proj_part = matmul_tn(mixed, grad_all).astype(BF)
    if spread:
        rest_part = jnp.concatenate(
            [p.reshape(shard_count, -1, model) for p in (down_part[:units], proj_part)], axis=1
        ).reshape(-1, model)
    else:
        rest_part = down_part[:units]
    rest_part, grad_all = stage(rest_part, grad_all)
    rest_first = scatter_first(halves(rest_part))
    grad_gate, grad_up, grad_mixed = grad_side(grad_all, slope, silu, w_lower, w_proj)
    grad_gate, grad_up, grad_mixed, rest_first = stage(grad_gate, grad_up, grad_mixed, rest_first)

    rest_second = scatter_second(halves(rest_part), rest_first)
    gate_part = matmul_tn(normed, grad_gate).astype(BF)
    up_part = matmul_tn(normed, grad_up).astype(BF)
    rest_sum = jnp.concatenate(scatter_last(halves(rest_part), rest_first, rest_second), axis=1)
    gate_part, up_part, rest_sum, grad_mixed = stage(gate_part, up_part, rest_sum, grad_mixed)
    rest_all = gather_ctx(rest_sum)

    pair_first = scatter_first((gate_part, up_part))
    grad_merged = attention_backward(heads, slots, lows, kept, grad_mixed, tables, stream_starts)
    grad_merged, pair_first = stage(grad_merged, pair_first)

    pair_second = scatter_second((gate_part, up_part), pair_first)
    grad_part, terms = input_side(
        grad_gate, grad_up, grad_merged, hidden_all, gate_pieces, up_pieces, attn_pieces
    )
    merged_term = jnp.sum(grad_merged, axis=0, dtype=F32).reshape(3, pieces, 1, head_width)
    merged_term = jnp.where(
        lax.broadcasted_iota(jnp.int32, (3, pieces, parts, head_width), 2) == ctx_at, merged_term, 0.0
    )
    terms = jnp.concatenate([terms.reshape(-1), merged_term.reshape(-1)]).reshape(-1, 128)
    pair_sum = jnp.concatenate(
        [p[:, :units] for p in scatter_last((gate_part, up_part), pair_first, pair_second)], axis=1
    )
    grad_part, terms, pair_sum, grad_merged = stage(grad_part, terms, pair_sum, grad_merged)
    pair_all = gather_ctx(pair_sum[None])

    part_own, part_other = split_cores(grad_part)
    part_other = flip(part_other, "ctx", 0)
    other_terms = others_of(terms, "ctx", 1, 2)
    attn_part = matmul_tn(normed, grad_merged).astype(BF)
    attn_part, part_other, terms, others = stage(attn_part, part_other, terms, other_terms[0])
    terms = sum_of(terms, others, other_terms[1])
    part_places = (part_own.astype(F32) + part_other.astype(F32)).astype(BF)

    attn_first = scatter_first(halves(attn_part))
    other_terms = others_of(terms, "fsdp", 1, shard_count)
    attn_first, terms, others, part_places = stage(attn_first, terms, other_terms[0], part_places)
    terms = sum_of(terms, others, other_terms[1])
    grad_normed = scatter_places(part_places)

    attn_second = scatter_second(halves(attn_part), attn_first)
    attn_sum = jnp.concatenate(scatter_last(halves(attn_part), attn_first, attn_second), axis=1)
    attn_all = gather_ctx(attn_sum[None])
    other_terms = others_of(terms, "ctx", 2, parts // 2)
    terms, others = stage(terms, other_terms[0])
    terms = sum_of(terms, others, other_terms[1]).reshape(-1)

    float_in = hidden_in[0].astype(F32)
    (out_rows,) = tie([out_rows], [attn_sum, terms])
    output = (float_in + out_rows.astype(F32)).astype(BF)[None]
    (rest_all,) = tie([rest_all], [output])
    rest_blocks = rest_all.reshape(parts, -1, model)
    grad_down_w = rest_blocks[:, :unit_width].reshape(-1, model).astype(F32)
    if spread:
        grad_proj_w = rest_blocks[:, unit_width:].reshape(-1, model).astype(F32)
    else:
        grad_proj_w = lax.dynamic_slice_in_dim(
            gather_ctx(lax.psum(proj_part.astype(F32), "fsdp")), fsdp_at * shard_rows, shard_rows, 0
        )
    grad_down_w, grad_proj_w = stage(grad_down_w, grad_proj_w)
    (pair_all,) = tie([pair_all], [grad_down_w])

    pair_plan = [
        [
            (c, side * units + p * unit_width, unit_width)
            for p in range(shard_count)
            for c in range(parts)
        ]
        for side in range(2)
    ]
    attn_plan = [
        [
            (c, (s * pieces + p) * head_width, head_width)
            for s in range(3)
            for p in range(pieces)
            for c in range(parts)
        ]
    ]
    grad_gate_w, grad_up_w = assemble(pair_all, pair_plan)
    (grad_normed,) = tie([grad_normed], [grad_gate_w])
    grad_normed = grad_normed.astype(F32)

    normal_hat, inverse_std = normalise(float_in)
    b_rows = b_qkv.shape[0]
    grad_b_attn = lax.dynamic_slice_in_dim(terms, 2 * model + fsdp_at * b_rows, b_rows, 0)
    grad_gain = lax.dynamic_slice_in_dim(terms, fsdp_at * shard_rows, shard_rows, 0)
    grad_bias = lax.dynamic_slice_in_dim(terms, model + fsdp_at * shard_rows, shard_rows, 0)

    grad_hat = grad_normed * gain_full
    grad_in = out_grad[0].astype(F32) + inverse_std * (
        grad_hat
        - jnp.mean(grad_hat, axis=1, keepdims=True)
        - normal_hat * jnp.mean(grad_hat * normal_hat, axis=1, keepdims=True)
    )
    grad_in = grad_in.astype(BF)[None]
    (attn_all,) = tie([attn_all], [grad_in])
    (grad_attn_w,) = assemble(attn_all, attn_plan)
    return (
        output,
        grad_in,
        grad_gain,
        grad_bias,
        grad_attn_w,
        grad_b_attn,
        grad_proj_w,
        grad_gate_w,
        grad_up_w,
        grad_down_w,
    )


def solution(mesh):
    return jax.shard_map(
        shards,
        mesh=mesh,
        in_specs=(
            P("fsdp", "ctx", None),
            P("fsdp", "ctx", None),
            P("fsdp", None),
            P("fsdp", None),
            P("fsdp"),
            P("fsdp"),
            P("fsdp", None),
            P("fsdp"),
            P("fsdp", None),
            P("fsdp", None),
            P("fsdp", None),
            P("fsdp", None),
        ),
        out_specs=(
            P("fsdp", "ctx", None),
            P("fsdp", "ctx", None),
            P("fsdp"),
            P("fsdp"),
            P("fsdp", None),
            P("fsdp"),
            P("fsdp", None),
            P("fsdp", None),
            P("fsdp", None),
            P("fsdp", None),
        ),
        check_vma=False,
    )
```

```python
import functools

import jax
import jax.numpy as jnp
from jax import lax
from jax.experimental import pallas as pl
from jax.experimental.pallas import tpu as pltpu
from jax.sharding import PartitionSpec as P

HD = 64
ROT = 16
BLOCK = 128
CHUNK = 256
BF = jnp.bfloat16
F32 = jnp.float32
MASKED = -1e30


def matmul(left, right):
    return jnp.dot(left, right, preferred_element_type=F32)


def matmul_nt(left, right):
    return lax.dot_general(left, right, (((1,), (1,)), ((), ())), preferred_element_type=F32)


def matmul_tn(left, right):
    return lax.dot_general(left, right, (((0,), (0,)), ((), ())), preferred_element_type=F32)


def flip(values, axis, bit):
    count = lax.axis_size(axis)
    return lax.ppermute(values, axis, [(i, i ^ (1 << bit)) for i in range(count)])


def bits_of(count):
    bits = count.bit_length() - 1
    assert count == 1 << bits
    return bits


def gather_rows(values, axis, order):
    me = lax.axis_index(axis)
    count = lax.axis_size(axis)
    held = values[None]
    steps = [0]
    for bit in order:
        other = flip(held, axis, bit)
        held = jnp.concatenate([held, other], axis=0)
        steps = steps + [s ^ (1 << bit) for s in steps]
    rows = values.shape[0]
    out = jnp.zeros((count * rows,) + values.shape[1:], values.dtype)
    for place, step in enumerate(steps):
        out = lax.dynamic_update_slice_in_dim(out, held[place], (me ^ step) * rows, 0)
    return out


def placed(pieces, places, total):
    out = jnp.zeros((total,) + pieces[0].shape[1:], pieces[0].dtype)
    for piece, place in zip(pieces, places):
        out = lax.dynamic_update_slice_in_dim(out, piece, place, 0)
    return out


def gather_first(values):
    if lax.axis_size("fsdp") != 4:
        return [gather_rows(values, "fsdp", list(range(bits_of(lax.axis_size("fsdp")))))]
    return [flip(values, "fsdp", 0), flip(values, "fsdp", 1)]


def gather_second(values, first):
    if lax.axis_size("fsdp") != 4:
        return []
    half = values.shape[0] // 2 // 16 * 16
    return [flip(first[0][:half], "fsdp", 1), flip(first[1][half:], "fsdp", 0)]


def gathered_pieces(values, first, second, rows):
    count = lax.axis_size("fsdp")
    shard = values.shape[0]
    if count != 4:
        return [(first[0], i * shard, rows, i * rows) for i in range(count)]
    me = lax.axis_index("fsdp")
    half = shard // 2 // 16 * 16
    return [
        (values, 0, rows, me * rows),
        (first[0], 0, rows, (me ^ 1) * rows),
        (first[1], 0, rows, (me ^ 2) * rows),
        (second[0], 0, half, (me ^ 3) * rows),
        (second[1], 0, rows - half, (me ^ 3) * rows + half),
    ]


def gathered_rest(values, first, second, rows):
    count = lax.axis_size("fsdp")
    shard = values.shape[0]
    if count != 4:
        return first[0].reshape(count, shard, -1)[:, rows:]
    me = lax.axis_index("fsdp")
    half = shard // 2 // 16 * 16
    tails = [values[rows:], first[0][rows:], first[1][rows:], second[1][rows - half :]]
    return placed([t[None] for t in tails], [me, me ^ 1, me ^ 2, me ^ 3], count)


def others_of(values, axis, stride, count):
    size = lax.axis_size(axis)
    digit = lax.axis_index(axis) // stride % count

    def moved(i, by):
        at = i // stride % count
        return i + ((at + by) % count - at) * stride

    return [lax.ppermute(values, axis, [(i, moved(i, by)) for i in range(size)]) for by in range(1, count)], digit


def sum_of(values, others, digit):
    count = len(others) + 1
    out = jnp.zeros((count,) + values.shape, values.dtype)
    for by, piece in enumerate([values] + others):
        out = lax.dynamic_update_slice_in_dim(out, piece[None], (digit + count - by) % count, 0)
    total = out[0]
    for at in range(1, count):
        total = total + out[at]
    return total


def scatter_rows(values, axis, order):
    me = lax.axis_index(axis)
    count = lax.axis_size(axis)
    bits = bits_of(count)
    rows = values.shape[0] // count
    held = values.reshape((2,) * bits + (rows,) + values.shape[1:])
    left = list(range(bits))
    for bit in order:
        at = len(left) - 1 - left.index(bit)
        mine = (me >> bit) & 1
        sent = lax.dynamic_index_in_dim(held, 1 - mine, at, keepdims=False).astype(BF)
        kept = lax.dynamic_index_in_dim(held, mine, at, keepdims=False)
        held = kept.astype(F32) + flip(sent, axis, bit).astype(F32)
        left.remove(bit)
    return held


def fsdp_block(part, index):
    rows = part.shape[0] // lax.axis_size("fsdp")
    return lax.dynamic_slice_in_dim(part, index * rows, rows, 0)


def halves(part):
    half = part.shape[1] // 2 // 128 * 128
    return part[:, :half], part[:, half:]


def scatter_first(sides):
    if lax.axis_size("fsdp") != 4:
        return [scatter_rows(part, "fsdp", list(range(bits_of(lax.axis_size("fsdp"))))) for part in sides]
    me = lax.axis_index("fsdp")
    return [
        flip(jnp.stack([fsdp_block(sides[1], me ^ 3), fsdp_block(sides[1], me ^ 1)]), "fsdp", 0),
        flip(jnp.stack([fsdp_block(sides[0], me ^ 3), fsdp_block(sides[0], me ^ 2)]), "fsdp", 1),
    ]


def scatter_second(sides, first):
    if lax.axis_size("fsdp") != 4:
        return []
    me = lax.axis_index("fsdp")
    across = fsdp_block(sides[0], me ^ 1).astype(F32) + first[1][0].astype(F32)
    along = fsdp_block(sides[1], me ^ 2).astype(F32) + first[0][0].astype(F32)
    return [flip(across.astype(BF), "fsdp", 0), flip(along.astype(BF), "fsdp", 1)]


def scatter_last(sides, first, second):
    if lax.axis_size("fsdp") != 4:
        return first[0].astype(BF), first[1].astype(BF)
    me = lax.axis_index("fsdp")
    left = fsdp_block(sides[0], me).astype(F32) + first[1][1].astype(F32) + second[0].astype(F32)
    right = fsdp_block(sides[1], me).astype(F32) + first[0][1].astype(F32) + second[1].astype(F32)
    return left.astype(BF), right.astype(BF)


def gather_ctx(values):
    return lax.all_gather(values, "ctx", axis=0, tiled=True)


def split_cores(part):
    parts = lax.axis_size("ctx")
    core = lax.axis_index("ctx") % 2
    blocks = part.reshape(parts // 2, 2, part.shape[0] // parts, part.shape[1])
    return [lax.dynamic_index_in_dim(blocks, k, 1, keepdims=False) for k in (core, 1 - core)]


def scatter_ctx(values):
    return lax.psum_scatter(values, "ctx", scatter_dimension=0, tiled=True)


def shift(values, by, keep):
    places = lax.axis_size("ctx") // 2
    pairs = [
        (2 * p + k, 2 * (p + by) + k) for p in range(places) for k in range(2) if keep(p) and 0 <= p + by < places
    ]
    return lax.ppermute(values, "ctx", pairs)


def line_block(blocks, s):
    places = blocks.shape[0]
    at = (lax.axis_index("ctx") // 2 + places - s) % places
    return lax.dynamic_index_in_dim(blocks, at, 0, keepdims=False).astype(F32)


def line_step(blocks, step, before):
    places = blocks.shape[0]
    up, down = line_block(blocks, step), line_block(blocks, places - step)
    if before:
        up, down = up + before[0].astype(F32), down + before[1].astype(F32)
    return [
        shift(up.astype(BF), 1, lambda p: p <= step - 1),
        shift(down.astype(BF), -1, lambda p: p >= places - step),
    ]


def nothing_kernel(*refs):
    return None


def tie(values, after):
    anywhere = pl.BlockSpec(memory_space=pl.ANY)
    return pl.pallas_call(
        nothing_kernel,
        out_shape=tuple(jax.ShapeDtypeStruct(v.shape, v.dtype) for v in values),
        in_specs=[anywhere] * (len(values) + len(after)),
        out_specs=tuple([anywhere] * len(values)),
        input_output_aliases={i: i for i in range(len(values))},
        name="tie",
    )(*values, *after)


def stage(*groups):
    leaves, tree = jax.tree.flatten(groups)
    return jax.tree.unflatten(tree, tie(leaves, []))


def rows_at(index, size):
    return pl.ds(pl.multiple_of(index * size, size), size)


def turn(values, tables, rows, direction):
    width = values.shape[1]
    cosine, lead, tail = (jnp.concatenate([ref[rows, :]] * (width // 128), axis=1) for ref in tables)
    ahead = pltpu.roll(values, width - ROT // 2, 1)
    behind = pltpu.roll(values, ROT // 2, 1)
    return values * cosine + direction * (ahead * lead + behind * tail)


def split_heads(target, values, heads):
    head_of = lax.broadcasted_iota(jnp.int32, values.shape, 1) // HD
    for h in range(heads):
        target[h * CHUNK : (h + 1) * CHUNK, :] = jnp.where(head_of == h, values, jnp.zeros_like(values))


def visible(i, j, begin):
    key_at = lax.broadcasted_iota(jnp.int32, (CHUNK, CHUNK), 0)
    query_at = lax.broadcasted_iota(jnp.int32, (CHUNK, CHUNK), 1)
    return (key_at - query_at <= (i - j) * CHUNK) & (key_at >= begin - j * CHUNK)


def forward_kernel(
    heads,
    slot_ref,
    low_ref,
    merged_ref,
    cos_ref,
    lead_ref,
    tail_ref,
    begin_ref,
    mixed_ref,
    q_ref,
    k_ref,
    v_ref,
    total_ref,
    ot_ref,
    vt_ref,
    qm_ref,
    s_ref,
):
    width = heads * HD
    tokens = merged_ref.shape[0]
    tables = (cos_ref, lead_ref, tail_ref)

    def prepare(block, carry):
        source = rows_at(slot_ref[block], BLOCK)
        target = rows_at(block, BLOCK)
        query = turn(merged_ref[source, 0:width], tables, source, 1.0).astype(BF)
        key = turn(merged_ref[source, width : 2 * width], tables, source, 1.0).astype(BF)
        value = merged_ref[source, 2 * width : 3 * width].astype(BF)
        q_ref[target, :] = query * jnp.asarray(HD ** (-0.5), BF)
        k_ref[target, :] = key
        v_ref[target, :] = value
        vt_ref[:, target] = value.T
        return carry

    lax.fori_loop(0, tokens // BLOCK, prepare, 0)

    def query_chunk(i, carry):
        here = rows_at(i, CHUNK)
        split_heads(qm_ref, q_ref[here, :], heads)
        ot_ref[:, here] = jnp.zeros((width, CHUNK), F32)
        low = low_ref[i]
        begin = begin_ref[i]

        def score(j, tops):
            there = rows_at(j, CHUNK)
            key = k_ref[there, :]
            allowed = visible(i, j, begin)
            out = []
            for h in range(heads):
                s = matmul_nt(key, qm_ref[h * CHUNK : (h + 1) * CHUNK, :])
                s = jnp.where(allowed, s, MASKED)
                s_ref[h, there, :] = s
                out.append(jnp.maximum(tops[h], jnp.max(s, axis=0, keepdims=True)))
            return tuple(out)

        tops = lax.fori_loop(
            low, i + 1, score, tuple(jnp.full((1, CHUNK), MASKED, F32) for _ in range(heads))
        )

        def value_side(j, sums):
            there = rows_at(j, CHUNK)
            out = []
            for h in range(heads):
                span = slice(h * HD, (h + 1) * HD)
                e = jnp.exp(s_ref[h, there, :] - tops[h])
                out.append(sums[h] + jnp.sum(e, axis=0, keepdims=True))
                ot_ref[span, here] += matmul(vt_ref[span, there], e.astype(BF))
            return tuple(out)

        sums = lax.fori_loop(low, i + 1, value_side, tuple(jnp.zeros((1, CHUNK), F32) for _ in range(heads)))
        for h in range(heads):
            span = slice(h * HD, (h + 1) * HD)
            ot_ref[span, here] = ot_ref[span, here] * (1.0 / sums[h])
            total_ref[i, h : h + 1, :] = tops[h] + jnp.log(sums[h])
        mixed = ot_ref[:, here].T.astype(BF)
        for part in range(CHUNK // BLOCK):
            target = rows_at(slot_ref[i * (CHUNK // BLOCK) + part], BLOCK)
            mixed_ref[target, :] = mixed[part * BLOCK : (part + 1) * BLOCK]
        return carry

    lax.fori_loop(0, tokens // CHUNK, query_chunk, 0)


def backward_kernel(
    heads,
    slot_ref,
    low_ref,
    q_ref,
    k_ref,
    v_ref,
    total_ref,
    ot_ref,
    grad_mixed_ref,
    cos_ref,
    lead_ref,
    tail_ref,
    begin_ref,
    grad_merged_ref,
    kt_ref,
    qm_ref,
    gm_ref,
    p_ref,
    ds_ref,
    dqt_ref,
    dk_ref,
    dv_ref,
):
    width = heads * HD
    tokens = q_ref.shape[0]
    tables = (cos_ref, lead_ref, tail_ref)

    def prepare(block, carry):
        here = rows_at(block, BLOCK)
        kt_ref[:, here] = k_ref[here, :].T
        dk_ref[here, :] = jnp.zeros((BLOCK, width), F32)
        dv_ref[here, :] = jnp.zeros((BLOCK, width), F32)
        return carry

    lax.fori_loop(0, tokens // BLOCK, prepare, 0)

    def query_chunk(i, carry):
        here = rows_at(i, CHUNK)
        targets = [rows_at(slot_ref[i * (CHUNK // BLOCK) + part], BLOCK) for part in range(CHUNK // BLOCK)]
        grad = jnp.concatenate([grad_mixed_ref[target, :] for target in targets], axis=0)
        split_heads(qm_ref, q_ref[here, :], heads)
        split_heads(gm_ref, grad, heads)
        dqt_ref[...] = jnp.zeros_like(dqt_ref)
        product = grad.T.astype(F32) * ot_ref[:, here]
        dots = [jnp.sum(product[h * HD : (h + 1) * HD], axis=0, keepdims=True) for h in range(heads)]
        totals = [total_ref[i, h : h + 1, :] for h in range(heads)]
        begin = begin_ref[i]

        def key_chunk(j, carry):
            there = rows_at(j, CHUNK)
            key = k_ref[there, :]
            value = v_ref[there, :]
            allowed = visible(i, j, begin)
            for h in range(heads):
                span = slice(h * HD, (h + 1) * HD)
                part = slice(h * CHUNK, (h + 1) * CHUNK)
                s = matmul_nt(key, qm_ref[part, :])
                probs = jnp.exp(jnp.where(allowed, s, MASKED) - totals[h])
                p_ref[:, part] = probs.astype(BF)
                ds = (probs * (matmul_nt(value, gm_ref[part, :]) - dots[h])).astype(BF)
                ds_ref[:, part] = ds
                dqt_ref[span, :] += matmul(kt_ref[span, there], ds)
            dv_ref[there, :] += matmul(p_ref[...], gm_ref[...])
            dk_ref[there, :] += matmul(ds_ref[...], qm_ref[...])
            return carry

        lax.fori_loop(low_ref[i], i + 1, key_chunk, 0)
        grad_query = dqt_ref[...].T * HD ** (-0.5)
        for part, target in enumerate(targets):
            rows = slice(part * BLOCK, (part + 1) * BLOCK)
            grad_merged_ref[target, 0:width] = turn(grad_query[rows], tables, target, -1.0).astype(BF)
        return carry

    lax.fori_loop(0, tokens // CHUNK, query_chunk, 0)

    def finish(block, carry):
        source = rows_at(block, BLOCK)
        target = rows_at(slot_ref[block], BLOCK)
        grad_merged_ref[target, width : 2 * width] = turn(dk_ref[source, :], tables, target, -1.0).astype(BF)
        grad_merged_ref[target, 2 * width : 3 * width] = dv_ref[source, :].astype(BF)
        return carry

    lax.fori_loop(0, tokens // BLOCK, finish, 0)


WHOLE = pl.BlockSpec(memory_space=pltpu.VMEM)
SCALAR = pl.BlockSpec(memory_space=pltpu.SMEM)
ANYWHERE = pl.BlockSpec(memory_space=pl.ANY)


def attention_forward(heads, slots, lows, merged, tables, begins):
    tokens = merged.shape[0]
    width = heads * HD
    rows = jax.ShapeDtypeStruct((tokens, width), BF)
    return pl.pallas_call(
        functools.partial(forward_kernel, heads),
        out_shape=(
            rows,
            rows,
            rows,
            rows,
            jax.ShapeDtypeStruct((tokens // CHUNK, heads, CHUNK), F32),
            jax.ShapeDtypeStruct((width, tokens), F32),
        ),
        in_specs=[SCALAR, SCALAR] + [WHOLE] * 5,
        out_specs=(WHOLE,) * 6,
        scratch_shapes=[
            pltpu.VMEM((width, tokens), BF),
            pltpu.VMEM((heads * CHUNK, width), BF),
            pltpu.VMEM((heads, tokens, CHUNK), F32),
        ],
        compiler_params=pltpu.CompilerParams(vmem_limit_bytes=48 * 1024 * 1024),
        cost_estimate=pl.CostEstimate(flops=25_000_000_000, transcendentals=0, bytes_accessed=0),
        name="attention_forward",
    )(slots, lows, merged, *tables, begins)


def attention_backward(heads, slots, lows, kept, grad_mixed, tables, begins):
    tokens, width = grad_mixed.shape
    return pl.pallas_call(
        functools.partial(backward_kernel, heads),
        out_shape=jax.ShapeDtypeStruct((tokens, 3 * width), BF),
        in_specs=[SCALAR, SCALAR] + [WHOLE] * 10,
        out_specs=WHOLE,
        scratch_shapes=[
            pltpu.VMEM((width, tokens), BF),
            pltpu.VMEM((heads * CHUNK, width), BF),
            pltpu.VMEM((heads * CHUNK, width), BF),
            pltpu.VMEM((CHUNK, heads * CHUNK), BF),
            pltpu.VMEM((CHUNK, heads * CHUNK), BF),
            pltpu.VMEM((width, CHUNK), F32),
            pltpu.VMEM((tokens, width), F32),
            pltpu.VMEM((tokens, width), F32),
        ],
        compiler_params=pltpu.CompilerParams(vmem_limit_bytes=48 * 1024 * 1024),
        cost_estimate=pl.CostEstimate(flops=40_000_000_000, transcendentals=0, bytes_accessed=0),
        name="attention_backward",
    )(slots, lows, *kept, grad_mixed, *tables, begins)


def fetch(at_ref, pieces, spans, target, sem):
    copies = []
    for n, (piece, (first, rows)) in enumerate(zip(pieces, spans)):
        place = pl.ds(pl.multiple_of(at_ref[n], 16), rows)
        copies.append(pltpu.make_async_copy(piece.at[pl.ds(first, rows), :], target.at[place, :], sem.at[n]))
    for copy in copies:
        copy.start()
    return copies


def attn_kernel(spans, at_ref, hidden_ref, gain_ref, bias_ref, shift_ref, *refs):
    n = len(spans)
    normed_ref, merged_ref, w_attn, sem = refs[n:]

    @pl.when(pl.program_id(0) == 0)
    def _():
        for copy in fetch(at_ref, refs[:n], spans, w_attn, sem):
            copy.wait()

    normal, _ = normalise(hidden_ref[...].astype(F32))
    normed = (normal * gain_ref[...] + bias_ref[...]).astype(BF)
    normed_ref[...] = normed
    merged_ref[...] = matmul(normed, w_attn[...]) + shift_ref[...]


def pair_kernel(spans, at_ref, normed_ref, *refs):
    n = len(spans)
    gate_pieces, up_pieces = refs[:n], refs[n : 2 * n]
    act_ref, slope_ref, silu_ref, w_gate, w_up, *sems = refs[2 * n :]

    @pl.when(pl.program_id(0) == 0)
    def _():
        copies = fetch(at_ref, gate_pieces, spans, w_gate, sems[0])
        copies += fetch(at_ref, up_pieces, spans, w_up, sems[1])
        for copy in copies:
            copy.wait()

    normed = normed_ref[...]
    gating = matmul(normed, w_gate[...])
    rising = matmul(normed, w_up[...])
    sigma = jax.nn.sigmoid(gating)
    silu = gating * sigma
    act_ref[...] = (silu * rising).astype(BF)
    slope_ref[...] = (rising * sigma * (1.0 + gating * (1.0 - sigma))).astype(BF)
    silu_ref[...] = silu.astype(BF)


def row_block(width):
    return pl.BlockSpec((CHUNK, width), lambda i: (i, 0))


def full_block(array):
    return pl.BlockSpec(array.shape, lambda i: (0, 0))


def split_pieces(pieces):
    at = jnp.stack([jnp.asarray(piece[3], jnp.int32) for piece in pieces])
    return at, [piece[0] for piece in pieces], tuple((piece[1], piece[2]) for piece in pieces)


def attn_side(hidden, gain, bias, shift, pieces):
    tokens, model = hidden.shape
    at, arrays, spans = split_pieces(pieces)
    n = len(spans)
    width = arrays[0].shape[1]
    return pl.pallas_call(
        functools.partial(attn_kernel, spans),
        grid=(tokens // CHUNK,),
        out_shape=(jax.ShapeDtypeStruct((tokens, model), BF), jax.ShapeDtypeStruct((tokens, width), F32)),
        in_specs=[SCALAR, row_block(model), full_block(gain), full_block(bias), full_block(shift)] + [ANYWHERE] * n,
        out_specs=(row_block(model), row_block(width)),
        scratch_shapes=[pltpu.VMEM((model, width), BF), pltpu.SemaphoreType.DMA((n,))],
        compiler_params=pltpu.CompilerParams(vmem_limit_bytes=56 * 1024 * 1024),
        cost_estimate=pl.CostEstimate(flops=18_000_000_000, transcendentals=0, bytes_accessed=0),
        name="attn_side",
    )(at, hidden, gain, bias, shift, *arrays)


def pair_side(normed, gate_pieces, up_pieces):
    tokens, model = normed.shape
    at, gates, spans = split_pieces(gate_pieces)
    ups = split_pieces(up_pieces)[1]
    n = len(spans)
    units = gates[0].shape[1]
    return pl.pallas_call(
        functools.partial(pair_kernel, spans),
        grid=(tokens // CHUNK,),
        out_shape=(jax.ShapeDtypeStruct((tokens, units), BF),) * 3,
        in_specs=[SCALAR, row_block(model)] + [ANYWHERE] * (2 * n),
        out_specs=(row_block(units),) * 3,
        scratch_shapes=[
            pltpu.VMEM((model, units), BF),
            pltpu.VMEM((model, units), BF),
            pltpu.SemaphoreType.DMA((n,)),
            pltpu.SemaphoreType.DMA((n,)),
        ],
        compiler_params=pltpu.CompilerParams(vmem_limit_bytes=56 * 1024 * 1024),
        cost_estimate=pl.CostEstimate(flops=28_000_000_000, transcendentals=0, bytes_accessed=0),
        name="pair_side",
    )(at, normed, *gates, *ups)


def fetch_rest(spans, at_ref, refs, lower, proj, sems):
    n = len(spans) // 2
    units = lower.shape[0]
    filled = sum(rows for _, rows in spans[:n])
    if filled < units:
        lower[filled:, :] = jnp.zeros((units - filled, lower.shape[1]), BF)
    copies = fetch(at_ref.at[0], refs[:n], spans[:n], lower, sems[0])
    copies += fetch(at_ref.at[1], refs[n:], spans[n:], proj, sems[1])
    for copy in copies:
        copy.wait()


def grad_kernel(spans, at_ref, grad_ref, slope_ref, silu_ref, *refs):
    n = len(spans)
    gate_ref, up_ref, mixed_ref, lower, proj, *sems = refs[n:]

    @pl.when(pl.program_id(0) == 0)
    def _():
        fetch_rest(spans, at_ref, refs[:n], lower, proj, sems)

    grad = grad_ref[...]
    act = matmul_nt(grad, lower[...])
    mixed_ref[...] = matmul_nt(grad, proj[...]).astype(BF)
    gate_ref[...] = (act * slope_ref[...].astype(F32)).astype(BF)
    up_ref[...] = (act * silu_ref[...].astype(F32)).astype(BF)


def rest_scratch(units, width, model, n):
    return [
        pltpu.VMEM((units, model), BF),
        pltpu.VMEM((width, model), BF),
        pltpu.SemaphoreType.DMA((n,)),
        pltpu.SemaphoreType.DMA((n,)),
    ]


def split_rest(lower_pieces, proj_pieces):
    lower_at, lowers, lower_spans = split_pieces(lower_pieces)
    proj_at, projs, proj_spans = split_pieces(proj_pieces)
    return jnp.stack([lower_at, proj_at]), lowers + projs, lower_spans + proj_spans


def grad_side(grad, slope, silu, width, lower_pieces, proj_pieces):
    tokens, model = grad.shape
    units = slope.shape[1]
    at, arrays, spans = split_rest(lower_pieces, proj_pieces)
    return pl.pallas_call(
        functools.partial(grad_kernel, spans),
        grid=(tokens // CHUNK,),
        out_shape=(
            jax.ShapeDtypeStruct((tokens, units), BF),
            jax.ShapeDtypeStruct((tokens, units), BF),
            jax.ShapeDtypeStruct((tokens, width), BF),
        ),
        in_specs=[SCALAR, row_block(model), row_block(units), row_block(units)] + [ANYWHERE] * len(arrays),
        out_specs=(row_block(units), row_block(units), row_block(width)),
        scratch_shapes=rest_scratch(units, width, model, len(arrays) // 2),
        compiler_params=pltpu.CompilerParams(vmem_limit_bytes=56 * 1024 * 1024),
        cost_estimate=pl.CostEstimate(flops=18_000_000_000, transcendentals=0, bytes_accessed=0),
        name="grad_side",
    )(at, grad, slope, silu, *arrays)


def out_kernel(spans, at_ref, mixed_ref, act_ref, *refs):
    n = len(spans)
    out_ref, lower, proj, *sems = refs[n:]

    @pl.when(pl.program_id(0) == 0)
    def _():
        fetch_rest(spans, at_ref, refs[:n], lower, proj, sems)

    out_ref[...] = (matmul(mixed_ref[...], proj[...]) + matmul(act_ref[...], lower[...])).astype(BF)


def out_side(mixed, act, model, lower_pieces, proj_pieces):
    tokens, width = mixed.shape
    units = act.shape[1]
    at, arrays, spans = split_rest(lower_pieces, proj_pieces)
    return pl.pallas_call(
        functools.partial(out_kernel, spans),
        grid=(tokens // CHUNK,),
        out_shape=jax.ShapeDtypeStruct((tokens, model), BF),
        in_specs=[SCALAR, row_block(width), row_block(units)] + [ANYWHERE] * len(arrays),
        out_specs=row_block(model),
        scratch_shapes=rest_scratch(units, width, model, len(arrays) // 2),
        compiler_params=pltpu.CompilerParams(vmem_limit_bytes=56 * 1024 * 1024),
        cost_estimate=pl.CostEstimate(flops=15_000_000_000, transcendentals=0, bytes_accessed=0),
        name="out_side",
    )(at, mixed, act, *arrays)


def input_kernel(spans, at_ref, gate_ref, up_ref, merged_ref, hidden_ref, *refs):
    n = len(spans)
    gate_pieces, up_pieces, attn_pieces = refs[:n], refs[n : 2 * n], refs[2 * n : 3 * n]
    part_ref, terms_ref, w_gate, w_up, w_attn, *sems = refs[3 * n :]

    @pl.when(pl.program_id(0) == 0)
    def _():
        copies = fetch(at_ref, gate_pieces, spans, w_gate, sems[0])
        copies += fetch(at_ref, up_pieces, spans, w_up, sems[1])
        copies += fetch(at_ref, attn_pieces, spans, w_attn, sems[2])
        terms_ref[...] = jnp.zeros_like(terms_ref)
        for copy in copies:
            copy.wait()

    part = matmul_nt(gate_ref[...], w_gate[...]) + matmul_nt(up_ref[...], w_up[...])
    part = part + matmul_nt(merged_ref[...], w_attn[...])
    part_ref[...] = part.astype(BF)
    normal, _ = normalise(hidden_ref[...].astype(F32))
    terms_ref[0:1, :] += jnp.sum(part * normal, axis=0, keepdims=True)
    terms_ref[1:2, :] += jnp.sum(part, axis=0, keepdims=True)


def input_side(grad_gate, grad_up, grad_merged, hidden, gate_pieces, up_pieces, attn_pieces):
    tokens, model = hidden.shape
    at, gates, spans = split_pieces(gate_pieces)
    ups, attns = split_pieces(up_pieces)[1], split_pieces(attn_pieces)[1]
    n = len(spans)
    units, width = grad_gate.shape[1], grad_merged.shape[1]
    return pl.pallas_call(
        functools.partial(input_kernel, spans),
        grid=(tokens // CHUNK,),
        out_shape=(jax.ShapeDtypeStruct((tokens, model), BF), jax.ShapeDtypeStruct((2, model), F32)),
        in_specs=[SCALAR, row_block(units), row_block(units), row_block(width), row_block(model)]
        + [ANYWHERE] * (3 * n),
        out_specs=(row_block(model), pl.BlockSpec((2, model), lambda i: (0, 0))),
        scratch_shapes=[
            pltpu.VMEM((model, units), BF),
            pltpu.VMEM((model, units), BF),
            pltpu.VMEM((model, width), BF),
            pltpu.SemaphoreType.DMA((n,)),
            pltpu.SemaphoreType.DMA((n,)),
            pltpu.SemaphoreType.DMA((n,)),
        ],
        compiler_params=pltpu.CompilerParams(vmem_limit_bytes=56 * 1024 * 1024),
        cost_estimate=pl.CostEstimate(flops=30_000_000_000, transcendentals=0, bytes_accessed=0),
        name="input_side",
    )(at, grad_gate, grad_up, grad_merged, hidden, *gates, *ups, *attns)


def assemble_kernel(plan, source_ref, *targets):
    for target, pieces in zip(targets, plan):
        at = 0
        for part, offset, width in pieces:
            target[:, at : at + width] = source_ref[part, :, offset : offset + width].astype(F32)
            at += width


def assemble(gathered, plan):
    parts, rows, columns = gathered.shape
    step = 64
    widths = [sum(piece[2] for piece in pieces) for pieces in plan]
    return pl.pallas_call(
        functools.partial(assemble_kernel, plan),
        grid=(rows // step,),
        out_shape=tuple(jax.ShapeDtypeStruct((rows, w), F32) for w in widths),
        in_specs=[pl.BlockSpec((parts, step, columns), lambda i: (0, i, 0))],
        out_specs=tuple(pl.BlockSpec((step, w), lambda i: (i, 0)) for w in widths),
        compiler_params=pltpu.CompilerParams(vmem_limit_bytes=40 * 1024 * 1024),
        name="assemble",
    )(gathered)


def stream_places(order_row, length_row):
    places = (order_row[:, None] * BLOCK + jnp.arange(BLOCK, dtype=jnp.int32)[None, :]).reshape(-1)
    return places, stream_begins(places, length_row)


def stream_begins(places, length_row):
    ends = jnp.cumsum(length_row)
    starts = ends - length_row
    return jnp.max(jnp.where(starts[None, :] <= places[:, None], starts[None, :], 0), axis=1)


def rotary_tables(places, begins):
    entry = jnp.arange(128) % HD
    turned = entry < ROT
    index = jnp.where(entry < ROT // 2, entry, entry - ROT // 2)
    inverse = 1.0 / 10000.0 ** ((2 * index).astype(F32) / ROT)
    angles = (places - begins).astype(F32)[:, None] * jnp.where(turned, inverse, 0.0)[None, :]
    cosine, sine = jnp.cos(angles), jnp.sin(angles)
    lead = jnp.where((entry < ROT // 2)[None, :], -sine, 0.0)
    tail = jnp.where((turned & (entry >= ROT // 2))[None, :], sine, 0.0)
    return cosine, lead, tail


def take_columns(array, starts, width):
    return [lax.dynamic_slice_in_dim(array, s, width, 1) for s in starts]


def normalise(rows):
    centre = jnp.mean(rows, axis=1, keepdims=True)
    deviation = rows - centre
    inverse_std = lax.rsqrt(jnp.mean(deviation * deviation, axis=1, keepdims=True) + 1e-05)
    return deviation * inverse_std, inverse_std


def shards(
    hidden_in,
    out_grad,
    lengths,
    block_order,
    ln_gain,
    ln_bias,
    w_qkv,
    b_qkv,
    w_out,
    w_gate,
    w_up,
    w_down,
):
    parts = lax.axis_size("ctx")
    shard_count = lax.axis_size("fsdp")
    ctx_at = lax.axis_index("ctx")
    fsdp_at = lax.axis_index("fsdp")
    rows = hidden_in.shape[1]
    model = w_out.shape[1]
    hidden = w_gate.shape[1]
    tokens = rows * parts
    heads = model // HD // parts
    width = heads * HD
    shard_rows = w_qkv.shape[0]

    hidden_all = gather_ctx(hidden_in[0])
    grad_all = gather_ctx(out_grad[0])

    spread = (model // HD) % (shard_count * parts) == 0
    pieces = shard_count if spread else 1
    head_span = model // pieces
    head_width = head_span // parts
    head_starts = [
        s * model + p * head_span + ctx_at * head_width for s in range(3) for p in range(pieces)
    ]
    unit_span = hidden // shard_count
    unit_width = unit_span // parts
    unit_starts = [p * unit_span + ctx_at * unit_width for p in range(shard_count)]

    units = shard_count * unit_width
    spare = -units % 128
    empty = jnp.zeros((shard_rows, spare), BF)
    vectors = jnp.concatenate([ln_gain, ln_bias, b_qkv])
    vector_rows = -(-vectors.shape[0] // (3 * width)) + 15
    vector_rows = vector_rows // 16 * 16
    vectors = jnp.pad(vectors, (0, vector_rows * 3 * width - vectors.shape[0])).reshape(vector_rows, 3 * width)
    w_attn_own = jnp.concatenate(take_columns(w_qkv, head_starts, head_width), axis=1)
    w_attn_own = jnp.concatenate([w_attn_own, vectors], axis=0)
    attn_near = gather_first(w_attn_own)
    w_gate_own = jnp.concatenate(take_columns(w_gate, unit_starts, unit_width) + [empty], axis=1)
    gate_near = gather_first(w_gate_own)
    w_up_own = jnp.concatenate(take_columns(w_up, unit_starts, unit_width) + [empty], axis=1)
    attn_near, w_up_own = stage(attn_near, w_up_own)
    attn_far = gather_second(w_attn_own, attn_near)
    up_near = gather_first(w_up_own)
    gate_near, attn_far = stage(gate_near, attn_far)
    gate_far = gather_second(w_gate_own, gate_near)
    w_down_own = lax.dynamic_slice_in_dim(w_down, ctx_at * unit_width, unit_width, 0)
    if spread:
        w_out_own = lax.dynamic_slice_in_dim(w_out, ctx_at * head_width, head_width, 0)
        w_rest_own = jnp.concatenate([w_down_own, w_out_own], axis=0)
    else:
        w_rest_own = w_down_own
    attn_pieces = gathered_pieces(w_attn_own, attn_near, attn_far, shard_rows)
    vectors = gathered_rest(w_attn_own, attn_near, attn_far, shard_rows).reshape(shard_count, -1)
    gain_full = vectors[:, :shard_rows].reshape(-1).astype(F32)
    bias_full = vectors[:, shard_rows : 2 * shard_rows].reshape(-1).astype(F32)
    b_attn = vectors[:, 2 * shard_rows : 2 * shard_rows + b_qkv.shape[0]].reshape(-1).astype(F32)
    b_attn_own = jnp.concatenate([lax.dynamic_slice_in_dim(b_attn, s, head_width, 0) for s in head_starts])

    order_row = block_order[0]
    blocks = order_row.shape[0]
    places, begins = stream_places(order_row, lengths[0])
    tables = rotary_tables(places, begins)
    slots = jnp.sum(
        jnp.where(
            order_row[None, :] == jnp.arange(blocks, dtype=jnp.int32)[:, None],
            jnp.arange(blocks, dtype=jnp.int32)[None, :],
            0,
        ),
        axis=1,
    ).astype(jnp.int32)
    stream_starts = stream_begins(jnp.arange(tokens, dtype=jnp.int32), lengths[0]).astype(jnp.int32)
    lows = stream_starts[::CHUNK] // CHUNK
    stream_starts = stream_starts.reshape(tokens // CHUNK, 1, CHUNK)

    up_near, gate_far, w_rest_own = stage(up_near, gate_far, w_rest_own)
    up_far = gather_second(w_up_own, up_near)
    rest_near = gather_first(w_rest_own)
    normed, merged = attn_side(hidden_all, gain_full[None], bias_full[None], b_attn_own[None], attn_pieces)
    mixed, *kept = attention_forward(heads, slots, lows, merged, tables, stream_starts)
    mixed, up_far, rest_near = stage(mixed, up_far, rest_near)
    rest_far = gather_second(w_rest_own, rest_near)
    gate_pieces = gathered_pieces(w_gate_own, gate_near, gate_far, shard_rows)
    up_pieces = gathered_pieces(w_up_own, up_near, up_far, shard_rows)
    act, slope, silu = pair_side(normed, gate_pieces, up_pieces)
    if spread and shard_count == 4:
        me = lax.axis_index("fsdp")
        corner = jnp.concatenate(rest_far, axis=0)
        held = list(zip([w_rest_own, rest_near[0], rest_near[1], corner], [me, me ^ 1, me ^ 2, me ^ 3]))
        lower_pieces = [(array, 0, unit_width, at * unit_width) for array, at in held]
        proj_pieces = [(array, unit_width, head_width, at * head_width) for array, at in held]
    else:
        w_rest = rest_near[0].reshape(shard_count, -1, model)
        w_lower = jnp.pad(w_rest[:, :unit_width].reshape(units, model), ((0, spare), (0, 0)))
        if spread:
            w_proj = w_rest[:, unit_width:].reshape(width, model)
        else:
            w_proj = lax.dynamic_slice_in_dim(
                lax.all_gather(w_out, "fsdp", axis=0, tiled=True), ctx_at * width, width, 0
            )
        lower_pieces = [(w_lower, 0, units + spare, 0)]
        proj_pieces = [(w_proj, 0, width, 0)]
    out_part = out_side(mixed, act, model, lower_pieces, proj_pieces)
    out_rows = scatter_ctx(out_part)

    (grad_all,) = tie([grad_all], [out_part])
    down_part = matmul_tn(act, grad_all).astype(BF)
    proj_part = matmul_tn(mixed, grad_all).astype(BF)
    if spread:
        rest_part = jnp.concatenate(
            [p.reshape(shard_count, -1, model) for p in (down_part[:units], proj_part)], axis=1
        ).reshape(-1, model)
    else:
        rest_part = down_part[:units]
    rest_part, grad_all = stage(rest_part, grad_all)
    rest_first = scatter_first(halves(rest_part))
    grad_gate, grad_up, grad_mixed = grad_side(grad_all, slope, silu, width, lower_pieces, proj_pieces)
    grad_gate, grad_up, grad_mixed, rest_first = stage(grad_gate, grad_up, grad_mixed, rest_first)

    rest_second = scatter_second(halves(rest_part), rest_first)
    gate_part = matmul_tn(normed, grad_gate).astype(BF)
    up_part = matmul_tn(normed, grad_up).astype(BF)
    rest_sum = jnp.concatenate(scatter_last(halves(rest_part), rest_first, rest_second), axis=1)
    gate_part, up_part, rest_sum, grad_mixed = stage(gate_part, up_part, rest_sum, grad_mixed)
    rest_all = gather_ctx(rest_sum)

    pair_first = scatter_first((gate_part, up_part))
    grad_merged = attention_backward(heads, slots, lows, kept, grad_mixed, tables, stream_starts)
    grad_merged, pair_first = stage(grad_merged, pair_first)

    pair_second = scatter_second((gate_part, up_part), pair_first)
    attn_part = matmul_tn(normed, grad_merged).astype(BF)
    pair_sum = jnp.concatenate(
        [p[:, :units] for p in scatter_last((gate_part, up_part), pair_first, pair_second)], axis=1
    )
    attn_part, pair_sum, grad_merged = stage(attn_part, pair_sum, grad_merged)
    pair_all = gather_ctx(pair_sum[None])

    attn_first = scatter_first(halves(attn_part))
    grad_part, terms = input_side(
        grad_gate, grad_up, grad_merged, hidden_all, gate_pieces, up_pieces, attn_pieces
    )
    merged_term = jnp.sum(grad_merged, axis=0, dtype=F32).reshape(3, pieces, 1, head_width)
    merged_term = jnp.where(
        lax.broadcasted_iota(jnp.int32, (3, pieces, parts, head_width), 2) == ctx_at, merged_term, 0.0
    )
    terms = jnp.concatenate([terms.reshape(-1), merged_term.reshape(-1)]).reshape(-1, 128)
    grad_part, terms, attn_first = stage(grad_part, terms, attn_first)

    attn_second = scatter_second(halves(attn_part), attn_first)
    part_own, part_other = split_cores(grad_part)
    part_other = flip(part_other, "ctx", 0)
    other_terms = others_of(terms, "ctx", 1, 2)
    attn_sum = jnp.concatenate(scatter_last(halves(attn_part), attn_first, attn_second), axis=1)
    attn_sum, part_other, terms, others = stage(attn_sum, part_other, terms, other_terms[0])
    attn_all = gather_ctx(attn_sum[None])
    terms = sum_of(terms, others, other_terms[1])

    part_places = (part_own.astype(F32) + part_other.astype(F32)).astype(BF)
    pair_plan = [
        [
            (c, side * units + p * unit_width, unit_width)
            for p in range(shard_count)
            for c in range(parts)
        ]
        for side in range(2)
    ]
    attn_plan = [
        [
            (c, (s * pieces + p) * head_width, head_width)
            for s in range(3)
            for p in range(pieces)
            for c in range(parts)
        ]
    ]
    places = parts // 2
    grad_step = line_step(part_places, 1, None)
    other_terms = others_of(terms, "fsdp", 1, shard_count)
    float_in = hidden_in[0].astype(F32)
    output = (float_in + out_rows.astype(F32)).astype(BF)[None]
    terms, others, part_places, grad_step, output = stage(terms, other_terms[0], part_places, grad_step, output)
    terms = sum_of(terms, others, other_terms[1])

    if places > 2:
        grad_step = line_step(part_places, 2, grad_step)
    other_terms = others_of(terms, "ctx", 2, places)
    (rest_all,) = tie([rest_all], [output])
    rest_blocks = rest_all.reshape(parts, -1, model)
    grad_down_w = rest_blocks[:, :unit_width].reshape(-1, model).astype(F32)
    if spread:
        grad_proj_w = rest_blocks[:, unit_width:].reshape(-1, model).astype(F32)
    else:
        grad_proj_w = lax.dynamic_slice_in_dim(
            gather_ctx(lax.psum(proj_part.astype(F32), "fsdp")), fsdp_at * shard_rows, shard_rows, 0
        )
    terms, others, grad_step, grad_down_w, grad_proj_w = stage(
        terms, other_terms[0], grad_step, grad_down_w, grad_proj_w
    )
    (pair_all,) = tie([pair_all], [grad_down_w])
    terms = sum_of(terms, others, other_terms[1]).reshape(-1)

    for step in range(3, places):
        grad_step = line_step(part_places, step, grad_step)
    grad_gate_w, grad_up_w = assemble(pair_all, pair_plan)
    part_places, grad_step, grad_gate_w, grad_up_w = stage(part_places, grad_step, grad_gate_w, grad_up_w)
    grad_normed = line_block(part_places, 0) + grad_step[0].astype(F32) + grad_step[1].astype(F32)

    normal_hat, inverse_std = normalise(float_in)
    b_rows = b_qkv.shape[0]
    grad_b_attn = lax.dynamic_slice_in_dim(terms, 2 * model + fsdp_at * b_rows, b_rows, 0)
    grad_gain = lax.dynamic_slice_in_dim(terms, fsdp_at * shard_rows, shard_rows, 0)
    grad_bias = lax.dynamic_slice_in_dim(terms, model + fsdp_at * shard_rows, shard_rows, 0)

    grad_hat = grad_normed * gain_full
    grad_in = out_grad[0].astype(F32) + inverse_std * (
        grad_hat
        - jnp.mean(grad_hat, axis=1, keepdims=True)
        - normal_hat * jnp.mean(grad_hat * normal_hat, axis=1, keepdims=True)
    )
    grad_in = grad_in.astype(BF)[None]
    (attn_all,) = tie([attn_all], [grad_in])
    (grad_attn_w,) = assemble(attn_all, attn_plan)
    return (
        output,
        grad_in,
        grad_gain,
        grad_bias,
        grad_attn_w,
        grad_b_attn,
        grad_proj_w,
        grad_gate_w,
        grad_up_w,
        grad_down_w,
    )


def solution(mesh):
    return jax.shard_map(
        shards,
        mesh=mesh,
        in_specs=(
            P("fsdp", "ctx", None),
            P("fsdp", "ctx", None),
            P("fsdp", None),
            P("fsdp", None),
            P("fsdp"),
            P("fsdp"),
            P("fsdp", None),
            P("fsdp"),
            P("fsdp", None),
            P("fsdp", None),
            P("fsdp", None),
            P("fsdp", None),
        ),
        out_specs=(
            P("fsdp", "ctx", None),
            P("fsdp", "ctx", None),
            P("fsdp"),
            P("fsdp"),
            P("fsdp", None),
            P("fsdp"),
            P("fsdp", None),
            P("fsdp", None),
            P("fsdp", None),
            P("fsdp", None),
        ),
        check_vma=False,
    )
```

```python
import functools

import jax
import jax.numpy as jnp
from jax import lax
from jax.experimental import pallas as pl
from jax.experimental.pallas import tpu as pltpu
from jax.sharding import PartitionSpec as P

HD = 64
ROT = 16
BLOCK = 128
CHUNK = 256
BF = jnp.bfloat16
F32 = jnp.float32
MASKED = -1e30


def matmul(left, right):
    return jnp.dot(left, right, preferred_element_type=F32)


def matmul_nt(left, right):
    return lax.dot_general(left, right, (((1,), (1,)), ((), ())), preferred_element_type=F32)


def matmul_tn(left, right):
    return lax.dot_general(left, right, (((0,), (0,)), ((), ())), preferred_element_type=F32)


def flip(values, axis, bit):
    count = lax.axis_size(axis)
    return lax.ppermute(values, axis, [(i, i ^ (1 << bit)) for i in range(count)])


def bits_of(count):
    bits = count.bit_length() - 1
    assert count == 1 << bits
    return bits


def gather_rows(values, axis, order):
    me = lax.axis_index(axis)
    count = lax.axis_size(axis)
    held = values[None]
    steps = [0]
    for bit in order:
        other = flip(held, axis, bit)
        held = jnp.concatenate([held, other], axis=0)
        steps = steps + [s ^ (1 << bit) for s in steps]
    rows = values.shape[0]
    out = jnp.zeros((count * rows,) + values.shape[1:], values.dtype)
    for place, step in enumerate(steps):
        out = lax.dynamic_update_slice_in_dim(out, held[place], (me ^ step) * rows, 0)
    return out


def placed(pieces, places, total):
    out = jnp.zeros((total,) + pieces[0].shape[1:], pieces[0].dtype)
    for piece, place in zip(pieces, places):
        out = lax.dynamic_update_slice_in_dim(out, piece, place, 0)
    return out


def gather_first(values):
    if lax.axis_size("fsdp") != 4:
        return [gather_rows(values, "fsdp", list(range(bits_of(lax.axis_size("fsdp")))))]
    return [flip(values, "fsdp", 0), flip(values, "fsdp", 1)]


def gather_second(values, first):
    if lax.axis_size("fsdp") != 4:
        return []
    half = values.shape[0] // 2 // 16 * 16
    return [flip(first[0][:half], "fsdp", 1), flip(first[1][half:], "fsdp", 0)]


def gathered_pieces(values, first, second, rows):
    count = lax.axis_size("fsdp")
    shard = values.shape[0]
    if count != 4:
        return [(first[0], i * shard, rows, i * rows) for i in range(count)]
    me = lax.axis_index("fsdp")
    half = shard // 2 // 16 * 16
    return [
        (values, 0, rows, me * rows),
        (first[0], 0, rows, (me ^ 1) * rows),
        (first[1], 0, rows, (me ^ 2) * rows),
        (second[0], 0, half, (me ^ 3) * rows),
        (second[1], 0, rows - half, (me ^ 3) * rows + half),
    ]


def gathered_rest(values, first, second, rows):
    count = lax.axis_size("fsdp")
    shard = values.shape[0]
    if count != 4:
        return first[0].reshape(count, shard, -1)[:, rows:]
    me = lax.axis_index("fsdp")
    half = shard // 2 // 16 * 16
    tails = [values[rows:], first[0][rows:], first[1][rows:], second[1][rows - half :]]
    return placed([t[None] for t in tails], [me, me ^ 1, me ^ 2, me ^ 3], count)


def others_of(values, axis, stride, count):
    size = lax.axis_size(axis)
    digit = lax.axis_index(axis) // stride % count

    def moved(i, by):
        at = i // stride % count
        return i + ((at + by) % count - at) * stride

    return [lax.ppermute(values, axis, [(i, moved(i, by)) for i in range(size)]) for by in range(1, count)], digit


def sum_of(values, others, digit):
    count = len(others) + 1
    out = jnp.zeros((count,) + values.shape, values.dtype)
    for by, piece in enumerate([values] + others):
        out = lax.dynamic_update_slice_in_dim(out, piece[None], (digit + count - by) % count, 0)
    total = out[0]
    for at in range(1, count):
        total = total + out[at]
    return total


def scatter_rows(values, axis, order):
    me = lax.axis_index(axis)
    count = lax.axis_size(axis)
    bits = bits_of(count)
    rows = values.shape[0] // count
    held = values.reshape((2,) * bits + (rows,) + values.shape[1:])
    left = list(range(bits))
    for bit in order:
        at = len(left) - 1 - left.index(bit)
        mine = (me >> bit) & 1
        sent = lax.dynamic_index_in_dim(held, 1 - mine, at, keepdims=False).astype(BF)
        kept = lax.dynamic_index_in_dim(held, mine, at, keepdims=False)
        held = kept.astype(F32) + flip(sent, axis, bit).astype(F32)
        left.remove(bit)
    return held


def fsdp_block(part, index):
    rows = part.shape[0] // lax.axis_size("fsdp")
    return lax.dynamic_slice_in_dim(part, index * rows, rows, 0)


def halves(part):
    half = part.shape[1] // 2 // 128 * 128
    return part[:, :half], part[:, half:]


def scatter_first(sides):
    if lax.axis_size("fsdp") != 4:
        return [scatter_rows(part, "fsdp", list(range(bits_of(lax.axis_size("fsdp"))))) for part in sides]
    me = lax.axis_index("fsdp")
    return [
        flip(jnp.stack([fsdp_block(sides[1], me ^ 3), fsdp_block(sides[1], me ^ 1)]), "fsdp", 0),
        flip(jnp.stack([fsdp_block(sides[0], me ^ 3), fsdp_block(sides[0], me ^ 2)]), "fsdp", 1),
    ]


def scatter_second(sides, first):
    if lax.axis_size("fsdp") != 4:
        return []
    me = lax.axis_index("fsdp")
    across = fsdp_block(sides[0], me ^ 1).astype(F32) + first[1][0].astype(F32)
    along = fsdp_block(sides[1], me ^ 2).astype(F32) + first[0][0].astype(F32)
    return [flip(across.astype(BF), "fsdp", 0), flip(along.astype(BF), "fsdp", 1)]


def scatter_last(sides, first, second):
    if lax.axis_size("fsdp") != 4:
        return first[0].astype(BF), first[1].astype(BF)
    me = lax.axis_index("fsdp")
    left = fsdp_block(sides[0], me).astype(F32) + first[1][1].astype(F32) + second[0].astype(F32)
    right = fsdp_block(sides[1], me).astype(F32) + first[0][1].astype(F32) + second[1].astype(F32)
    return left.astype(BF), right.astype(BF)


def gather_ctx(values):
    return lax.all_gather(values, "ctx", axis=0, tiled=True)


def split_cores(part):
    parts = lax.axis_size("ctx")
    core = lax.axis_index("ctx") % 2
    blocks = part.reshape(parts // 2, 2, part.shape[0] // parts, part.shape[1])
    return [lax.dynamic_index_in_dim(blocks, k, 1, keepdims=False) for k in (core, 1 - core)]


def scatter_ctx(values):
    return lax.psum_scatter(values, "ctx", scatter_dimension=0, tiled=True)


def shift(values, by, keep):
    places = lax.axis_size("ctx") // 2
    pairs = [
        (2 * p + k, 2 * (p + by) + k) for p in range(places) for k in range(2) if keep(p) and 0 <= p + by < places
    ]
    return lax.ppermute(values, "ctx", pairs)


def line_block(blocks, s):
    places = blocks.shape[0]
    at = (lax.axis_index("ctx") // 2 + places - s) % places
    return lax.dynamic_index_in_dim(blocks, at, 0, keepdims=False).astype(F32)


def line_start(ends):
    last = lax.axis_size("ctx") // 2 - 1
    return [shift(ends[0], 1, lambda p: p <= 0), shift(ends[1], -1, lambda p: p >= last)]


def line_step(blocks, step, before):
    places = blocks.shape[0]
    up, down = line_block(blocks, step), line_block(blocks, places - step)
    if before:
        up, down = up + before[0].astype(F32), down + before[1].astype(F32)
    return [
        shift(up.astype(BF), 1, lambda p: p <= step - 1),
        shift(down.astype(BF), -1, lambda p: p >= places - step),
    ]


def gather_step(step, before):
    places = lax.axis_size("ctx") // 2
    return [
        shift(before[0], 1, lambda p: p >= step - 1),
        shift(before[1], -1, lambda p: p <= places - step),
    ]


def line_origins():
    me = lax.axis_index("ctx")
    places = lax.axis_size("ctx") // 2
    at, core = me // 2, me % 2
    out = [me, me ^ 1]
    for s in range(1, places):
        ends = (jnp.where(at >= s, at - s, -1), jnp.where(at + s < places, at + s, -1))
        for j in range(2):
            out += [jnp.where(p < 0, -1, 2 * p + (core ^ j)) for p in ends]
    return jnp.stack(out).astype(jnp.int32)


def nothing_kernel(*refs):
    return None


def tie(values, after):
    anywhere = pl.BlockSpec(memory_space=pl.ANY)
    return pl.pallas_call(
        nothing_kernel,
        out_shape=tuple(jax.ShapeDtypeStruct(v.shape, v.dtype) for v in values),
        in_specs=[anywhere] * (len(values) + len(after)),
        out_specs=tuple([anywhere] * len(values)),
        input_output_aliases={i: i for i in range(len(values))},
        name="tie",
    )(*values, *after)


def stage(*groups):
    leaves, tree = jax.tree.flatten(groups)
    return jax.tree.unflatten(tree, tie(leaves, []))


def rows_at(index, size):
    return pl.ds(pl.multiple_of(index * size, size), size)


def turn(values, tables, rows, direction):
    width = values.shape[1]
    cosine, lead, tail = (jnp.concatenate([ref[rows, :]] * (width // 128), axis=1) for ref in tables)
    ahead = pltpu.roll(values, width - ROT // 2, 1)
    behind = pltpu.roll(values, ROT // 2, 1)
    return values * cosine + direction * (ahead * lead + behind * tail)


def split_heads(target, values, heads):
    head_of = lax.broadcasted_iota(jnp.int32, values.shape, 1) // HD
    for h in range(heads):
        target[h * CHUNK : (h + 1) * CHUNK, :] = jnp.where(head_of == h, values, jnp.zeros_like(values))


def visible(i, j, begin):
    key_at = lax.broadcasted_iota(jnp.int32, (CHUNK, CHUNK), 0)
    query_at = lax.broadcasted_iota(jnp.int32, (CHUNK, CHUNK), 1)
    return (key_at - query_at <= (i - j) * CHUNK) & (key_at >= begin - j * CHUNK)


def forward_kernel(
    heads,
    slot_ref,
    low_ref,
    merged_ref,
    cos_ref,
    lead_ref,
    tail_ref,
    begin_ref,
    mixed_ref,
    q_ref,
    k_ref,
    v_ref,
    total_ref,
    ot_ref,
    vt_ref,
    qm_ref,
    s_ref,
):
    width = heads * HD
    tokens = merged_ref.shape[0]
    tables = (cos_ref, lead_ref, tail_ref)

    def prepare(block, carry):
        source = rows_at(slot_ref[block], BLOCK)
        target = rows_at(block, BLOCK)
        query = turn(merged_ref[source, 0:width], tables, source, 1.0).astype(BF)
        key = turn(merged_ref[source, width : 2 * width], tables, source, 1.0).astype(BF)
        value = merged_ref[source, 2 * width : 3 * width].astype(BF)
        q_ref[target, :] = query * jnp.asarray(HD ** (-0.5), BF)
        k_ref[target, :] = key
        v_ref[target, :] = value
        vt_ref[:, target] = value.T
        return carry

    lax.fori_loop(0, tokens // BLOCK, prepare, 0)

    def query_chunk(i, carry):
        here = rows_at(i, CHUNK)
        split_heads(qm_ref, q_ref[here, :], heads)
        ot_ref[:, here] = jnp.zeros((width, CHUNK), F32)
        low = low_ref[i]
        begin = begin_ref[i]

        def score(j, tops):
            there = rows_at(j, CHUNK)
            key = k_ref[there, :]
            allowed = visible(i, j, begin)
            out = []
            for h in range(heads):
                s = matmul_nt(key, qm_ref[h * CHUNK : (h + 1) * CHUNK, :])
                s = jnp.where(allowed, s, MASKED)
                s_ref[h, there, :] = s
                out.append(jnp.maximum(tops[h], jnp.max(s, axis=0, keepdims=True)))
            return tuple(out)

        tops = lax.fori_loop(
            low, i + 1, score, tuple(jnp.full((1, CHUNK), MASKED, F32) for _ in range(heads))
        )

        def value_side(j, sums):
            there = rows_at(j, CHUNK)
            out = []
            for h in range(heads):
                span = slice(h * HD, (h + 1) * HD)
                e = jnp.exp(s_ref[h, there, :] - tops[h])
                out.append(sums[h] + jnp.sum(e, axis=0, keepdims=True))
                ot_ref[span, here] += matmul(vt_ref[span, there], e.astype(BF))
            return tuple(out)

        sums = lax.fori_loop(low, i + 1, value_side, tuple(jnp.zeros((1, CHUNK), F32) for _ in range(heads)))
        for h in range(heads):
            span = slice(h * HD, (h + 1) * HD)
            ot_ref[span, here] = ot_ref[span, here] * (1.0 / sums[h])
            total_ref[i, h : h + 1, :] = tops[h] + jnp.log(sums[h])
        mixed = ot_ref[:, here].T.astype(BF)
        for part in range(CHUNK // BLOCK):
            target = rows_at(slot_ref[i * (CHUNK // BLOCK) + part], BLOCK)
            mixed_ref[target, :] = mixed[part * BLOCK : (part + 1) * BLOCK]
        return carry

    lax.fori_loop(0, tokens // CHUNK, query_chunk, 0)


def backward_kernel(
    heads,
    slot_ref,
    low_ref,
    q_ref,
    k_ref,
    v_ref,
    total_ref,
    ot_ref,
    grad_mixed_ref,
    cos_ref,
    lead_ref,
    tail_ref,
    begin_ref,
    grad_merged_ref,
    kt_ref,
    qm_ref,
    gm_ref,
    p_ref,
    ds_ref,
    dqt_ref,
    dk_ref,
    dv_ref,
):
    width = heads * HD
    tokens = q_ref.shape[0]
    tables = (cos_ref, lead_ref, tail_ref)

    def prepare(block, carry):
        here = rows_at(block, BLOCK)
        kt_ref[:, here] = k_ref[here, :].T
        dk_ref[here, :] = jnp.zeros((BLOCK, width), F32)
        dv_ref[here, :] = jnp.zeros((BLOCK, width), F32)
        return carry

    lax.fori_loop(0, tokens // BLOCK, prepare, 0)

    def query_chunk(i, carry):
        here = rows_at(i, CHUNK)
        targets = [rows_at(slot_ref[i * (CHUNK // BLOCK) + part], BLOCK) for part in range(CHUNK // BLOCK)]
        grad = jnp.concatenate([grad_mixed_ref[target, :] for target in targets], axis=0)
        split_heads(qm_ref, q_ref[here, :], heads)
        split_heads(gm_ref, grad, heads)
        dqt_ref[...] = jnp.zeros_like(dqt_ref)
        product = grad.T.astype(F32) * ot_ref[:, here]
        dots = [jnp.sum(product[h * HD : (h + 1) * HD], axis=0, keepdims=True) for h in range(heads)]
        totals = [total_ref[i, h : h + 1, :] for h in range(heads)]
        begin = begin_ref[i]

        def key_chunk(j, carry):
            there = rows_at(j, CHUNK)
            key = k_ref[there, :]
            value = v_ref[there, :]
            allowed = visible(i, j, begin)
            for h in range(heads):
                span = slice(h * HD, (h + 1) * HD)
                part = slice(h * CHUNK, (h + 1) * CHUNK)
                s = matmul_nt(key, qm_ref[part, :])
                probs = jnp.exp(jnp.where(allowed, s, MASKED) - totals[h])
                p_ref[:, part] = probs.astype(BF)
                ds = (probs * (matmul_nt(value, gm_ref[part, :]) - dots[h])).astype(BF)
                ds_ref[:, part] = ds
                dqt_ref[span, :] += matmul(kt_ref[span, there], ds)
            dv_ref[there, :] += matmul(p_ref[...], gm_ref[...])
            dk_ref[there, :] += matmul(ds_ref[...], qm_ref[...])
            return carry

        lax.fori_loop(low_ref[i], i + 1, key_chunk, 0)
        grad_query = dqt_ref[...].T * HD ** (-0.5)
        for part, target in enumerate(targets):
            rows = slice(part * BLOCK, (part + 1) * BLOCK)
            grad_merged_ref[target, 0:width] = turn(grad_query[rows], tables, target, -1.0).astype(BF)
        return carry

    lax.fori_loop(0, tokens // CHUNK, query_chunk, 0)

    def finish(block, carry):
        source = rows_at(block, BLOCK)
        target = rows_at(slot_ref[block], BLOCK)
        grad_merged_ref[target, width : 2 * width] = turn(dk_ref[source, :], tables, target, -1.0).astype(BF)
        grad_merged_ref[target, 2 * width : 3 * width] = dv_ref[source, :].astype(BF)
        return carry

    lax.fori_loop(0, tokens // BLOCK, finish, 0)


WHOLE = pl.BlockSpec(memory_space=pltpu.VMEM)
SCALAR = pl.BlockSpec(memory_space=pltpu.SMEM)
ANYWHERE = pl.BlockSpec(memory_space=pl.ANY)


def attention_forward(heads, slots, lows, merged, tables, begins):
    tokens = merged.shape[0]
    width = heads * HD
    rows = jax.ShapeDtypeStruct((tokens, width), BF)
    return pl.pallas_call(
        functools.partial(forward_kernel, heads),
        out_shape=(
            rows,
            rows,
            rows,
            rows,
            jax.ShapeDtypeStruct((tokens // CHUNK, heads, CHUNK), F32),
            jax.ShapeDtypeStruct((width, tokens), F32),
        ),
        in_specs=[SCALAR, SCALAR] + [WHOLE] * 5,
        out_specs=(WHOLE,) * 6,
        scratch_shapes=[
            pltpu.VMEM((width, tokens), BF),
            pltpu.VMEM((heads * CHUNK, width), BF),
            pltpu.VMEM((heads, tokens, CHUNK), F32),
        ],
        compiler_params=pltpu.CompilerParams(vmem_limit_bytes=48 * 1024 * 1024),
        cost_estimate=pl.CostEstimate(flops=25_000_000_000, transcendentals=0, bytes_accessed=0),
        name="attention_forward",
    )(slots, lows, merged, *tables, begins)


def attention_backward(heads, slots, lows, kept, grad_mixed, tables, begins):
    tokens, width = grad_mixed.shape
    return pl.pallas_call(
        functools.partial(backward_kernel, heads),
        out_shape=jax.ShapeDtypeStruct((tokens, 3 * width), BF),
        in_specs=[SCALAR, SCALAR] + [WHOLE] * 10,
        out_specs=WHOLE,
        scratch_shapes=[
            pltpu.VMEM((width, tokens), BF),
            pltpu.VMEM((heads * CHUNK, width), BF),
            pltpu.VMEM((heads * CHUNK, width), BF),
            pltpu.VMEM((CHUNK, heads * CHUNK), BF),
            pltpu.VMEM((CHUNK, heads * CHUNK), BF),
            pltpu.VMEM((width, CHUNK), F32),
            pltpu.VMEM((tokens, width), F32),
            pltpu.VMEM((tokens, width), F32),
        ],
        compiler_params=pltpu.CompilerParams(vmem_limit_bytes=48 * 1024 * 1024),
        cost_estimate=pl.CostEstimate(flops=40_000_000_000, transcendentals=0, bytes_accessed=0),
        name="attention_backward",
    )(slots, lows, *kept, grad_mixed, *tables, begins)


def fetch(at_ref, pieces, spans, target, sem):
    copies = []
    for n, (piece, (first, rows)) in enumerate(zip(pieces, spans)):
        place = pl.ds(pl.multiple_of(at_ref[n], 16), rows)
        copies.append(pltpu.make_async_copy(piece.at[pl.ds(first, rows), :], target.at[place, :], sem.at[n]))
    for copy in copies:
        copy.start()
    return copies


def attn_kernel(spans, at_ref, hidden_ref, gain_ref, bias_ref, shift_ref, *refs):
    n = len(spans)
    normed_ref, merged_ref, w_attn, sem = refs[n:]

    @pl.when(pl.program_id(0) == 0)
    def _():
        for copy in fetch(at_ref, refs[:n], spans, w_attn, sem):
            copy.wait()

    normal, _ = normalise(hidden_ref[...].astype(F32))
    normed = (normal * gain_ref[...] + bias_ref[...]).astype(BF)
    normed_ref[...] = normed
    merged_ref[...] = matmul(normed, w_attn[...]) + shift_ref[...]


def pair_kernel(spans, at_ref, normed_ref, *refs):
    n = len(spans)
    gate_pieces, up_pieces = refs[:n], refs[n : 2 * n]
    act_ref, slope_ref, silu_ref, w_gate, w_up, *sems = refs[2 * n :]

    @pl.when(pl.program_id(0) == 0)
    def _():
        copies = fetch(at_ref, gate_pieces, spans, w_gate, sems[0])
        copies += fetch(at_ref, up_pieces, spans, w_up, sems[1])
        for copy in copies:
            copy.wait()

    normed = normed_ref[...]
    gating = matmul(normed, w_gate[...])
    rising = matmul(normed, w_up[...])
    sigma = jax.nn.sigmoid(gating)
    silu = gating * sigma
    act_ref[...] = (silu * rising).astype(BF)
    slope_ref[...] = (rising * sigma * (1.0 + gating * (1.0 - sigma))).astype(BF)
    silu_ref[...] = silu.astype(BF)


def row_block(width):
    return pl.BlockSpec((CHUNK, width), lambda i: (i, 0))


def full_block(array):
    return pl.BlockSpec(array.shape, lambda i: (0, 0))


def split_pieces(pieces):
    at = jnp.stack([jnp.asarray(piece[3], jnp.int32) for piece in pieces])
    return at, [piece[0] for piece in pieces], tuple((piece[1], piece[2]) for piece in pieces)


def attn_side(hidden, gain, bias, shift, pieces):
    tokens, model = hidden.shape
    at, arrays, spans = split_pieces(pieces)
    n = len(spans)
    width = arrays[0].shape[1]
    return pl.pallas_call(
        functools.partial(attn_kernel, spans),
        grid=(tokens // CHUNK,),
        out_shape=(jax.ShapeDtypeStruct((tokens, model), BF), jax.ShapeDtypeStruct((tokens, width), F32)),
        in_specs=[SCALAR, row_block(model), full_block(gain), full_block(bias), full_block(shift)] + [ANYWHERE] * n,
        out_specs=(row_block(model), row_block(width)),
        scratch_shapes=[pltpu.VMEM((model, width), BF), pltpu.SemaphoreType.DMA((n,))],
        compiler_params=pltpu.CompilerParams(vmem_limit_bytes=56 * 1024 * 1024),
        cost_estimate=pl.CostEstimate(flops=18_000_000_000, transcendentals=0, bytes_accessed=0),
        name="attn_side",
    )(at, hidden, gain, bias, shift, *arrays)


def pair_side(normed, gate_pieces, up_pieces):
    tokens, model = normed.shape
    at, gates, spans = split_pieces(gate_pieces)
    ups = split_pieces(up_pieces)[1]
    n = len(spans)
    units = gates[0].shape[1]
    return pl.pallas_call(
        functools.partial(pair_kernel, spans),
        grid=(tokens // CHUNK,),
        out_shape=(jax.ShapeDtypeStruct((tokens, units), BF),) * 3,
        in_specs=[SCALAR, row_block(model)] + [ANYWHERE] * (2 * n),
        out_specs=(row_block(units),) * 3,
        scratch_shapes=[
            pltpu.VMEM((model, units), BF),
            pltpu.VMEM((model, units), BF),
            pltpu.SemaphoreType.DMA((n,)),
            pltpu.SemaphoreType.DMA((n,)),
        ],
        compiler_params=pltpu.CompilerParams(vmem_limit_bytes=56 * 1024 * 1024),
        cost_estimate=pl.CostEstimate(flops=28_000_000_000, transcendentals=0, bytes_accessed=0),
        name="pair_side",
    )(at, normed, *gates, *ups)


def fetch_rest(spans, at_ref, refs, lower, proj, sems):
    n = len(spans) // 2
    units = lower.shape[0]
    filled = sum(rows for _, rows in spans[:n])
    if filled < units:
        lower[filled:, :] = jnp.zeros((units - filled, lower.shape[1]), BF)
    copies = fetch(at_ref.at[0], refs[:n], spans[:n], lower, sems[0])
    copies += fetch(at_ref.at[1], refs[n:], spans[n:], proj, sems[1])
    for copy in copies:
        copy.wait()


def grad_kernel(spans, at_ref, grad_ref, slope_ref, silu_ref, *refs):
    n = len(spans)
    gate_ref, up_ref, mixed_ref, lower, proj, *sems = refs[n:]

    @pl.when(pl.program_id(0) == 0)
    def _():
        fetch_rest(spans, at_ref, refs[:n], lower, proj, sems)

    grad = grad_ref[...]
    act = matmul_nt(grad, lower[...])
    mixed_ref[...] = matmul_nt(grad, proj[...]).astype(BF)
    gate_ref[...] = (act * slope_ref[...].astype(F32)).astype(BF)
    up_ref[...] = (act * silu_ref[...].astype(F32)).astype(BF)


def rest_scratch(units, width, model, n):
    return [
        pltpu.VMEM((units, model), BF),
        pltpu.VMEM((width, model), BF),
        pltpu.SemaphoreType.DMA((n,)),
        pltpu.SemaphoreType.DMA((n,)),
    ]


def split_rest(lower_pieces, proj_pieces):
    lower_at, lowers, lower_spans = split_pieces(lower_pieces)
    proj_at, projs, proj_spans = split_pieces(proj_pieces)
    return jnp.stack([lower_at, proj_at]), lowers + projs, lower_spans + proj_spans


def grad_side(grad, slope, silu, width, lower_pieces, proj_pieces):
    tokens, model = grad.shape
    units = slope.shape[1]
    at, arrays, spans = split_rest(lower_pieces, proj_pieces)
    return pl.pallas_call(
        functools.partial(grad_kernel, spans),
        grid=(tokens // CHUNK,),
        out_shape=(
            jax.ShapeDtypeStruct((tokens, units), BF),
            jax.ShapeDtypeStruct((tokens, units), BF),
            jax.ShapeDtypeStruct((tokens, width), BF),
        ),
        in_specs=[SCALAR, row_block(model), row_block(units), row_block(units)] + [ANYWHERE] * len(arrays),
        out_specs=(row_block(units), row_block(units), row_block(width)),
        scratch_shapes=rest_scratch(units, width, model, len(arrays) // 2),
        compiler_params=pltpu.CompilerParams(vmem_limit_bytes=56 * 1024 * 1024),
        cost_estimate=pl.CostEstimate(flops=18_000_000_000, transcendentals=0, bytes_accessed=0),
        name="grad_side",
    )(at, grad, slope, silu, *arrays)


def out_kernel(spans, at_ref, mixed_ref, act_ref, *refs):
    n = len(spans)
    out_ref, lower, proj, *sems = refs[n:]

    @pl.when(pl.program_id(0) == 0)
    def _():
        fetch_rest(spans, at_ref, refs[:n], lower, proj, sems)

    out_ref[...] = (matmul(mixed_ref[...], proj[...]) + matmul(act_ref[...], lower[...])).astype(BF)


def out_side(mixed, act, model, lower_pieces, proj_pieces):
    tokens, width = mixed.shape
    units = act.shape[1]
    at, arrays, spans = split_rest(lower_pieces, proj_pieces)
    return pl.pallas_call(
        functools.partial(out_kernel, spans),
        grid=(tokens // CHUNK,),
        out_shape=jax.ShapeDtypeStruct((tokens, model), BF),
        in_specs=[SCALAR, row_block(width), row_block(units)] + [ANYWHERE] * len(arrays),
        out_specs=row_block(model),
        scratch_shapes=rest_scratch(units, width, model, len(arrays) // 2),
        compiler_params=pltpu.CompilerParams(vmem_limit_bytes=56 * 1024 * 1024),
        cost_estimate=pl.CostEstimate(flops=15_000_000_000, transcendentals=0, bytes_accessed=0),
        name="out_side",
    )(at, mixed, act, *arrays)


def input_kernel(spans, at_ref, gate_ref, up_ref, merged_ref, hidden_ref, *refs):
    n = len(spans)
    gate_pieces, up_pieces, attn_pieces = refs[:n], refs[n : 2 * n], refs[2 * n : 3 * n]
    part_ref, terms_ref, w_gate, w_up, w_attn, *sems = refs[3 * n :]

    @pl.when(pl.program_id(0) == 0)
    def _():
        copies = fetch(at_ref, gate_pieces, spans, w_gate, sems[0])
        copies += fetch(at_ref, up_pieces, spans, w_up, sems[1])
        copies += fetch(at_ref, attn_pieces, spans, w_attn, sems[2])
        terms_ref[...] = jnp.zeros_like(terms_ref)
        for copy in copies:
            copy.wait()

    part = matmul_nt(gate_ref[...], w_gate[...]) + matmul_nt(up_ref[...], w_up[...])
    part = part + matmul_nt(merged_ref[...], w_attn[...])
    part_ref[...] = part.astype(BF)
    normal, _ = normalise(hidden_ref[...].astype(F32))
    terms_ref[0:1, :] += jnp.sum(part * normal, axis=0, keepdims=True)
    terms_ref[1:2, :] += jnp.sum(part, axis=0, keepdims=True)


def input_side(grad_gate, grad_up, grad_merged, hidden, gate_pieces, up_pieces, attn_pieces):
    tokens, model = hidden.shape
    at, gates, spans = split_pieces(gate_pieces)
    ups, attns = split_pieces(up_pieces)[1], split_pieces(attn_pieces)[1]
    n = len(spans)
    units, width = grad_gate.shape[1], grad_merged.shape[1]
    return pl.pallas_call(
        functools.partial(input_kernel, spans),
        grid=(tokens // CHUNK,),
        out_shape=(jax.ShapeDtypeStruct((tokens, model), BF), jax.ShapeDtypeStruct((2, model), F32)),
        in_specs=[SCALAR, row_block(units), row_block(units), row_block(width), row_block(model)]
        + [ANYWHERE] * (3 * n),
        out_specs=(row_block(model), pl.BlockSpec((2, model), lambda i: (0, 0))),
        scratch_shapes=[
            pltpu.VMEM((model, units), BF),
            pltpu.VMEM((model, units), BF),
            pltpu.VMEM((model, width), BF),
            pltpu.SemaphoreType.DMA((n,)),
            pltpu.SemaphoreType.DMA((n,)),
            pltpu.SemaphoreType.DMA((n,)),
        ],
        compiler_params=pltpu.CompilerParams(vmem_limit_bytes=56 * 1024 * 1024),
        cost_estimate=pl.CostEstimate(flops=30_000_000_000, transcendentals=0, bytes_accessed=0),
        name="input_side",
    )(at, grad_gate, grad_up, grad_merged, hidden, *gates, *ups, *attns)


def assemble_kernel(plan, source_ref, *targets):
    for target, pieces in zip(targets, plan):
        at = 0
        for part, offset, width in pieces:
            target[:, at : at + width] = source_ref[part, :, offset : offset + width].astype(F32)
            at += width


def assemble(gathered, plan):
    parts, rows, columns = gathered.shape
    step = 64
    widths = [sum(piece[2] for piece in pieces) for pieces in plan]
    return pl.pallas_call(
        functools.partial(assemble_kernel, plan),
        grid=(rows // step,),
        out_shape=tuple(jax.ShapeDtypeStruct((rows, w), F32) for w in widths),
        in_specs=[pl.BlockSpec((parts, step, columns), lambda i: (0, i, 0))],
        out_specs=tuple(pl.BlockSpec((step, w), lambda i: (i, 0)) for w in widths),
        compiler_params=pltpu.CompilerParams(vmem_limit_bytes=40 * 1024 * 1024),
        name="assemble",
    )(gathered)


def assemble_line_kernel(plan, count, at_ref, *refs):
    target, held = refs[count], refs[count + 1]
    for n in range(count):

        @pl.when(at_ref[n] >= 0)
        def _():
            held[jnp.maximum(at_ref[n], 0)] = refs[n][0]

    at = 0
    for part, offset, width in plan:
        target[:, at : at + width] = held[part, :, offset : offset + width].astype(F32)
        at += width


def assemble_line(sources, origins, plan):
    parts = lax.axis_size("ctx")
    rows, columns = sources[0][0].shape[1:]
    step = 64
    width = sum(piece[2] for piece in plan)

    def block(n, index):
        return pl.BlockSpec((1, step, columns), lambda i, at: (index, jnp.where(at[n] >= 0, i, 0), 0))

    return pl.pallas_call(
        functools.partial(assemble_line_kernel, plan, len(sources)),
        out_shape=jax.ShapeDtypeStruct((rows, width), F32),
        grid_spec=pltpu.PrefetchScalarGridSpec(
            num_scalar_prefetch=1,
            grid=(rows // step,),
            in_specs=[block(n, index) for n, (_, index) in enumerate(sources)],
            out_specs=pl.BlockSpec((step, width), lambda i, at: (i, 0)),
            scratch_shapes=[pltpu.VMEM((parts, step, columns), BF)],
        ),
        compiler_params=pltpu.CompilerParams(vmem_limit_bytes=40 * 1024 * 1024),
        name="assemble_line",
    )(origins, *[array for array, _ in sources])


def stream_places(order_row, length_row):
    places = (order_row[:, None] * BLOCK + jnp.arange(BLOCK, dtype=jnp.int32)[None, :]).reshape(-1)
    return places, stream_begins(places, length_row)


def stream_begins(places, length_row):
    ends = jnp.cumsum(length_row)
    starts = ends - length_row
    return jnp.max(jnp.where(starts[None, :] <= places[:, None], starts[None, :], 0), axis=1)


def rotary_tables(places, begins):
    entry = jnp.arange(128) % HD
    turned = entry < ROT
    index = jnp.where(entry < ROT // 2, entry, entry - ROT // 2)
    inverse = 1.0 / 10000.0 ** ((2 * index).astype(F32) / ROT)
    angles = (places - begins).astype(F32)[:, None] * jnp.where(turned, inverse, 0.0)[None, :]
    cosine, sine = jnp.cos(angles), jnp.sin(angles)
    lead = jnp.where((entry < ROT // 2)[None, :], -sine, 0.0)
    tail = jnp.where((turned & (entry >= ROT // 2))[None, :], sine, 0.0)
    return cosine, lead, tail


def take_columns(array, starts, width):
    return [lax.dynamic_slice_in_dim(array, s, width, 1) for s in starts]


def normalise(rows):
    centre = jnp.mean(rows, axis=1, keepdims=True)
    deviation = rows - centre
    inverse_std = lax.rsqrt(jnp.mean(deviation * deviation, axis=1, keepdims=True) + 1e-05)
    return deviation * inverse_std, inverse_std


def shards(
    hidden_in,
    out_grad,
    lengths,
    block_order,
    ln_gain,
    ln_bias,
    w_qkv,
    b_qkv,
    w_out,
    w_gate,
    w_up,
    w_down,
):
    parts = lax.axis_size("ctx")
    shard_count = lax.axis_size("fsdp")
    ctx_at = lax.axis_index("ctx")
    fsdp_at = lax.axis_index("fsdp")
    rows = hidden_in.shape[1]
    model = w_out.shape[1]
    hidden = w_gate.shape[1]
    tokens = rows * parts
    heads = model // HD // parts
    width = heads * HD
    shard_rows = w_qkv.shape[0]

    hidden_all = gather_ctx(hidden_in[0])
    grad_all = gather_ctx(out_grad[0])

    spread = (model // HD) % (shard_count * parts) == 0
    pieces = shard_count if spread else 1
    head_span = model // pieces
    head_width = head_span // parts
    head_starts = [
        s * model + p * head_span + ctx_at * head_width for s in range(3) for p in range(pieces)
    ]
    unit_span = hidden // shard_count
    unit_width = unit_span // parts
    unit_starts = [p * unit_span + ctx_at * unit_width for p in range(shard_count)]

    units = shard_count * unit_width
    spare = -units % 128
    empty = jnp.zeros((shard_rows, spare), BF)
    vectors = jnp.concatenate([ln_gain, ln_bias, b_qkv])
    vector_rows = -(-vectors.shape[0] // (3 * width)) + 15
    vector_rows = vector_rows // 16 * 16
    vectors = jnp.pad(vectors, (0, vector_rows * 3 * width - vectors.shape[0])).reshape(vector_rows, 3 * width)
    w_attn_own = jnp.concatenate(take_columns(w_qkv, head_starts, head_width), axis=1)
    w_attn_own = jnp.concatenate([w_attn_own, vectors], axis=0)
    attn_near = gather_first(w_attn_own)
    w_gate_own = jnp.concatenate(take_columns(w_gate, unit_starts, unit_width) + [empty], axis=1)
    gate_near = gather_first(w_gate_own)
    w_up_own = jnp.concatenate(take_columns(w_up, unit_starts, unit_width) + [empty], axis=1)
    attn_near, w_up_own = stage(attn_near, w_up_own)
    attn_far = gather_second(w_attn_own, attn_near)
    up_near = gather_first(w_up_own)
    gate_near, attn_far = stage(gate_near, attn_far)
    gate_far = gather_second(w_gate_own, gate_near)
    w_down_own = lax.dynamic_slice_in_dim(w_down, ctx_at * unit_width, unit_width, 0)
    if spread:
        w_out_own = lax.dynamic_slice_in_dim(w_out, ctx_at * head_width, head_width, 0)
        w_rest_own = jnp.concatenate([w_down_own, w_out_own], axis=0)
    else:
        w_rest_own = w_down_own
    attn_pieces = gathered_pieces(w_attn_own, attn_near, attn_far, shard_rows)
    vectors = gathered_rest(w_attn_own, attn_near, attn_far, shard_rows).reshape(shard_count, -1)
    gain_full = vectors[:, :shard_rows].reshape(-1).astype(F32)
    bias_full = vectors[:, shard_rows : 2 * shard_rows].reshape(-1).astype(F32)
    b_attn = vectors[:, 2 * shard_rows : 2 * shard_rows + b_qkv.shape[0]].reshape(-1).astype(F32)
    b_attn_own = jnp.concatenate([lax.dynamic_slice_in_dim(b_attn, s, head_width, 0) for s in head_starts])

    order_row = block_order[0]
    blocks = order_row.shape[0]
    places, begins = stream_places(order_row, lengths[0])
    tables = rotary_tables(places, begins)
    slots = jnp.sum(
        jnp.where(
            order_row[None, :] == jnp.arange(blocks, dtype=jnp.int32)[:, None],
            jnp.arange(blocks, dtype=jnp.int32)[None, :],
            0,
        ),
        axis=1,
    ).astype(jnp.int32)
    stream_starts = stream_begins(jnp.arange(tokens, dtype=jnp.int32), lengths[0]).astype(jnp.int32)
    lows = stream_starts[::CHUNK] // CHUNK
    stream_starts = stream_starts.reshape(tokens // CHUNK, 1, CHUNK)

    up_near, gate_far, w_rest_own = stage(up_near, gate_far, w_rest_own)
    up_far = gather_second(w_up_own, up_near)
    rest_near = gather_first(w_rest_own)
    normed, merged = attn_side(hidden_all, gain_full[None], bias_full[None], b_attn_own[None], attn_pieces)
    mixed, *kept = attention_forward(heads, slots, lows, merged, tables, stream_starts)
    mixed, up_far, rest_near = stage(mixed, up_far, rest_near)
    rest_far = gather_second(w_rest_own, rest_near)
    gate_pieces = gathered_pieces(w_gate_own, gate_near, gate_far, shard_rows)
    up_pieces = gathered_pieces(w_up_own, up_near, up_far, shard_rows)
    act, slope, silu = pair_side(normed, gate_pieces, up_pieces)
    if spread and shard_count == 4:
        me = lax.axis_index("fsdp")
        corner = jnp.concatenate(rest_far, axis=0)
        held = list(zip([w_rest_own, rest_near[0], rest_near[1], corner], [me, me ^ 1, me ^ 2, me ^ 3]))
        lower_pieces = [(array, 0, unit_width, at * unit_width) for array, at in held]
        proj_pieces = [(array, unit_width, head_width, at * head_width) for array, at in held]
    else:
        w_rest = rest_near[0].reshape(shard_count, -1, model)
        w_lower = jnp.pad(w_rest[:, :unit_width].reshape(units, model), ((0, spare), (0, 0)))
        if spread:
            w_proj = w_rest[:, unit_width:].reshape(width, model)
        else:
            w_proj = lax.dynamic_slice_in_dim(
                lax.all_gather(w_out, "fsdp", axis=0, tiled=True), ctx_at * width, width, 0
            )
        lower_pieces = [(w_lower, 0, units + spare, 0)]
        proj_pieces = [(w_proj, 0, width, 0)]
    out_part = out_side(mixed, act, model, lower_pieces, proj_pieces)
    out_rows = scatter_ctx(out_part)

    (grad_all,) = tie([grad_all], [out_part])
    down_part = matmul_tn(act, grad_all).astype(BF)
    proj_part = matmul_tn(mixed, grad_all).astype(BF)
    if spread:
        rest_part = jnp.concatenate(
            [p.reshape(shard_count, -1, model) for p in (down_part[:units], proj_part)], axis=1
        ).reshape(-1, model)
    else:
        rest_part = down_part[:units]
    rest_part, grad_all = stage(rest_part, grad_all)
    rest_first = scatter_first(halves(rest_part))
    grad_gate, grad_up, grad_mixed = grad_side(grad_all, slope, silu, width, lower_pieces, proj_pieces)
    grad_gate, grad_up, grad_mixed, rest_first = stage(grad_gate, grad_up, grad_mixed, rest_first)

    rest_second = scatter_second(halves(rest_part), rest_first)
    gate_part = matmul_tn(normed, grad_gate).astype(BF)
    up_part = matmul_tn(normed, grad_up).astype(BF)
    rest_sum = jnp.concatenate(scatter_last(halves(rest_part), rest_first, rest_second), axis=1)
    gate_part, up_part, rest_sum, grad_mixed = stage(gate_part, up_part, rest_sum, grad_mixed)
    rest_all = gather_ctx(rest_sum)

    pair_first = scatter_first((gate_part, up_part))
    grad_merged = attention_backward(heads, slots, lows, kept, grad_mixed, tables, stream_starts)
    grad_merged, pair_first = stage(grad_merged, pair_first)

    pair_second = scatter_second((gate_part, up_part), pair_first)
    attn_part = matmul_tn(normed, grad_merged).astype(BF)
    pair_sum = jnp.concatenate(
        [p[:, :units] for p in scatter_last((gate_part, up_part), pair_first, pair_second)], axis=1
    )
    attn_part, pair_sum, grad_merged = stage(attn_part, pair_sum, grad_merged)
    pair_all = gather_ctx(pair_sum[None])

    attn_first = scatter_first(halves(attn_part))
    grad_part, terms = input_side(
        grad_gate, grad_up, grad_merged, hidden_all, gate_pieces, up_pieces, attn_pieces
    )
    merged_term = jnp.sum(grad_merged, axis=0, dtype=F32).reshape(3, pieces, 1, head_width)
    merged_term = jnp.where(
        lax.broadcasted_iota(jnp.int32, (3, pieces, parts, head_width), 2) == ctx_at, merged_term, 0.0
    )
    terms = jnp.concatenate([terms.reshape(-1), merged_term.reshape(-1)]).reshape(-1, 128)
    grad_part, terms, attn_first = stage(grad_part, terms, attn_first)

    attn_second = scatter_second(halves(attn_part), attn_first)
    attn_sum = jnp.concatenate(scatter_last(halves(attn_part), attn_first, attn_second), axis=1)
    attn_sum, grad_part, terms = stage(attn_sum, grad_part, terms)

    pair_plan = [
        [
            (c, side * units + p * unit_width, unit_width)
            for p in range(shard_count)
            for c in range(parts)
        ]
        for side in range(2)
    ]
    attn_plan = [
        [
            (c, (s * pieces + p) * head_width, head_width)
            for s in range(3)
            for p in range(pieces)
            for c in range(parts)
        ]
    ]
    places = parts // 2
    attn_got = gather_step(1, [attn_sum, attn_sum])
    attn_held, attn_other = [attn_sum[None]], []
    other_terms = others_of(terms, "fsdp", 1, shard_count)
    part_own, part_other = split_cores(grad_part)
    part_other = flip(part_other, "ctx", 0)
    part_places = (part_own.astype(F32) + part_other.astype(F32)).astype(BF)
    part_ends = [line_block(part_places, 1).astype(BF), line_block(part_places, places - 1).astype(BF)]
    float_in = hidden_in[0].astype(F32)
    output = (float_in + out_rows.astype(F32)).astype(BF)[None]
    (rest_all,) = tie([rest_all], [output])
    rest_blocks = rest_all.reshape(parts, -1, model)
    grad_down_w = rest_blocks[:, :unit_width].reshape(-1, model).astype(F32)
    if spread:
        grad_proj_w = rest_blocks[:, unit_width:].reshape(-1, model).astype(F32)
    else:
        grad_proj_w = lax.dynamic_slice_in_dim(
            gather_ctx(lax.psum(proj_part.astype(F32), "fsdp")), fsdp_at * shard_rows, shard_rows, 0
        )
    terms, others, part_places, part_ends, attn_got, output, grad_down_w, grad_proj_w = stage(
        terms, other_terms[0], part_places, part_ends, attn_got, output, grad_down_w, grad_proj_w
    )
    terms = sum_of(terms, others, other_terms[1])

    waiting = jnp.stack([attn_sum, *attn_got])
    grad_step = None
    for step in range(2, places):
        attn_held += [block[None] for block in attn_got]
        attn_got = gather_step(step, attn_got)
        grad_step = line_step(part_places, step - 1, grad_step) if grad_step else line_start(part_ends)
        attn_other.append(flip(waiting, "ctx", 0))
        late = []
        if step == 3:
            (pair_all,) = tie([pair_all], [grad_down_w])
            late = list(assemble(pair_all, pair_plan))
        grad_step, attn_got, attn_other, late, part_places = stage(
            grad_step, attn_got, attn_other, late, part_places
        )
        if step == 3:
            grad_gate_w, grad_up_w = late
        waiting = jnp.stack(attn_got)
    attn_held += [block[None] for block in attn_got]
    grad_step = line_step(part_places, places - 1, grad_step) if grad_step else line_start(part_ends)
    attn_other.append(flip(waiting, "ctx", 0))
    sources = [(attn_held[0], 0), (attn_other[0], 0)]
    for step in range(1, places):
        sources += [(attn_held[2 * step - 1], 0), (attn_held[2 * step], 0)]
        first = 1 if step == 1 else 0
        sources += [(attn_other[step - 1], first), (attn_other[step - 1], first + 1)]
    grad_attn_w = assemble_line(sources, line_origins(), attn_plan[0])
    terms = terms + flip(terms, "ctx", 0)
    other_terms = flip(terms, "ctx", 1)
    grad_attn_w, other_terms, grad_step, part_places = stage(grad_attn_w, other_terms, grad_step, part_places)
    terms = terms + other_terms
    for bit in range(2, bits_of(parts)):
        terms = terms + flip(terms, "ctx", bit)
    terms = terms.reshape(-1)
    grad_normed = line_block(part_places, 0) + grad_step[0].astype(F32) + grad_step[1].astype(F32)

    normal_hat, inverse_std = normalise(float_in)
    b_rows = b_qkv.shape[0]
    grad_b_attn = lax.dynamic_slice_in_dim(terms, 2 * model + fsdp_at * b_rows, b_rows, 0)
    grad_gain = lax.dynamic_slice_in_dim(terms, fsdp_at * shard_rows, shard_rows, 0)
    grad_bias = lax.dynamic_slice_in_dim(terms, model + fsdp_at * shard_rows, shard_rows, 0)

    grad_hat = grad_normed * gain_full
    grad_in = out_grad[0].astype(F32) + inverse_std * (
        grad_hat
        - jnp.mean(grad_hat, axis=1, keepdims=True)
        - normal_hat * jnp.mean(grad_hat * normal_hat, axis=1, keepdims=True)
    )
    grad_in = grad_in.astype(BF)[None]
    return (
        output,
        grad_in,
        grad_gain,
        grad_bias,
        grad_attn_w,
        grad_b_attn,
        grad_proj_w,
        grad_gate_w,
        grad_up_w,
        grad_down_w,
    )


def solution(mesh):
    return jax.shard_map(
        shards,
        mesh=mesh,
        in_specs=(
            P("fsdp", "ctx", None),
            P("fsdp", "ctx", None),
            P("fsdp", None),
            P("fsdp", None),
            P("fsdp"),
            P("fsdp"),
            P("fsdp", None),
            P("fsdp"),
            P("fsdp", None),
            P("fsdp", None),
            P("fsdp", None),
            P("fsdp", None),
        ),
        out_specs=(
            P("fsdp", "ctx", None),
            P("fsdp", "ctx", None),
            P("fsdp"),
            P("fsdp"),
            P("fsdp", None),
            P("fsdp"),
            P("fsdp", None),
            P("fsdp", None),
            P("fsdp", None),
            P("fsdp", None),
        ),
        check_vma=False,
    )
```

```python
import functools

import jax
import jax.numpy as jnp
from jax import lax
from jax.experimental import pallas as pl
from jax.experimental.pallas import tpu as pltpu
from jax.sharding import PartitionSpec as P

HD = 64
ROT = 16
BLOCK = 128
CHUNK = 256
BF = jnp.bfloat16
F32 = jnp.float32
MASKED = -1e30


def matmul(left, right):
    return jnp.dot(left, right, preferred_element_type=F32)


def matmul_nt(left, right):
    return lax.dot_general(left, right, (((1,), (1,)), ((), ())), preferred_element_type=F32)


def matmul_tn(left, right):
    return lax.dot_general(left, right, (((0,), (0,)), ((), ())), preferred_element_type=F32)


def flip(values, axis, bit):
    count = lax.axis_size(axis)
    return lax.ppermute(values, axis, [(i, i ^ (1 << bit)) for i in range(count)])


def bits_of(count):
    bits = count.bit_length() - 1
    assert count == 1 << bits
    return bits


def gather_rows(values, axis, order):
    me = lax.axis_index(axis)
    count = lax.axis_size(axis)
    held = values[None]
    steps = [0]
    for bit in order:
        other = flip(held, axis, bit)
        held = jnp.concatenate([held, other], axis=0)
        steps = steps + [s ^ (1 << bit) for s in steps]
    rows = values.shape[0]
    out = jnp.zeros((count * rows,) + values.shape[1:], values.dtype)
    for place, step in enumerate(steps):
        out = lax.dynamic_update_slice_in_dim(out, held[place], (me ^ step) * rows, 0)
    return out


def placed(pieces, places, total):
    out = jnp.zeros((total,) + pieces[0].shape[1:], pieces[0].dtype)
    for piece, place in zip(pieces, places):
        out = lax.dynamic_update_slice_in_dim(out, piece, place, 0)
    return out


def gather_first(values):
    if lax.axis_size("fsdp") != 4:
        return [gather_rows(values, "fsdp", list(range(bits_of(lax.axis_size("fsdp")))))]
    return [flip(values, "fsdp", 0), flip(values, "fsdp", 1)]


def gather_second(values, first):
    if lax.axis_size("fsdp") != 4:
        return []
    half = values.shape[0] // 2 // 16 * 16
    return [flip(first[0][:half], "fsdp", 1), flip(first[1][half:], "fsdp", 0)]


def gathered_pieces(values, first, second, rows):
    count = lax.axis_size("fsdp")
    shard = values.shape[0]
    if count != 4:
        return [(first[0], i * shard, rows, i * rows) for i in range(count)]
    me = lax.axis_index("fsdp")
    half = shard // 2 // 16 * 16
    return [
        (values, 0, rows, me * rows),
        (first[0], 0, rows, (me ^ 1) * rows),
        (first[1], 0, rows, (me ^ 2) * rows),
        (second[0], 0, half, (me ^ 3) * rows),
        (second[1], 0, rows - half, (me ^ 3) * rows + half),
    ]


def gathered_rest(values, first, second, rows):
    count = lax.axis_size("fsdp")
    shard = values.shape[0]
    if count != 4:
        return first[0].reshape(count, shard, -1)[:, rows:]
    me = lax.axis_index("fsdp")
    half = shard // 2 // 16 * 16
    tails = [values[rows:], first[0][rows:], first[1][rows:], second[1][rows - half :]]
    return placed([t[None] for t in tails], [me, me ^ 1, me ^ 2, me ^ 3], count)


def others_of(values, axis, stride, count):
    size = lax.axis_size(axis)
    digit = lax.axis_index(axis) // stride % count

    def moved(i, by):
        at = i // stride % count
        return i + ((at + by) % count - at) * stride

    return [lax.ppermute(values, axis, [(i, moved(i, by)) for i in range(size)]) for by in range(1, count)], digit


def sum_of(values, others, digit):
    count = len(others) + 1
    out = jnp.zeros((count,) + values.shape, values.dtype)
    for by, piece in enumerate([values] + others):
        out = lax.dynamic_update_slice_in_dim(out, piece[None], (digit + count - by) % count, 0)
    total = out[0]
    for at in range(1, count):
        total = total + out[at]
    return total


def scatter_rows(values, axis, order):
    me = lax.axis_index(axis)
    count = lax.axis_size(axis)
    bits = bits_of(count)
    rows = values.shape[0] // count
    held = values.reshape((2,) * bits + (rows,) + values.shape[1:])
    left = list(range(bits))
    for bit in order:
        at = len(left) - 1 - left.index(bit)
        mine = (me >> bit) & 1
        sent = lax.dynamic_index_in_dim(held, 1 - mine, at, keepdims=False).astype(BF)
        kept = lax.dynamic_index_in_dim(held, mine, at, keepdims=False)
        held = kept.astype(F32) + flip(sent, axis, bit).astype(F32)
        left.remove(bit)
    return held


def fsdp_block(part, index):
    rows = part.shape[0] // lax.axis_size("fsdp")
    return lax.dynamic_slice_in_dim(part, index * rows, rows, 0)


def halves(part):
    half = part.shape[1] // 2 // 128 * 128
    return part[:, :half], part[:, half:]


def scatter_first(sides):
    if lax.axis_size("fsdp") != 4:
        return [scatter_rows(part, "fsdp", list(range(bits_of(lax.axis_size("fsdp"))))) for part in sides]
    me = lax.axis_index("fsdp")
    return [
        flip(jnp.stack([fsdp_block(sides[1], me ^ 3), fsdp_block(sides[1], me ^ 1)]), "fsdp", 0),
        flip(jnp.stack([fsdp_block(sides[0], me ^ 3), fsdp_block(sides[0], me ^ 2)]), "fsdp", 1),
    ]


def scatter_second(sides, first):
    if lax.axis_size("fsdp") != 4:
        return []
    me = lax.axis_index("fsdp")
    across = fsdp_block(sides[0], me ^ 1).astype(F32) + first[1][0].astype(F32)
    along = fsdp_block(sides[1], me ^ 2).astype(F32) + first[0][0].astype(F32)
    return [flip(across.astype(BF), "fsdp", 0), flip(along.astype(BF), "fsdp", 1)]


def scatter_last(sides, first, second):
    if lax.axis_size("fsdp") != 4:
        return first[0].astype(BF), first[1].astype(BF)
    me = lax.axis_index("fsdp")
    left = fsdp_block(sides[0], me).astype(F32) + first[1][1].astype(F32) + second[0].astype(F32)
    right = fsdp_block(sides[1], me).astype(F32) + first[0][1].astype(F32) + second[1].astype(F32)
    return left.astype(BF), right.astype(BF)


def gather_ctx(values):
    return lax.all_gather(values, "ctx", axis=0, tiled=True)


def split_cores(part):
    parts = lax.axis_size("ctx")
    core = lax.axis_index("ctx") % 2
    blocks = part.reshape(parts // 2, 2, part.shape[0] // parts, part.shape[1])
    return [lax.dynamic_index_in_dim(blocks, k, 1, keepdims=False) for k in (core, 1 - core)]


def scatter_ctx(values):
    return lax.psum_scatter(values, "ctx", scatter_dimension=0, tiled=True)


def shift(values, by, keep):
    places = lax.axis_size("ctx") // 2
    pairs = [
        (2 * p + k, 2 * (p + by) + k) for p in range(places) for k in range(2) if keep(p) and 0 <= p + by < places
    ]
    return lax.ppermute(values, "ctx", pairs)


def line_block(blocks, s):
    places = blocks.shape[0]
    at = (lax.axis_index("ctx") // 2 + places - s) % places
    return lax.dynamic_index_in_dim(blocks, at, 0, keepdims=False).astype(F32)


def line_start(ends):
    last = lax.axis_size("ctx") // 2 - 1
    return [shift(ends[0], 1, lambda p: p <= 0), shift(ends[1], -1, lambda p: p >= last)]


def line_step(blocks, step, before):
    places = blocks.shape[0]
    up, down = line_block(blocks, step), line_block(blocks, places - step)
    if before:
        up, down = up + before[0].astype(F32), down + before[1].astype(F32)
    return [
        shift(up.astype(BF), 1, lambda p: p <= step - 1),
        shift(down.astype(BF), -1, lambda p: p >= places - step),
    ]


def gather_step(step, before):
    places = lax.axis_size("ctx") // 2
    return [
        shift(before[0], 1, lambda p: p >= step - 1),
        shift(before[1], -1, lambda p: p <= places - step),
    ]


def line_origins():
    me = lax.axis_index("ctx")
    places = lax.axis_size("ctx") // 2
    at, core = me // 2, me % 2
    out = [me, me ^ 1]
    for s in range(1, places):
        ends = (jnp.where(at >= s, at - s, -1), jnp.where(at + s < places, at + s, -1))
        for j in range(2):
            out += [jnp.where(p < 0, -1, 2 * p + (core ^ j)) for p in ends]
    return jnp.stack(out).astype(jnp.int32)


def nothing_kernel(*refs):
    return None


def tie(values, after):
    anywhere = pl.BlockSpec(memory_space=pl.ANY)
    return pl.pallas_call(
        nothing_kernel,
        out_shape=tuple(jax.ShapeDtypeStruct(v.shape, v.dtype) for v in values),
        in_specs=[anywhere] * (len(values) + len(after)),
        out_specs=tuple([anywhere] * len(values)),
        input_output_aliases={i: i for i in range(len(values))},
        name="tie",
    )(*values, *after)


def stage(*groups):
    leaves, tree = jax.tree.flatten(groups)
    return jax.tree.unflatten(tree, tie(leaves, []))


def rows_at(index, size):
    return pl.ds(pl.multiple_of(index * size, size), size)


def turn(values, tables, rows, direction):
    width = values.shape[1]
    cosine, lead, tail = (jnp.concatenate([ref[rows, :]] * (width // 128), axis=1) for ref in tables)
    ahead = pltpu.roll(values, width - ROT // 2, 1)
    behind = pltpu.roll(values, ROT // 2, 1)
    return values * cosine + direction * (ahead * lead + behind * tail)


def split_heads(target, values, heads):
    head_of = lax.broadcasted_iota(jnp.int32, values.shape, 1) // HD
    for h in range(heads):
        target[h * CHUNK : (h + 1) * CHUNK, :] = jnp.where(head_of == h, values, jnp.zeros_like(values))


def visible(i, j, begin):
    key_at = lax.broadcasted_iota(jnp.int32, (CHUNK, CHUNK), 0)
    query_at = lax.broadcasted_iota(jnp.int32, (CHUNK, CHUNK), 1)
    return (key_at - query_at <= (i - j) * CHUNK) & (key_at >= begin - j * CHUNK)


def forward_kernel(
    heads,
    slot_ref,
    low_ref,
    merged_ref,
    cos_ref,
    lead_ref,
    tail_ref,
    begin_ref,
    mixed_ref,
    q_ref,
    k_ref,
    v_ref,
    total_ref,
    ot_ref,
    vt_ref,
    qm_ref,
    s_ref,
):
    width = heads * HD
    tokens = merged_ref.shape[0]
    tables = (cos_ref, lead_ref, tail_ref)

    def prepare(block, carry):
        source = rows_at(slot_ref[block], BLOCK)
        target = rows_at(block, BLOCK)
        query = turn(merged_ref[source, 0:width], tables, source, 1.0).astype(BF)
        key = turn(merged_ref[source, width : 2 * width], tables, source, 1.0).astype(BF)
        value = merged_ref[source, 2 * width : 3 * width].astype(BF)
        q_ref[target, :] = query * jnp.asarray(HD ** (-0.5), BF)
        k_ref[target, :] = key
        v_ref[target, :] = value
        vt_ref[:, target] = value.T
        return carry

    lax.fori_loop(0, tokens // BLOCK, prepare, 0)

    def query_chunk(i, carry):
        here = rows_at(i, CHUNK)
        split_heads(qm_ref, q_ref[here, :], heads)
        ot_ref[:, here] = jnp.zeros((width, CHUNK), F32)
        low = low_ref[i]
        begin = begin_ref[i]

        def score(j, tops):
            there = rows_at(j, CHUNK)
            key = k_ref[there, :]
            allowed = visible(i, j, begin)
            out = []
            for h in range(heads):
                s = matmul_nt(key, qm_ref[h * CHUNK : (h + 1) * CHUNK, :])
                s = jnp.where(allowed, s, MASKED)
                s_ref[h, there, :] = s
                out.append(jnp.maximum(tops[h], jnp.max(s, axis=0, keepdims=True)))
            return tuple(out)

        tops = lax.fori_loop(
            low, i + 1, score, tuple(jnp.full((1, CHUNK), MASKED, F32) for _ in range(heads))
        )

        def value_side(j, sums):
            there = rows_at(j, CHUNK)
            out = []
            for h in range(heads):
                span = slice(h * HD, (h + 1) * HD)
                e = jnp.exp(s_ref[h, there, :] - tops[h])
                out.append(sums[h] + jnp.sum(e, axis=0, keepdims=True))
                ot_ref[span, here] += matmul(vt_ref[span, there], e.astype(BF))
            return tuple(out)

        sums = lax.fori_loop(low, i + 1, value_side, tuple(jnp.zeros((1, CHUNK), F32) for _ in range(heads)))
        for h in range(heads):
            span = slice(h * HD, (h + 1) * HD)
            ot_ref[span, here] = ot_ref[span, here] * (1.0 / sums[h])
            total_ref[i, h : h + 1, :] = tops[h] + jnp.log(sums[h])
        mixed = ot_ref[:, here].T.astype(BF)
        for part in range(CHUNK // BLOCK):
            target = rows_at(slot_ref[i * (CHUNK // BLOCK) + part], BLOCK)
            mixed_ref[target, :] = mixed[part * BLOCK : (part + 1) * BLOCK]
        return carry

    lax.fori_loop(0, tokens // CHUNK, query_chunk, 0)


def backward_kernel(
    heads,
    slot_ref,
    low_ref,
    q_ref,
    k_ref,
    v_ref,
    total_ref,
    ot_ref,
    grad_mixed_ref,
    cos_ref,
    lead_ref,
    tail_ref,
    begin_ref,
    grad_merged_ref,
    kt_ref,
    qm_ref,
    gm_ref,
    p_ref,
    ds_ref,
    dqt_ref,
    dk_ref,
    dv_ref,
):
    width = heads * HD
    tokens = q_ref.shape[0]
    tables = (cos_ref, lead_ref, tail_ref)

    def prepare(block, carry):
        here = rows_at(block, BLOCK)
        kt_ref[:, here] = k_ref[here, :].T
        dk_ref[here, :] = jnp.zeros((BLOCK, width), F32)
        dv_ref[here, :] = jnp.zeros((BLOCK, width), F32)
        return carry

    lax.fori_loop(0, tokens // BLOCK, prepare, 0)

    def query_chunk(i, carry):
        here = rows_at(i, CHUNK)
        targets = [rows_at(slot_ref[i * (CHUNK // BLOCK) + part], BLOCK) for part in range(CHUNK // BLOCK)]
        grad = jnp.concatenate([grad_mixed_ref[target, :] for target in targets], axis=0)
        split_heads(qm_ref, q_ref[here, :], heads)
        split_heads(gm_ref, grad, heads)
        dqt_ref[...] = jnp.zeros_like(dqt_ref)
        product = grad.T.astype(F32) * ot_ref[:, here]
        dots = [jnp.sum(product[h * HD : (h + 1) * HD], axis=0, keepdims=True) for h in range(heads)]
        totals = [total_ref[i, h : h + 1, :] for h in range(heads)]
        begin = begin_ref[i]

        def key_chunk(j, carry):
            there = rows_at(j, CHUNK)
            key = k_ref[there, :]
            value = v_ref[there, :]
            allowed = visible(i, j, begin)
            for h in range(heads):
                span = slice(h * HD, (h + 1) * HD)
                part = slice(h * CHUNK, (h + 1) * CHUNK)
                s = matmul_nt(key, qm_ref[part, :])
                probs = jnp.exp(jnp.where(allowed, s, MASKED) - totals[h])
                p_ref[:, part] = probs.astype(BF)
                ds = (probs * (matmul_nt(value, gm_ref[part, :]) - dots[h])).astype(BF)
                ds_ref[:, part] = ds
                dqt_ref[span, :] += matmul(kt_ref[span, there], ds)
            dv_ref[there, :] += matmul(p_ref[...], gm_ref[...])
            dk_ref[there, :] += matmul(ds_ref[...], qm_ref[...])
            return carry

        lax.fori_loop(low_ref[i], i + 1, key_chunk, 0)
        grad_query = dqt_ref[...].T * HD ** (-0.5)
        for part, target in enumerate(targets):
            rows = slice(part * BLOCK, (part + 1) * BLOCK)
            grad_merged_ref[target, 0:width] = turn(grad_query[rows], tables, target, -1.0).astype(BF)
        return carry

    lax.fori_loop(0, tokens // CHUNK, query_chunk, 0)

    def finish(block, carry):
        source = rows_at(block, BLOCK)
        target = rows_at(slot_ref[block], BLOCK)
        grad_merged_ref[target, width : 2 * width] = turn(dk_ref[source, :], tables, target, -1.0).astype(BF)
        grad_merged_ref[target, 2 * width : 3 * width] = dv_ref[source, :].astype(BF)
        return carry

    lax.fori_loop(0, tokens // BLOCK, finish, 0)


WHOLE = pl.BlockSpec(memory_space=pltpu.VMEM)
SCALAR = pl.BlockSpec(memory_space=pltpu.SMEM)
ANYWHERE = pl.BlockSpec(memory_space=pl.ANY)


def attention_forward(heads, slots, lows, merged, tables, begins):
    tokens = merged.shape[0]
    width = heads * HD
    rows = jax.ShapeDtypeStruct((tokens, width), BF)
    return pl.pallas_call(
        functools.partial(forward_kernel, heads),
        out_shape=(
            rows,
            rows,
            rows,
            rows,
            jax.ShapeDtypeStruct((tokens // CHUNK, heads, CHUNK), F32),
            jax.ShapeDtypeStruct((width, tokens), F32),
        ),
        in_specs=[SCALAR, SCALAR] + [WHOLE] * 5,
        out_specs=(WHOLE,) * 6,
        scratch_shapes=[
            pltpu.VMEM((width, tokens), BF),
            pltpu.VMEM((heads * CHUNK, width), BF),
            pltpu.VMEM((heads, tokens, CHUNK), F32),
        ],
        compiler_params=pltpu.CompilerParams(vmem_limit_bytes=48 * 1024 * 1024),
        cost_estimate=pl.CostEstimate(flops=25_000_000_000, transcendentals=0, bytes_accessed=0),
        name="attention_forward",
    )(slots, lows, merged, *tables, begins)


def attention_backward(heads, slots, lows, kept, grad_mixed, tables, begins):
    tokens, width = grad_mixed.shape
    return pl.pallas_call(
        functools.partial(backward_kernel, heads),
        out_shape=jax.ShapeDtypeStruct((tokens, 3 * width), BF),
        in_specs=[SCALAR, SCALAR] + [WHOLE] * 10,
        out_specs=WHOLE,
        scratch_shapes=[
            pltpu.VMEM((width, tokens), BF),
            pltpu.VMEM((heads * CHUNK, width), BF),
            pltpu.VMEM((heads * CHUNK, width), BF),
            pltpu.VMEM((CHUNK, heads * CHUNK), BF),
            pltpu.VMEM((CHUNK, heads * CHUNK), BF),
            pltpu.VMEM((width, CHUNK), F32),
            pltpu.VMEM((tokens, width), F32),
            pltpu.VMEM((tokens, width), F32),
        ],
        compiler_params=pltpu.CompilerParams(vmem_limit_bytes=48 * 1024 * 1024),
        cost_estimate=pl.CostEstimate(flops=40_000_000_000, transcendentals=0, bytes_accessed=0),
        name="attention_backward",
    )(slots, lows, *kept, grad_mixed, *tables, begins)


def fetch(at_ref, pieces, spans, target, sem):
    copies = []
    for n, (piece, (first, rows)) in enumerate(zip(pieces, spans)):
        place = pl.ds(pl.multiple_of(at_ref[n], 16), rows)
        copies.append(pltpu.make_async_copy(piece.at[pl.ds(first, rows), :], target.at[place, :], sem.at[n]))
    for copy in copies:
        copy.start()
    return copies


def attn_kernel(spans, at_ref, hidden_ref, gain_ref, bias_ref, shift_ref, *refs):
    n = len(spans)
    normed_ref, merged_ref, w_attn, sem = refs[n:]

    @pl.when(pl.program_id(0) == 0)
    def _():
        for copy in fetch(at_ref, refs[:n], spans, w_attn, sem):
            copy.wait()

    normal, _ = normalise(hidden_ref[...].astype(F32))
    normed = (normal * gain_ref[...] + bias_ref[...]).astype(BF)
    normed_ref[...] = normed
    merged_ref[...] = matmul(normed, w_attn[...]) + shift_ref[...]


def pair_kernel(spans, at_ref, normed_ref, *refs):
    n = len(spans)
    gate_pieces, up_pieces = refs[:n], refs[n : 2 * n]
    act_ref, slope_ref, silu_ref, w_gate, w_up, *sems = refs[2 * n :]

    @pl.when(pl.program_id(0) == 0)
    def _():
        copies = fetch(at_ref, gate_pieces, spans, w_gate, sems[0])
        copies += fetch(at_ref, up_pieces, spans, w_up, sems[1])
        for copy in copies:
            copy.wait()

    normed = normed_ref[...]
    gating = matmul(normed, w_gate[...])
    rising = matmul(normed, w_up[...])
    sigma = jax.nn.sigmoid(gating)
    silu = gating * sigma
    act_ref[...] = (silu * rising).astype(BF)
    slope_ref[...] = (rising * sigma * (1.0 + gating * (1.0 - sigma))).astype(BF)
    silu_ref[...] = silu.astype(BF)


def row_block(width):
    return pl.BlockSpec((CHUNK, width), lambda i: (i, 0))


def full_block(array):
    return pl.BlockSpec(array.shape, lambda i: (0, 0))


def split_pieces(pieces):
    at = jnp.stack([jnp.asarray(piece[3], jnp.int32) for piece in pieces])
    return at, [piece[0] for piece in pieces], tuple((piece[1], piece[2]) for piece in pieces)


def attn_side(hidden, gain, bias, shift, pieces):
    tokens, model = hidden.shape
    at, arrays, spans = split_pieces(pieces)
    n = len(spans)
    width = arrays[0].shape[1]
    return pl.pallas_call(
        functools.partial(attn_kernel, spans),
        grid=(tokens // CHUNK,),
        out_shape=(jax.ShapeDtypeStruct((tokens, model), BF), jax.ShapeDtypeStruct((tokens, width), F32)),
        in_specs=[SCALAR, row_block(model), full_block(gain), full_block(bias), full_block(shift)] + [ANYWHERE] * n,
        out_specs=(row_block(model), row_block(width)),
        scratch_shapes=[pltpu.VMEM((model, width), BF), pltpu.SemaphoreType.DMA((n,))],
        compiler_params=pltpu.CompilerParams(vmem_limit_bytes=56 * 1024 * 1024),
        cost_estimate=pl.CostEstimate(flops=18_000_000_000, transcendentals=0, bytes_accessed=0),
        name="attn_side",
    )(at, hidden, gain, bias, shift, *arrays)


def pair_side(normed, gate_pieces, up_pieces):
    tokens, model = normed.shape
    at, gates, spans = split_pieces(gate_pieces)
    ups = split_pieces(up_pieces)[1]
    n = len(spans)
    units = gates[0].shape[1]
    return pl.pallas_call(
        functools.partial(pair_kernel, spans),
        grid=(tokens // CHUNK,),
        out_shape=(jax.ShapeDtypeStruct((tokens, units), BF),) * 3,
        in_specs=[SCALAR, row_block(model)] + [ANYWHERE] * (2 * n),
        out_specs=(row_block(units),) * 3,
        scratch_shapes=[
            pltpu.VMEM((model, units), BF),
            pltpu.VMEM((model, units), BF),
            pltpu.SemaphoreType.DMA((n,)),
            pltpu.SemaphoreType.DMA((n,)),
        ],
        compiler_params=pltpu.CompilerParams(vmem_limit_bytes=56 * 1024 * 1024),
        cost_estimate=pl.CostEstimate(flops=28_000_000_000, transcendentals=0, bytes_accessed=0),
        name="pair_side",
    )(at, normed, *gates, *ups)


def fetch_rest(spans, at_ref, refs, lower, proj, sems):
    n = len(spans) // 2
    units = lower.shape[0]
    filled = sum(rows for _, rows in spans[:n])
    if filled < units:
        lower[filled:, :] = jnp.zeros((units - filled, lower.shape[1]), BF)
    copies = fetch(at_ref.at[0], refs[:n], spans[:n], lower, sems[0])
    copies += fetch(at_ref.at[1], refs[n:], spans[n:], proj, sems[1])
    for copy in copies:
        copy.wait()


def grad_kernel(spans, at_ref, grad_ref, slope_ref, silu_ref, *refs):
    n = len(spans)
    gate_ref, up_ref, mixed_ref, lower, proj, *sems = refs[n:]

    @pl.when(pl.program_id(0) == 0)
    def _():
        fetch_rest(spans, at_ref, refs[:n], lower, proj, sems)

    grad = grad_ref[...]
    act = matmul_nt(grad, lower[...])
    mixed_ref[...] = matmul_nt(grad, proj[...]).astype(BF)
    gate_ref[...] = (act * slope_ref[...].astype(F32)).astype(BF)
    up_ref[...] = (act * silu_ref[...].astype(F32)).astype(BF)


def rest_scratch(units, width, model, n):
    return [
        pltpu.VMEM((units, model), BF),
        pltpu.VMEM((width, model), BF),
        pltpu.SemaphoreType.DMA((n,)),
        pltpu.SemaphoreType.DMA((n,)),
    ]


def split_rest(lower_pieces, proj_pieces):
    lower_at, lowers, lower_spans = split_pieces(lower_pieces)
    proj_at, projs, proj_spans = split_pieces(proj_pieces)
    return jnp.stack([lower_at, proj_at]), lowers + projs, lower_spans + proj_spans


def grad_side(grad, slope, silu, width, lower_pieces, proj_pieces):
    tokens, model = grad.shape
    units = slope.shape[1]
    at, arrays, spans = split_rest(lower_pieces, proj_pieces)
    return pl.pallas_call(
        functools.partial(grad_kernel, spans),
        grid=(tokens // CHUNK,),
        out_shape=(
            jax.ShapeDtypeStruct((tokens, units), BF),
            jax.ShapeDtypeStruct((tokens, units), BF),
            jax.ShapeDtypeStruct((tokens, width), BF),
        ),
        in_specs=[SCALAR, row_block(model), row_block(units), row_block(units)] + [ANYWHERE] * len(arrays),
        out_specs=(row_block(units), row_block(units), row_block(width)),
        scratch_shapes=rest_scratch(units, width, model, len(arrays) // 2),
        compiler_params=pltpu.CompilerParams(vmem_limit_bytes=56 * 1024 * 1024),
        cost_estimate=pl.CostEstimate(flops=18_000_000_000, transcendentals=0, bytes_accessed=0),
        name="grad_side",
    )(at, grad, slope, silu, *arrays)


def out_kernel(spans, at_ref, mixed_ref, act_ref, *refs):
    n = len(spans)
    out_ref, lower, proj, *sems = refs[n:]

    @pl.when(pl.program_id(0) == 0)
    def _():
        fetch_rest(spans, at_ref, refs[:n], lower, proj, sems)

    out_ref[...] = (matmul(mixed_ref[...], proj[...]) + matmul(act_ref[...], lower[...])).astype(BF)


def out_side(mixed, act, model, lower_pieces, proj_pieces):
    tokens, width = mixed.shape
    units = act.shape[1]
    at, arrays, spans = split_rest(lower_pieces, proj_pieces)
    return pl.pallas_call(
        functools.partial(out_kernel, spans),
        grid=(tokens // CHUNK,),
        out_shape=jax.ShapeDtypeStruct((tokens, model), BF),
        in_specs=[SCALAR, row_block(width), row_block(units)] + [ANYWHERE] * len(arrays),
        out_specs=row_block(model),
        scratch_shapes=rest_scratch(units, width, model, len(arrays) // 2),
        compiler_params=pltpu.CompilerParams(vmem_limit_bytes=56 * 1024 * 1024),
        cost_estimate=pl.CostEstimate(flops=15_000_000_000, transcendentals=0, bytes_accessed=0),
        name="out_side",
    )(at, mixed, act, *arrays)


def input_kernel(spans, at_ref, gate_ref, up_ref, merged_ref, hidden_ref, *refs):
    n = len(spans)
    gate_pieces, up_pieces, attn_pieces = refs[:n], refs[n : 2 * n], refs[2 * n : 3 * n]
    part_ref, terms_ref, w_gate, w_up, w_attn, *sems = refs[3 * n :]

    @pl.when(pl.program_id(0) == 0)
    def _():
        copies = fetch(at_ref, gate_pieces, spans, w_gate, sems[0])
        copies += fetch(at_ref, up_pieces, spans, w_up, sems[1])
        copies += fetch(at_ref, attn_pieces, spans, w_attn, sems[2])
        terms_ref[...] = jnp.zeros_like(terms_ref)
        for copy in copies:
            copy.wait()

    part = matmul_nt(gate_ref[...], w_gate[...]) + matmul_nt(up_ref[...], w_up[...])
    part = part + matmul_nt(merged_ref[...], w_attn[...])
    part_ref[...] = part.astype(BF)
    normal, _ = normalise(hidden_ref[...].astype(F32))
    terms_ref[0:1, :] += jnp.sum(part * normal, axis=0, keepdims=True)
    terms_ref[1:2, :] += jnp.sum(part, axis=0, keepdims=True)


def input_side(grad_gate, grad_up, grad_merged, hidden, gate_pieces, up_pieces, attn_pieces):
    tokens, model = hidden.shape
    at, gates, spans = split_pieces(gate_pieces)
    ups, attns = split_pieces(up_pieces)[1], split_pieces(attn_pieces)[1]
    n = len(spans)
    units, width = grad_gate.shape[1], grad_merged.shape[1]
    return pl.pallas_call(
        functools.partial(input_kernel, spans),
        grid=(tokens // CHUNK,),
        out_shape=(jax.ShapeDtypeStruct((tokens, model), BF), jax.ShapeDtypeStruct((2, model), F32)),
        in_specs=[SCALAR, row_block(units), row_block(units), row_block(width), row_block(model)]
        + [ANYWHERE] * (3 * n),
        out_specs=(row_block(model), pl.BlockSpec((2, model), lambda i: (0, 0))),
        scratch_shapes=[
            pltpu.VMEM((model, units), BF),
            pltpu.VMEM((model, units), BF),
            pltpu.VMEM((model, width), BF),
            pltpu.SemaphoreType.DMA((n,)),
            pltpu.SemaphoreType.DMA((n,)),
            pltpu.SemaphoreType.DMA((n,)),
        ],
        compiler_params=pltpu.CompilerParams(vmem_limit_bytes=56 * 1024 * 1024),
        cost_estimate=pl.CostEstimate(flops=30_000_000_000, transcendentals=0, bytes_accessed=0),
        name="input_side",
    )(at, grad_gate, grad_up, grad_merged, hidden, *gates, *ups, *attns)


def assemble_kernel(plan, source_ref, *targets):
    for target, pieces in zip(targets, plan):
        at = 0
        for part, offset, width in pieces:
            target[:, at : at + width] = source_ref[part, :, offset : offset + width].astype(F32)
            at += width


def assemble(gathered, plan):
    parts, rows, columns = gathered.shape
    step = 64
    widths = [sum(piece[2] for piece in pieces) for pieces in plan]
    return pl.pallas_call(
        functools.partial(assemble_kernel, plan),
        grid=(rows // step,),
        out_shape=tuple(jax.ShapeDtypeStruct((rows, w), F32) for w in widths),
        in_specs=[pl.BlockSpec((parts, step, columns), lambda i: (0, i, 0))],
        out_specs=tuple(pl.BlockSpec((step, w), lambda i: (i, 0)) for w in widths),
        compiler_params=pltpu.CompilerParams(vmem_limit_bytes=40 * 1024 * 1024),
        name="assemble",
    )(gathered)


def assemble_line_kernel(plan, count, at_ref, *refs):
    target, held = refs[count], refs[count + 1]
    for n in range(count):

        @pl.when(at_ref[n] >= 0)
        def _():
            held[jnp.maximum(at_ref[n], 0)] = refs[n][0]

    at = 0
    for part, offset, width in plan:
        target[:, at : at + width] = held[part, :, offset : offset + width].astype(F32)
        at += width


def assemble_line(sources, origins, plan):
    parts = lax.axis_size("ctx")
    rows, columns = sources[0][0].shape[1:]
    step = 64
    width = sum(piece[2] for piece in plan)

    def block(n, index):
        return pl.BlockSpec((1, step, columns), lambda i, at: (index, jnp.where(at[n] >= 0, i, 0), 0))

    return pl.pallas_call(
        functools.partial(assemble_line_kernel, plan, len(sources)),
        out_shape=jax.ShapeDtypeStruct((rows, width), F32),
        grid_spec=pltpu.PrefetchScalarGridSpec(
            num_scalar_prefetch=1,
            grid=(rows // step,),
            in_specs=[block(n, index) for n, (_, index) in enumerate(sources)],
            out_specs=pl.BlockSpec((step, width), lambda i, at: (i, 0)),
            scratch_shapes=[pltpu.VMEM((parts, step, columns), BF)],
        ),
        compiler_params=pltpu.CompilerParams(vmem_limit_bytes=40 * 1024 * 1024),
        name="assemble_line",
    )(origins, *[array for array, _ in sources])


def stream_places(order_row, length_row):
    places = (order_row[:, None] * BLOCK + jnp.arange(BLOCK, dtype=jnp.int32)[None, :]).reshape(-1)
    return places, stream_begins(places, length_row)


def stream_begins(places, length_row):
    ends = jnp.cumsum(length_row)
    starts = ends - length_row
    return jnp.max(jnp.where(starts[None, :] <= places[:, None], starts[None, :], 0), axis=1)


def rotary_tables(places, begins):
    entry = jnp.arange(128) % HD
    turned = entry < ROT
    index = jnp.where(entry < ROT // 2, entry, entry - ROT // 2)
    inverse = 1.0 / 10000.0 ** ((2 * index).astype(F32) / ROT)
    angles = (places - begins).astype(F32)[:, None] * jnp.where(turned, inverse, 0.0)[None, :]
    cosine, sine = jnp.cos(angles), jnp.sin(angles)
    lead = jnp.where((entry < ROT // 2)[None, :], -sine, 0.0)
    tail = jnp.where((turned & (entry >= ROT // 2))[None, :], sine, 0.0)
    return cosine, lead, tail


def take_columns(array, starts, width):
    return [lax.dynamic_slice_in_dim(array, s, width, 1) for s in starts]


def normalise(rows):
    centre = jnp.mean(rows, axis=1, keepdims=True)
    deviation = rows - centre
    inverse_std = lax.rsqrt(jnp.mean(deviation * deviation, axis=1, keepdims=True) + 1e-05)
    return deviation * inverse_std, inverse_std


def shards(
    hidden_in,
    out_grad,
    lengths,
    block_order,
    ln_gain,
    ln_bias,
    w_qkv,
    b_qkv,
    w_out,
    w_gate,
    w_up,
    w_down,
):
    parts = lax.axis_size("ctx")
    shard_count = lax.axis_size("fsdp")
    ctx_at = lax.axis_index("ctx")
    fsdp_at = lax.axis_index("fsdp")
    rows = hidden_in.shape[1]
    model = w_out.shape[1]
    hidden = w_gate.shape[1]
    tokens = rows * parts
    heads = model // HD // parts
    width = heads * HD
    shard_rows = w_qkv.shape[0]

    hidden_all = gather_ctx(hidden_in[0])
    grad_all = gather_ctx(out_grad[0])

    spread = (model // HD) % (shard_count * parts) == 0
    pieces = shard_count if spread else 1
    head_span = model // pieces
    head_width = head_span // parts
    head_starts = [
        s * model + p * head_span + ctx_at * head_width for s in range(3) for p in range(pieces)
    ]
    unit_span = hidden // shard_count
    unit_width = unit_span // parts
    unit_starts = [p * unit_span + ctx_at * unit_width for p in range(shard_count)]

    units = shard_count * unit_width
    spare = -units % 128
    empty = jnp.zeros((shard_rows, spare), BF)
    vectors = jnp.concatenate([ln_gain, ln_bias, b_qkv])
    vector_rows = -(-vectors.shape[0] // (3 * width)) + 15
    vector_rows = vector_rows // 16 * 16
    vectors = jnp.pad(vectors, (0, vector_rows * 3 * width - vectors.shape[0])).reshape(vector_rows, 3 * width)
    w_attn_own = jnp.concatenate(take_columns(w_qkv, head_starts, head_width), axis=1)
    w_attn_own = jnp.concatenate([w_attn_own, vectors], axis=0)
    attn_near = gather_first(w_attn_own)
    w_gate_own = jnp.concatenate(take_columns(w_gate, unit_starts, unit_width) + [empty], axis=1)
    gate_near = gather_first(w_gate_own)
    w_up_own = jnp.concatenate(take_columns(w_up, unit_starts, unit_width) + [empty], axis=1)
    attn_near, w_up_own = stage(attn_near, w_up_own)
    attn_far = gather_second(w_attn_own, attn_near)
    up_near = gather_first(w_up_own)
    gate_near, attn_far = stage(gate_near, attn_far)
    gate_far = gather_second(w_gate_own, gate_near)
    w_down_own = lax.dynamic_slice_in_dim(w_down, ctx_at * unit_width, unit_width, 0)
    if spread:
        w_out_own = lax.dynamic_slice_in_dim(w_out, ctx_at * head_width, head_width, 0)
        w_rest_own = jnp.concatenate([w_down_own, w_out_own], axis=0)
    else:
        w_rest_own = w_down_own
    attn_pieces = gathered_pieces(w_attn_own, attn_near, attn_far, shard_rows)
    vectors = gathered_rest(w_attn_own, attn_near, attn_far, shard_rows).reshape(shard_count, -1)
    gain_full = vectors[:, :shard_rows].reshape(-1).astype(F32)
    bias_full = vectors[:, shard_rows : 2 * shard_rows].reshape(-1).astype(F32)
    b_attn = vectors[:, 2 * shard_rows : 2 * shard_rows + b_qkv.shape[0]].reshape(-1).astype(F32)
    b_attn_own = jnp.concatenate([lax.dynamic_slice_in_dim(b_attn, s, head_width, 0) for s in head_starts])

    order_row = block_order[0]
    blocks = order_row.shape[0]
    places, begins = stream_places(order_row, lengths[0])
    tables = rotary_tables(places, begins)
    slots = jnp.sum(
        jnp.where(
            order_row[None, :] == jnp.arange(blocks, dtype=jnp.int32)[:, None],
            jnp.arange(blocks, dtype=jnp.int32)[None, :],
            0,
        ),
        axis=1,
    ).astype(jnp.int32)
    stream_starts = stream_begins(jnp.arange(tokens, dtype=jnp.int32), lengths[0]).astype(jnp.int32)
    lows = stream_starts[::CHUNK] // CHUNK
    stream_starts = stream_starts.reshape(tokens // CHUNK, 1, CHUNK)

    up_near, gate_far, w_rest_own = stage(up_near, gate_far, w_rest_own)
    up_far = gather_second(w_up_own, up_near)
    rest_near = gather_first(w_rest_own)
    normed, merged = attn_side(hidden_all, gain_full[None], bias_full[None], b_attn_own[None], attn_pieces)
    mixed, *kept = attention_forward(heads, slots, lows, merged, tables, stream_starts)
    mixed, up_far, rest_near = stage(mixed, up_far, rest_near)
    rest_far = gather_second(w_rest_own, rest_near)
    gate_pieces = gathered_pieces(w_gate_own, gate_near, gate_far, shard_rows)
    up_pieces = gathered_pieces(w_up_own, up_near, up_far, shard_rows)
    act, slope, silu = pair_side(normed, gate_pieces, up_pieces)
    if spread and shard_count == 4:
        me = lax.axis_index("fsdp")
        corner = jnp.concatenate(rest_far, axis=0)
        held = list(zip([w_rest_own, rest_near[0], rest_near[1], corner], [me, me ^ 1, me ^ 2, me ^ 3]))
        lower_pieces = [(array, 0, unit_width, at * unit_width) for array, at in held]
        proj_pieces = [(array, unit_width, head_width, at * head_width) for array, at in held]
    else:
        w_rest = rest_near[0].reshape(shard_count, -1, model)
        w_lower = jnp.pad(w_rest[:, :unit_width].reshape(units, model), ((0, spare), (0, 0)))
        if spread:
            w_proj = w_rest[:, unit_width:].reshape(width, model)
        else:
            w_proj = lax.dynamic_slice_in_dim(
                lax.all_gather(w_out, "fsdp", axis=0, tiled=True), ctx_at * width, width, 0
            )
        lower_pieces = [(w_lower, 0, units + spare, 0)]
        proj_pieces = [(w_proj, 0, width, 0)]
    out_part = out_side(mixed, act, model, lower_pieces, proj_pieces)
    out_rows = scatter_ctx(out_part)

    (grad_all,) = tie([grad_all], [out_part])
    down_part = matmul_tn(act, grad_all).astype(BF)
    proj_part = matmul_tn(mixed, grad_all).astype(BF)
    if spread:
        rest_part = jnp.concatenate(
            [p.reshape(shard_count, -1, model) for p in (down_part[:units], proj_part)], axis=1
        ).reshape(-1, model)
    else:
        rest_part = down_part[:units]
    rest_part, grad_all = stage(rest_part, grad_all)
    rest_first = scatter_first(halves(rest_part))
    grad_gate, grad_up, grad_mixed = grad_side(grad_all, slope, silu, width, lower_pieces, proj_pieces)
    grad_gate, grad_up, grad_mixed, rest_first = stage(grad_gate, grad_up, grad_mixed, rest_first)

    rest_second = scatter_second(halves(rest_part), rest_first)
    gate_part = matmul_tn(normed, grad_gate).astype(BF)
    up_part = matmul_tn(normed, grad_up).astype(BF)
    rest_sum = jnp.concatenate(scatter_last(halves(rest_part), rest_first, rest_second), axis=1)
    gate_part, up_part, rest_sum, grad_mixed = stage(gate_part, up_part, rest_sum, grad_mixed)
    rest_all = gather_ctx(rest_sum)

    pair_first = scatter_first((gate_part, up_part))
    grad_merged = attention_backward(heads, slots, lows, kept, grad_mixed, tables, stream_starts)
    grad_merged, pair_first = stage(grad_merged, pair_first)

    pair_second = scatter_second((gate_part, up_part), pair_first)
    attn_part = matmul_tn(normed, grad_merged).astype(BF)
    pair_sum = jnp.concatenate(
        [p[:, :units] for p in scatter_last((gate_part, up_part), pair_first, pair_second)], axis=1
    )
    attn_part, pair_sum, grad_merged = stage(attn_part, pair_sum, grad_merged)
    pair_all = gather_ctx(pair_sum[None])

    attn_first = scatter_first(halves(attn_part))
    grad_part, terms = input_side(
        grad_gate, grad_up, grad_merged, hidden_all, gate_pieces, up_pieces, attn_pieces
    )
    merged_term = jnp.sum(grad_merged, axis=0, dtype=F32).reshape(3, pieces, 1, head_width)
    merged_term = jnp.where(
        lax.broadcasted_iota(jnp.int32, (3, pieces, parts, head_width), 2) == ctx_at, merged_term, 0.0
    )
    terms = jnp.concatenate([terms.reshape(-1), merged_term.reshape(-1)]).reshape(-1, 128)
    grad_part, terms, attn_first = stage(grad_part, terms, attn_first)

    attn_second = scatter_second(halves(attn_part), attn_first)
    attn_sum = jnp.concatenate(scatter_last(halves(attn_part), attn_first, attn_second), axis=1)
    attn_sum, grad_part, terms = stage(attn_sum, grad_part, terms)

    pair_plan = [
        [
            (c, side * units + p * unit_width, unit_width)
            for p in range(shard_count)
            for c in range(parts)
        ]
        for side in range(2)
    ]
    attn_plan = [
        [
            (c, (s * pieces + p) * head_width, head_width)
            for s in range(3)
            for p in range(pieces)
            for c in range(parts)
        ]
    ]
    places = parts // 2
    attn_got = gather_step(1, [attn_sum, attn_sum])
    attn_held, attn_other = [attn_sum[None]], []
    other_terms = others_of(terms, "fsdp", 1, shard_count)
    part_own, part_other = split_cores(grad_part)
    part_other = flip(part_other, "ctx", 0)
    part_places = (part_own.astype(F32) + part_other.astype(F32)).astype(BF)
    part_ends = [line_block(part_places, 1).astype(BF), line_block(part_places, places - 1).astype(BF)]
    float_in = hidden_in[0].astype(F32)
    output = (float_in + out_rows.astype(F32)).astype(BF)[None]
    (rest_all,) = tie([rest_all], [output])
    rest_blocks = rest_all.reshape(parts, -1, model)
    grad_down_w = rest_blocks[:, :unit_width].reshape(-1, model).astype(F32)
    if spread:
        grad_proj_w = rest_blocks[:, unit_width:].reshape(-1, model).astype(F32)
    else:
        grad_proj_w = lax.dynamic_slice_in_dim(
            gather_ctx(lax.psum(proj_part.astype(F32), "fsdp")), fsdp_at * shard_rows, shard_rows, 0
        )
    terms, others, part_places, part_ends, attn_got, output, grad_down_w, grad_proj_w = stage(
        terms, other_terms[0], part_places, part_ends, attn_got, output, grad_down_w, grad_proj_w
    )
    terms = sum_of(terms, others, other_terms[1])

    waiting = None
    grad_step = None
    for step in range(2, places):
        attn_held += [block[None] for block in attn_got]
        attn_before = attn_got
        attn_got = gather_step(step, attn_got)
        grad_step = line_step(part_places, step - 1, grad_step) if grad_step else line_start(part_ends)
        if waiting is not None:
            attn_other.append(flip(waiting, "ctx", 0))
        waiting = jnp.stack([attn_sum, *attn_before] if step == 2 else attn_before)
        other_terms = flip(terms, "ctx", 0) if step == 2 else terms
        late = []
        if step == 3:
            (pair_all,) = tie([pair_all], [grad_down_w])
            late = list(assemble(pair_all, pair_plan))
        grad_step, attn_got, attn_other, late, part_places, waiting, terms, other_terms = stage(
            grad_step, attn_got, attn_other, late, part_places, waiting, terms, other_terms
        )
        if step == 2:
            terms = terms + other_terms
        if step == 3:
            grad_gate_w, grad_up_w = late
    attn_held += [block[None] for block in attn_got]
    grad_step = line_step(part_places, places - 1, grad_step) if grad_step else line_start(part_ends)
    attn_other.append(flip(waiting, "ctx", 0))
    attn_last = [flip(block[None], "ctx", 0) for block in attn_got]
    sources = [(attn_held[0], 0), (attn_other[0], 0)]
    for step in range(1, places):
        sources += [(attn_held[2 * step - 1], 0), (attn_held[2 * step], 0)]
        first = 1 if step == 1 else 0
        if step < places - 1:
            sources += [(attn_other[step - 1], first), (attn_other[step - 1], first + 1)]
        else:
            sources += [(block, 0) for block in attn_last]
    grad_attn_w = assemble_line(sources, line_origins(), attn_plan[0])
    other_terms = flip(terms, "ctx", 1)
    grad_attn_w, other_terms, grad_step, part_places = stage(grad_attn_w, other_terms, grad_step, part_places)
    terms = terms + other_terms
    for bit in range(2, bits_of(parts)):
        terms = terms + flip(terms, "ctx", bit)
    terms = terms.reshape(-1)
    grad_normed = line_block(part_places, 0) + grad_step[0].astype(F32) + grad_step[1].astype(F32)

    normal_hat, inverse_std = normalise(float_in)
    b_rows = b_qkv.shape[0]
    grad_b_attn = lax.dynamic_slice_in_dim(terms, 2 * model + fsdp_at * b_rows, b_rows, 0)
    grad_gain = lax.dynamic_slice_in_dim(terms, fsdp_at * shard_rows, shard_rows, 0)
    grad_bias = lax.dynamic_slice_in_dim(terms, model + fsdp_at * shard_rows, shard_rows, 0)

    grad_hat = grad_normed * gain_full
    grad_in = out_grad[0].astype(F32) + inverse_std * (
        grad_hat
        - jnp.mean(grad_hat, axis=1, keepdims=True)
        - normal_hat * jnp.mean(grad_hat * normal_hat, axis=1, keepdims=True)
    )
    grad_in = grad_in.astype(BF)[None]
    return (
        output,
        grad_in,
        grad_gain,
        grad_bias,
        grad_attn_w,
        grad_b_attn,
        grad_proj_w,
        grad_gate_w,
        grad_up_w,
        grad_down_w,
    )


def solution(mesh):
    return jax.shard_map(
        shards,
        mesh=mesh,
        in_specs=(
            P("fsdp", "ctx", None),
            P("fsdp", "ctx", None),
            P("fsdp", None),
            P("fsdp", None),
            P("fsdp"),
            P("fsdp"),
            P("fsdp", None),
            P("fsdp"),
            P("fsdp", None),
            P("fsdp", None),
            P("fsdp", None),
            P("fsdp", None),
        ),
        out_specs=(
            P("fsdp", "ctx", None),
            P("fsdp", "ctx", None),
            P("fsdp"),
            P("fsdp"),
            P("fsdp", None),
            P("fsdp"),
            P("fsdp", None),
            P("fsdp", None),
            P("fsdp", None),
            P("fsdp", None),
        ),
        check_vma=False,
    )
```

```python
import functools

import jax
import jax.numpy as jnp
from jax import lax
from jax.experimental import pallas as pl
from jax.experimental.pallas import tpu as pltpu
from jax.sharding import PartitionSpec as P

HD = 64
ROT = 16
BLOCK = 128
CHUNK = 256
BF = jnp.bfloat16
F32 = jnp.float32
MASKED = -1e30


def matmul(left, right):
    return jnp.dot(left, right, preferred_element_type=F32)


def matmul_nt(left, right):
    return lax.dot_general(left, right, (((1,), (1,)), ((), ())), preferred_element_type=F32)


def matmul_tn(left, right):
    return lax.dot_general(left, right, (((0,), (0,)), ((), ())), preferred_element_type=F32)


def flip(values, axis, bit):
    count = lax.axis_size(axis)
    return lax.ppermute(values, axis, [(i, i ^ (1 << bit)) for i in range(count)])


def bits_of(count):
    bits = count.bit_length() - 1
    assert count == 1 << bits
    return bits


def gather_rows(values, axis, order):
    me = lax.axis_index(axis)
    count = lax.axis_size(axis)
    held = values[None]
    steps = [0]
    for bit in order:
        other = flip(held, axis, bit)
        held = jnp.concatenate([held, other], axis=0)
        steps = steps + [s ^ (1 << bit) for s in steps]
    rows = values.shape[0]
    out = jnp.zeros((count * rows,) + values.shape[1:], values.dtype)
    for place, step in enumerate(steps):
        out = lax.dynamic_update_slice_in_dim(out, held[place], (me ^ step) * rows, 0)
    return out


def placed(pieces, places, total):
    out = jnp.zeros((total,) + pieces[0].shape[1:], pieces[0].dtype)
    for piece, place in zip(pieces, places):
        out = lax.dynamic_update_slice_in_dim(out, piece, place, 0)
    return out


def gather_first(values):
    if lax.axis_size("fsdp") != 4:
        return [gather_rows(values, "fsdp", list(range(bits_of(lax.axis_size("fsdp")))))]
    return [flip(values, "fsdp", 0), flip(values, "fsdp", 1)]


def gather_second(values, first):
    if lax.axis_size("fsdp") != 4:
        return []
    half = values.shape[0] // 2 // 16 * 16
    return [flip(first[0][:half], "fsdp", 1), flip(first[1][half:], "fsdp", 0)]


def gathered_pieces(values, first, second, rows):
    count = lax.axis_size("fsdp")
    shard = values.shape[0]
    if count != 4:
        return [(first[0], i * shard, rows, i * rows) for i in range(count)]
    me = lax.axis_index("fsdp")
    half = shard // 2 // 16 * 16
    return [
        (values, 0, rows, me * rows),
        (first[0], 0, rows, (me ^ 1) * rows),
        (first[1], 0, rows, (me ^ 2) * rows),
        (second[0], 0, half, (me ^ 3) * rows),
        (second[1], 0, rows - half, (me ^ 3) * rows + half),
    ]


def gathered_rest(values, first, second, rows):
    count = lax.axis_size("fsdp")
    shard = values.shape[0]
    if count != 4:
        return first[0].reshape(count, shard, -1)[:, rows:]
    me = lax.axis_index("fsdp")
    half = shard // 2 // 16 * 16
    tails = [values[rows:], first[0][rows:], first[1][rows:], second[1][rows - half :]]
    return placed([t[None] for t in tails], [me, me ^ 1, me ^ 2, me ^ 3], count)


def others_of(values, axis, stride, count):
    size = lax.axis_size(axis)
    digit = lax.axis_index(axis) // stride % count

    def moved(i, by):
        at = i // stride % count
        return i + ((at + by) % count - at) * stride

    return [lax.ppermute(values, axis, [(i, moved(i, by)) for i in range(size)]) for by in range(1, count)], digit


def sum_of(values, others, digit):
    count = len(others) + 1
    out = jnp.zeros((count,) + values.shape, values.dtype)
    for by, piece in enumerate([values] + others):
        out = lax.dynamic_update_slice_in_dim(out, piece[None], (digit + count - by) % count, 0)
    total = out[0]
    for at in range(1, count):
        total = total + out[at]
    return total


def scatter_rows(values, axis, order):
    me = lax.axis_index(axis)
    count = lax.axis_size(axis)
    bits = bits_of(count)
    rows = values.shape[0] // count
    held = values.reshape((2,) * bits + (rows,) + values.shape[1:])
    left = list(range(bits))
    for bit in order:
        at = len(left) - 1 - left.index(bit)
        mine = (me >> bit) & 1
        sent = lax.dynamic_index_in_dim(held, 1 - mine, at, keepdims=False).astype(BF)
        kept = lax.dynamic_index_in_dim(held, mine, at, keepdims=False)
        held = kept.astype(F32) + flip(sent, axis, bit).astype(F32)
        left.remove(bit)
    return held


def fsdp_block(part, index):
    rows = part.shape[0] // lax.axis_size("fsdp")
    return lax.dynamic_slice_in_dim(part, index * rows, rows, 0)


def halves(part):
    half = part.shape[1] // 2 // 128 * 128
    return part[:, :half], part[:, half:]


def scatter_first(sides):
    if lax.axis_size("fsdp") != 4:
        return [scatter_rows(part, "fsdp", list(range(bits_of(lax.axis_size("fsdp"))))) for part in sides]
    me = lax.axis_index("fsdp")
    return [
        flip(jnp.stack([fsdp_block(sides[1], me ^ 3), fsdp_block(sides[1], me ^ 1)]), "fsdp", 0),
        flip(jnp.stack([fsdp_block(sides[0], me ^ 3), fsdp_block(sides[0], me ^ 2)]), "fsdp", 1),
    ]


def scatter_second(sides, first):
    if lax.axis_size("fsdp") != 4:
        return []
    me = lax.axis_index("fsdp")
    across = fsdp_block(sides[0], me ^ 1).astype(F32) + first[1][0].astype(F32)
    along = fsdp_block(sides[1], me ^ 2).astype(F32) + first[0][0].astype(F32)
    return [flip(across.astype(BF), "fsdp", 0), flip(along.astype(BF), "fsdp", 1)]


def scatter_last(sides, first, second):
    if lax.axis_size("fsdp") != 4:
        return first[0].astype(BF), first[1].astype(BF)
    me = lax.axis_index("fsdp")
    left = fsdp_block(sides[0], me).astype(F32) + first[1][1].astype(F32) + second[0].astype(F32)
    right = fsdp_block(sides[1], me).astype(F32) + first[0][1].astype(F32) + second[1].astype(F32)
    return left.astype(BF), right.astype(BF)


def gather_ctx(values):
    return lax.all_gather(values, "ctx", axis=0, tiled=True)


def split_cores(part):
    parts = lax.axis_size("ctx")
    core = lax.axis_index("ctx") % 2
    blocks = part.reshape(parts // 2, 2, part.shape[0] // parts, part.shape[1])
    return [lax.dynamic_index_in_dim(blocks, k, 1, keepdims=False) for k in (core, 1 - core)]


def scatter_ctx(values):
    return lax.psum_scatter(values, "ctx", scatter_dimension=0, tiled=True)


def shift(values, by, keep):
    places = lax.axis_size("ctx") // 2
    pairs = [
        (2 * p + k, 2 * (p + by) + k) for p in range(places) for k in range(2) if keep(p) and 0 <= p + by < places
    ]
    return lax.ppermute(values, "ctx", pairs)


def line_block(blocks, s):
    places = blocks.shape[0]
    at = (lax.axis_index("ctx") // 2 + places - s) % places
    return lax.dynamic_index_in_dim(blocks, at, 0, keepdims=False).astype(F32)


def line_start(ends):
    last = lax.axis_size("ctx") // 2 - 1
    return [shift(ends[0], 1, lambda p: p <= 0), shift(ends[1], -1, lambda p: p >= last)]


def line_step(blocks, step, before):
    places = blocks.shape[0]
    up, down = line_block(blocks, step), line_block(blocks, places - step)
    if before:
        up, down = up + before[0].astype(F32), down + before[1].astype(F32)
    return [
        shift(up.astype(BF), 1, lambda p: p <= step - 1),
        shift(down.astype(BF), -1, lambda p: p >= places - step),
    ]


def gather_step(step, before):
    places = lax.axis_size("ctx") // 2
    return [
        shift(before[0], 1, lambda p: p >= step - 1),
        shift(before[1], -1, lambda p: p <= places - step),
    ]


def line_origins():
    me = lax.axis_index("ctx")
    places = lax.axis_size("ctx") // 2
    at, core = me // 2, me % 2
    out = [me, me ^ 1]
    for s in range(1, places):
        ends = (jnp.where(at >= s, at - s, -1), jnp.where(at + s < places, at + s, -1))
        for j in range(2):
            out += [jnp.where(p < 0, -1, 2 * p + (core ^ j)) for p in ends]
    return jnp.stack(out).astype(jnp.int32)


def nothing_kernel(*refs):
    return None


def tie(values, after):
    anywhere = pl.BlockSpec(memory_space=pl.ANY)
    return pl.pallas_call(
        nothing_kernel,
        out_shape=tuple(jax.ShapeDtypeStruct(v.shape, v.dtype) for v in values),
        in_specs=[anywhere] * (len(values) + len(after)),
        out_specs=tuple([anywhere] * len(values)),
        input_output_aliases={i: i for i in range(len(values))},
        name="tie",
    )(*values, *after)


def stage(*groups):
    leaves, tree = jax.tree.flatten(groups)
    return jax.tree.unflatten(tree, tie(leaves, []))


def rows_at(index, size):
    return pl.ds(pl.multiple_of(index * size, size), size)


def turn(values, tables, rows, direction):
    width = values.shape[1]
    cosine, lead, tail = (jnp.concatenate([ref[rows, :]] * (width // 128), axis=1) for ref in tables)
    ahead = pltpu.roll(values, width - ROT // 2, 1)
    behind = pltpu.roll(values, ROT // 2, 1)
    return values * cosine + direction * (ahead * lead + behind * tail)


def split_heads(target, values, heads):
    head_of = lax.broadcasted_iota(jnp.int32, values.shape, 1) // HD
    for h in range(heads):
        target[h * CHUNK : (h + 1) * CHUNK, :] = jnp.where(head_of == h, values, jnp.zeros_like(values))


def visible(i, j, begin):
    key_at = lax.broadcasted_iota(jnp.int32, (CHUNK, CHUNK), 0)
    query_at = lax.broadcasted_iota(jnp.int32, (CHUNK, CHUNK), 1)
    return (key_at - query_at <= (i - j) * CHUNK) & (key_at >= begin - j * CHUNK)


def forward_kernel(
    heads,
    slot_ref,
    low_ref,
    merged_ref,
    cos_ref,
    lead_ref,
    tail_ref,
    begin_ref,
    mixed_ref,
    q_ref,
    k_ref,
    v_ref,
    total_ref,
    ot_ref,
    vt_ref,
    qm_ref,
    s_ref,
):
    width = heads * HD
    tokens = merged_ref.shape[0]
    tables = (cos_ref, lead_ref, tail_ref)

    def prepare(block, carry):
        source = rows_at(slot_ref[block], BLOCK)
        target = rows_at(block, BLOCK)
        query = turn(merged_ref[source, 0:width], tables, source, 1.0).astype(BF)
        key = turn(merged_ref[source, width : 2 * width], tables, source, 1.0).astype(BF)
        value = merged_ref[source, 2 * width : 3 * width].astype(BF)
        q_ref[target, :] = query * jnp.asarray(HD ** (-0.5), BF)
        k_ref[target, :] = key
        v_ref[target, :] = value
        vt_ref[:, target] = value.T
        return carry

    lax.fori_loop(0, tokens // BLOCK, prepare, 0)

    def query_chunk(i, carry):
        here = rows_at(i, CHUNK)
        split_heads(qm_ref, q_ref[here, :], heads)
        ot_ref[:, here] = jnp.zeros((width, CHUNK), F32)
        low = low_ref[i]
        begin = begin_ref[i]

        def score(j, tops):
            there = rows_at(j, CHUNK)
            key = k_ref[there, :]
            allowed = visible(i, j, begin)
            out = []
            for h in range(heads):
                s = matmul_nt(key, qm_ref[h * CHUNK : (h + 1) * CHUNK, :])
                s = jnp.where(allowed, s, MASKED)
                s_ref[h, there, :] = s
                out.append(jnp.maximum(tops[h], jnp.max(s, axis=0, keepdims=True)))
            return tuple(out)

        tops = lax.fori_loop(
            low, i + 1, score, tuple(jnp.full((1, CHUNK), MASKED, F32) for _ in range(heads))
        )

        def value_side(j, sums):
            there = rows_at(j, CHUNK)
            out = []
            for h in range(heads):
                span = slice(h * HD, (h + 1) * HD)
                e = jnp.exp(s_ref[h, there, :] - tops[h])
                out.append(sums[h] + jnp.sum(e, axis=0, keepdims=True))
                ot_ref[span, here] += matmul(vt_ref[span, there], e.astype(BF))
            return tuple(out)

        sums = lax.fori_loop(low, i + 1, value_side, tuple(jnp.zeros((1, CHUNK), F32) for _ in range(heads)))
        for h in range(heads):
            span = slice(h * HD, (h + 1) * HD)
            ot_ref[span, here] = ot_ref[span, here] * (1.0 / sums[h])
            total_ref[i, h : h + 1, :] = tops[h] + jnp.log(sums[h])
        mixed = ot_ref[:, here].T.astype(BF)
        for part in range(CHUNK // BLOCK):
            target = rows_at(slot_ref[i * (CHUNK // BLOCK) + part], BLOCK)
            mixed_ref[target, :] = mixed[part * BLOCK : (part + 1) * BLOCK]
        return carry

    lax.fori_loop(0, tokens // CHUNK, query_chunk, 0)


def backward_kernel(
    heads,
    slot_ref,
    low_ref,
    q_ref,
    k_ref,
    v_ref,
    total_ref,
    ot_ref,
    grad_mixed_ref,
    cos_ref,
    lead_ref,
    tail_ref,
    begin_ref,
    grad_merged_ref,
    kt_ref,
    qm_ref,
    gm_ref,
    p_ref,
    ds_ref,
    dqt_ref,
    dk_ref,
    dv_ref,
):
    width = heads * HD
    tokens = q_ref.shape[0]
    tables = (cos_ref, lead_ref, tail_ref)

    def prepare(block, carry):
        here = rows_at(block, BLOCK)
        kt_ref[:, here] = k_ref[here, :].T
        dk_ref[here, :] = jnp.zeros((BLOCK, width), F32)
        dv_ref[here, :] = jnp.zeros((BLOCK, width), F32)
        return carry

    lax.fori_loop(0, tokens // BLOCK, prepare, 0)

    def query_chunk(i, carry):
        here = rows_at(i, CHUNK)
        targets = [rows_at(slot_ref[i * (CHUNK // BLOCK) + part], BLOCK) for part in range(CHUNK // BLOCK)]
        grad = jnp.concatenate([grad_mixed_ref[target, :] for target in targets], axis=0)
        split_heads(qm_ref, q_ref[here, :], heads)
        split_heads(gm_ref, grad, heads)
        dqt_ref[...] = jnp.zeros_like(dqt_ref)
        product = grad.T.astype(F32) * ot_ref[:, here]
        dots = [jnp.sum(product[h * HD : (h + 1) * HD], axis=0, keepdims=True) for h in range(heads)]
        totals = [total_ref[i, h : h + 1, :] for h in range(heads)]
        begin = begin_ref[i]

        def key_chunk(j, carry):
            there = rows_at(j, CHUNK)
            key = k_ref[there, :]
            value = v_ref[there, :]
            allowed = visible(i, j, begin)
            for h in range(heads):
                span = slice(h * HD, (h + 1) * HD)
                part = slice(h * CHUNK, (h + 1) * CHUNK)
                s = matmul_nt(key, qm_ref[part, :])
                probs = jnp.exp(jnp.where(allowed, s, MASKED) - totals[h])
                p_ref[:, part] = probs.astype(BF)
                ds = (probs * (matmul_nt(value, gm_ref[part, :]) - dots[h])).astype(BF)
                ds_ref[:, part] = ds
                dqt_ref[span, :] += matmul(kt_ref[span, there], ds)
            dv_ref[there, :] += matmul(p_ref[...], gm_ref[...])
            dk_ref[there, :] += matmul(ds_ref[...], qm_ref[...])
            return carry

        lax.fori_loop(low_ref[i], i + 1, key_chunk, 0)
        grad_query = dqt_ref[...].T * HD ** (-0.5)
        for part, target in enumerate(targets):
            rows = slice(part * BLOCK, (part + 1) * BLOCK)
            grad_merged_ref[target, 0:width] = turn(grad_query[rows], tables, target, -1.0).astype(BF)
        return carry

    lax.fori_loop(0, tokens // CHUNK, query_chunk, 0)

    def finish(block, carry):
        source = rows_at(block, BLOCK)
        target = rows_at(slot_ref[block], BLOCK)
        grad_merged_ref[target, width : 2 * width] = turn(dk_ref[source, :], tables, target, -1.0).astype(BF)
        grad_merged_ref[target, 2 * width : 3 * width] = dv_ref[source, :].astype(BF)
        return carry

    lax.fori_loop(0, tokens // BLOCK, finish, 0)


WHOLE = pl.BlockSpec(memory_space=pltpu.VMEM)
SCALAR = pl.BlockSpec(memory_space=pltpu.SMEM)
ANYWHERE = pl.BlockSpec(memory_space=pl.ANY)


def attention_forward(heads, slots, lows, merged, tables, begins):
    tokens = merged.shape[0]
    width = heads * HD
    rows = jax.ShapeDtypeStruct((tokens, width), BF)
    return pl.pallas_call(
        functools.partial(forward_kernel, heads),
        out_shape=(
            rows,
            rows,
            rows,
            rows,
            jax.ShapeDtypeStruct((tokens // CHUNK, heads, CHUNK), F32),
            jax.ShapeDtypeStruct((width, tokens), F32),
        ),
        in_specs=[SCALAR, SCALAR] + [WHOLE] * 5,
        out_specs=(WHOLE,) * 6,
        scratch_shapes=[
            pltpu.VMEM((width, tokens), BF),
            pltpu.VMEM((heads * CHUNK, width), BF),
            pltpu.VMEM((heads, tokens, CHUNK), F32),
        ],
        compiler_params=pltpu.CompilerParams(vmem_limit_bytes=48 * 1024 * 1024),
        cost_estimate=pl.CostEstimate(flops=25_000_000_000, transcendentals=0, bytes_accessed=0),
        name="attention_forward",
    )(slots, lows, merged, *tables, begins)


def attention_backward(heads, slots, lows, kept, grad_mixed, tables, begins):
    tokens, width = grad_mixed.shape
    return pl.pallas_call(
        functools.partial(backward_kernel, heads),
        out_shape=jax.ShapeDtypeStruct((tokens, 3 * width), BF),
        in_specs=[SCALAR, SCALAR] + [WHOLE] * 10,
        out_specs=WHOLE,
        scratch_shapes=[
            pltpu.VMEM((width, tokens), BF),
            pltpu.VMEM((heads * CHUNK, width), BF),
            pltpu.VMEM((heads * CHUNK, width), BF),
            pltpu.VMEM((CHUNK, heads * CHUNK), BF),
            pltpu.VMEM((CHUNK, heads * CHUNK), BF),
            pltpu.VMEM((width, CHUNK), F32),
            pltpu.VMEM((tokens, width), F32),
            pltpu.VMEM((tokens, width), F32),
        ],
        compiler_params=pltpu.CompilerParams(vmem_limit_bytes=48 * 1024 * 1024),
        cost_estimate=pl.CostEstimate(flops=40_000_000_000, transcendentals=0, bytes_accessed=0),
        name="attention_backward",
    )(slots, lows, *kept, grad_mixed, *tables, begins)


def fetch(at_ref, pieces, spans, target, sem):
    copies = []
    for n, (piece, (first, rows)) in enumerate(zip(pieces, spans)):
        place = pl.ds(pl.multiple_of(at_ref[n], 16), rows)
        copies.append(pltpu.make_async_copy(piece.at[pl.ds(first, rows), :], target.at[place, :], sem.at[n]))
    for copy in copies:
        copy.start()
    return copies


def attn_kernel(spans, at_ref, hidden_ref, gain_ref, bias_ref, shift_ref, *refs):
    n = len(spans)
    normed_ref, merged_ref, w_attn, sem = refs[n:]

    @pl.when(pl.program_id(0) == 0)
    def _():
        for copy in fetch(at_ref, refs[:n], spans, w_attn, sem):
            copy.wait()

    normal, _ = normalise(hidden_ref[...].astype(F32))
    normed = (normal * gain_ref[...] + bias_ref[...]).astype(BF)
    normed_ref[...] = normed
    merged_ref[...] = matmul(normed, w_attn[...]) + shift_ref[...]


def pair_kernel(spans, at_ref, normed_ref, *refs):
    n = len(spans)
    gate_pieces, up_pieces = refs[:n], refs[n : 2 * n]
    act_ref, slope_ref, silu_ref, w_gate, w_up, *sems = refs[2 * n :]

    @pl.when(pl.program_id(0) == 0)
    def _():
        copies = fetch(at_ref, gate_pieces, spans, w_gate, sems[0])
        copies += fetch(at_ref, up_pieces, spans, w_up, sems[1])
        for copy in copies:
            copy.wait()

    normed = normed_ref[...]
    gating = matmul(normed, w_gate[...])
    rising = matmul(normed, w_up[...])
    sigma = jax.nn.sigmoid(gating)
    silu = gating * sigma
    act_ref[...] = (silu * rising).astype(BF)
    slope_ref[...] = (rising * sigma * (1.0 + gating * (1.0 - sigma))).astype(BF)
    silu_ref[...] = silu.astype(BF)


def row_block(width):
    return pl.BlockSpec((CHUNK, width), lambda i: (i, 0))


def full_block(array):
    return pl.BlockSpec(array.shape, lambda i: (0, 0))


def split_pieces(pieces):
    at = jnp.stack([jnp.asarray(piece[3], jnp.int32) for piece in pieces])
    return at, [piece[0] for piece in pieces], tuple((piece[1], piece[2]) for piece in pieces)


def attn_side(hidden, gain, bias, shift, pieces):
    tokens, model = hidden.shape
    at, arrays, spans = split_pieces(pieces)
    n = len(spans)
    width = arrays[0].shape[1]
    return pl.pallas_call(
        functools.partial(attn_kernel, spans),
        grid=(tokens // CHUNK,),
        out_shape=(jax.ShapeDtypeStruct((tokens, model), BF), jax.ShapeDtypeStruct((tokens, width), F32)),
        in_specs=[SCALAR, row_block(model), full_block(gain), full_block(bias), full_block(shift)] + [ANYWHERE] * n,
        out_specs=(row_block(model), row_block(width)),
        scratch_shapes=[pltpu.VMEM((model, width), BF), pltpu.SemaphoreType.DMA((n,))],
        compiler_params=pltpu.CompilerParams(vmem_limit_bytes=56 * 1024 * 1024),
        cost_estimate=pl.CostEstimate(flops=18_000_000_000, transcendentals=0, bytes_accessed=0),
        name="attn_side",
    )(at, hidden, gain, bias, shift, *arrays)


def pair_side(normed, gate_pieces, up_pieces):
    tokens, model = normed.shape
    at, gates, spans = split_pieces(gate_pieces)
    ups = split_pieces(up_pieces)[1]
    n = len(spans)
    units = gates[0].shape[1]
    return pl.pallas_call(
        functools.partial(pair_kernel, spans),
        grid=(tokens // CHUNK,),
        out_shape=(jax.ShapeDtypeStruct((tokens, units), BF),) * 3,
        in_specs=[SCALAR, row_block(model)] + [ANYWHERE] * (2 * n),
        out_specs=(row_block(units),) * 3,
        scratch_shapes=[
            pltpu.VMEM((model, units), BF),
            pltpu.VMEM((model, units), BF),
            pltpu.SemaphoreType.DMA((n,)),
            pltpu.SemaphoreType.DMA((n,)),
        ],
        compiler_params=pltpu.CompilerParams(vmem_limit_bytes=56 * 1024 * 1024),
        cost_estimate=pl.CostEstimate(flops=28_000_000_000, transcendentals=0, bytes_accessed=0),
        name="pair_side",
    )(at, normed, *gates, *ups)


def fetch_rest(spans, at_ref, refs, lower, proj, sems):
    n = len(spans) // 2
    units = lower.shape[0]
    filled = sum(rows for _, rows in spans[:n])
    if filled < units:
        lower[filled:, :] = jnp.zeros((units - filled, lower.shape[1]), BF)
    copies = fetch(at_ref.at[0], refs[:n], spans[:n], lower, sems[0])
    copies += fetch(at_ref.at[1], refs[n:], spans[n:], proj, sems[1])
    for copy in copies:
        copy.wait()


def grad_kernel(spans, at_ref, grad_ref, slope_ref, silu_ref, *refs):
    n = len(spans)
    gate_ref, up_ref, mixed_ref, lower, proj, *sems = refs[n:]

    @pl.when(pl.program_id(0) == 0)
    def _():
        fetch_rest(spans, at_ref, refs[:n], lower, proj, sems)

    grad = grad_ref[...]
    act = matmul_nt(grad, lower[...])
    mixed_ref[...] = matmul_nt(grad, proj[...]).astype(BF)
    gate_ref[...] = (act * slope_ref[...].astype(F32)).astype(BF)
    up_ref[...] = (act * silu_ref[...].astype(F32)).astype(BF)


def rest_scratch(units, width, model, n):
    return [
        pltpu.VMEM((units, model), BF),
        pltpu.VMEM((width, model), BF),
        pltpu.SemaphoreType.DMA((n,)),
        pltpu.SemaphoreType.DMA((n,)),
    ]


def split_rest(lower_pieces, proj_pieces):
    lower_at, lowers, lower_spans = split_pieces(lower_pieces)
    proj_at, projs, proj_spans = split_pieces(proj_pieces)
    return jnp.stack([lower_at, proj_at]), lowers + projs, lower_spans + proj_spans


def grad_side(grad, slope, silu, width, lower_pieces, proj_pieces):
    tokens, model = grad.shape
    units = slope.shape[1]
    at, arrays, spans = split_rest(lower_pieces, proj_pieces)
    return pl.pallas_call(
        functools.partial(grad_kernel, spans),
        grid=(tokens // CHUNK,),
        out_shape=(
            jax.ShapeDtypeStruct((tokens, units), BF),
            jax.ShapeDtypeStruct((tokens, units), BF),
            jax.ShapeDtypeStruct((tokens, width), BF),
        ),
        in_specs=[SCALAR, row_block(model), row_block(units), row_block(units)] + [ANYWHERE] * len(arrays),
        out_specs=(row_block(units), row_block(units), row_block(width)),
        scratch_shapes=rest_scratch(units, width, model, len(arrays) // 2),
        compiler_params=pltpu.CompilerParams(vmem_limit_bytes=56 * 1024 * 1024),
        cost_estimate=pl.CostEstimate(flops=18_000_000_000, transcendentals=0, bytes_accessed=0),
        name="grad_side",
    )(at, grad, slope, silu, *arrays)


def out_kernel(spans, at_ref, mixed_ref, act_ref, *refs):
    n = len(spans)
    out_ref, lower, proj, *sems = refs[n:]

    @pl.when(pl.program_id(0) == 0)
    def _():
        fetch_rest(spans, at_ref, refs[:n], lower, proj, sems)

    out_ref[...] = (matmul(mixed_ref[...], proj[...]) + matmul(act_ref[...], lower[...])).astype(BF)


def out_side(mixed, act, model, lower_pieces, proj_pieces):
    tokens, width = mixed.shape
    units = act.shape[1]
    at, arrays, spans = split_rest(lower_pieces, proj_pieces)
    return pl.pallas_call(
        functools.partial(out_kernel, spans),
        grid=(tokens // CHUNK,),
        out_shape=jax.ShapeDtypeStruct((tokens, model), BF),
        in_specs=[SCALAR, row_block(width), row_block(units)] + [ANYWHERE] * len(arrays),
        out_specs=row_block(model),
        scratch_shapes=rest_scratch(units, width, model, len(arrays) // 2),
        compiler_params=pltpu.CompilerParams(vmem_limit_bytes=56 * 1024 * 1024),
        cost_estimate=pl.CostEstimate(flops=15_000_000_000, transcendentals=0, bytes_accessed=0),
        name="out_side",
    )(at, mixed, act, *arrays)


def input_kernel(spans, at_ref, gate_ref, up_ref, merged_ref, hidden_ref, *refs):
    n = len(spans)
    gate_pieces, up_pieces, attn_pieces = refs[:n], refs[n : 2 * n], refs[2 * n : 3 * n]
    part_ref, terms_ref, w_gate, w_up, w_attn, *sems = refs[3 * n :]

    @pl.when(pl.program_id(0) == 0)
    def _():
        copies = fetch(at_ref, gate_pieces, spans, w_gate, sems[0])
        copies += fetch(at_ref, up_pieces, spans, w_up, sems[1])
        copies += fetch(at_ref, attn_pieces, spans, w_attn, sems[2])
        terms_ref[...] = jnp.zeros_like(terms_ref)
        for copy in copies:
            copy.wait()

    part = matmul_nt(gate_ref[...], w_gate[...]) + matmul_nt(up_ref[...], w_up[...])
    part = part + matmul_nt(merged_ref[...], w_attn[...])
    part_ref[...] = part.astype(BF)
    normal, _ = normalise(hidden_ref[...].astype(F32))
    terms_ref[0:1, :] += jnp.sum(part * normal, axis=0, keepdims=True)
    terms_ref[1:2, :] += jnp.sum(part, axis=0, keepdims=True)


def input_side(grad_gate, grad_up, grad_merged, hidden, gate_pieces, up_pieces, attn_pieces):
    tokens, model = hidden.shape
    at, gates, spans = split_pieces(gate_pieces)
    ups, attns = split_pieces(up_pieces)[1], split_pieces(attn_pieces)[1]
    n = len(spans)
    units, width = grad_gate.shape[1], grad_merged.shape[1]
    return pl.pallas_call(
        functools.partial(input_kernel, spans),
        grid=(tokens // CHUNK,),
        out_shape=(jax.ShapeDtypeStruct((tokens, model), BF), jax.ShapeDtypeStruct((2, model), F32)),
        in_specs=[SCALAR, row_block(units), row_block(units), row_block(width), row_block(model)]
        + [ANYWHERE] * (3 * n),
        out_specs=(row_block(model), pl.BlockSpec((2, model), lambda i: (0, 0))),
        scratch_shapes=[
            pltpu.VMEM((model, units), BF),
            pltpu.VMEM((model, units), BF),
            pltpu.VMEM((model, width), BF),
            pltpu.SemaphoreType.DMA((n,)),
            pltpu.SemaphoreType.DMA((n,)),
            pltpu.SemaphoreType.DMA((n,)),
        ],
        compiler_params=pltpu.CompilerParams(vmem_limit_bytes=56 * 1024 * 1024),
        cost_estimate=pl.CostEstimate(flops=30_000_000_000, transcendentals=0, bytes_accessed=0),
        name="input_side",
    )(at, grad_gate, grad_up, grad_merged, hidden, *gates, *ups, *attns)


def assemble_kernel(plan, source_ref, *targets):
    for target, pieces in zip(targets, plan):
        at = 0
        for part, offset, width in pieces:
            target[:, at : at + width] = source_ref[part, :, offset : offset + width].astype(F32)
            at += width


def assemble(gathered, plan):
    parts, rows, columns = gathered.shape
    step = 64
    widths = [sum(piece[2] for piece in pieces) for pieces in plan]
    return pl.pallas_call(
        functools.partial(assemble_kernel, plan),
        grid=(rows // step,),
        out_shape=tuple(jax.ShapeDtypeStruct((rows, w), F32) for w in widths),
        in_specs=[pl.BlockSpec((parts, step, columns), lambda i: (0, i, 0))],
        out_specs=tuple(pl.BlockSpec((step, w), lambda i: (i, 0)) for w in widths),
        compiler_params=pltpu.CompilerParams(vmem_limit_bytes=40 * 1024 * 1024),
        name="assemble",
    )(gathered)


def assemble_line_kernel(plan, count, at_ref, *refs):
    target, held = refs[count], refs[count + 1]
    for n in range(count):

        @pl.when(at_ref[n] >= 0)
        def _():
            held[jnp.maximum(at_ref[n], 0)] = refs[n][0]

    at = 0
    for part, offset, width in plan:
        target[:, at : at + width] = held[part, :, offset : offset + width].astype(F32)
        at += width


def assemble_line(sources, origins, plan):
    parts = lax.axis_size("ctx")
    rows, columns = sources[0][0].shape[1:]
    step = 64
    width = sum(piece[2] for piece in plan)

    def block(n, index):
        return pl.BlockSpec((1, step, columns), lambda i, at: (index, jnp.where(at[n] >= 0, i, 0), 0))

    return pl.pallas_call(
        functools.partial(assemble_line_kernel, plan, len(sources)),
        out_shape=jax.ShapeDtypeStruct((rows, width), F32),
        grid_spec=pltpu.PrefetchScalarGridSpec(
            num_scalar_prefetch=1,
            grid=(rows // step,),
            in_specs=[block(n, index) for n, (_, index) in enumerate(sources)],
            out_specs=pl.BlockSpec((step, width), lambda i, at: (i, 0)),
            scratch_shapes=[pltpu.VMEM((parts, step, columns), BF)],
        ),
        compiler_params=pltpu.CompilerParams(vmem_limit_bytes=40 * 1024 * 1024),
        name="assemble_line",
    )(origins, *[array for array, _ in sources])


def stream_places(order_row, length_row):
    places = (order_row[:, None] * BLOCK + jnp.arange(BLOCK, dtype=jnp.int32)[None, :]).reshape(-1)
    return places, stream_begins(places, length_row)


def stream_begins(places, length_row):
    ends = jnp.cumsum(length_row)
    starts = ends - length_row
    return jnp.max(jnp.where(starts[None, :] <= places[:, None], starts[None, :], 0), axis=1)


def rotary_tables(places, begins):
    entry = jnp.arange(128) % HD
    turned = entry < ROT
    index = jnp.where(entry < ROT // 2, entry, entry - ROT // 2)
    inverse = 1.0 / 10000.0 ** ((2 * index).astype(F32) / ROT)
    angles = (places - begins).astype(F32)[:, None] * jnp.where(turned, inverse, 0.0)[None, :]
    cosine, sine = jnp.cos(angles), jnp.sin(angles)
    lead = jnp.where((entry < ROT // 2)[None, :], -sine, 0.0)
    tail = jnp.where((turned & (entry >= ROT // 2))[None, :], sine, 0.0)
    return cosine, lead, tail


def take_columns(array, starts, width):
    return [lax.dynamic_slice_in_dim(array, s, width, 1) for s in starts]


def normalise(rows):
    centre = jnp.mean(rows, axis=1, keepdims=True)
    deviation = rows - centre
    inverse_std = lax.rsqrt(jnp.mean(deviation * deviation, axis=1, keepdims=True) + 1e-05)
    return deviation * inverse_std, inverse_std


def shards(
    hidden_in,
    out_grad,
    lengths,
    block_order,
    ln_gain,
    ln_bias,
    w_qkv,
    b_qkv,
    w_out,
    w_gate,
    w_up,
    w_down,
):
    parts = lax.axis_size("ctx")
    shard_count = lax.axis_size("fsdp")
    ctx_at = lax.axis_index("ctx")
    fsdp_at = lax.axis_index("fsdp")
    rows = hidden_in.shape[1]
    model = w_out.shape[1]
    hidden = w_gate.shape[1]
    tokens = rows * parts
    heads = model // HD // parts
    width = heads * HD
    shard_rows = w_qkv.shape[0]

    hidden_all = gather_ctx(hidden_in[0])
    grad_all = gather_ctx(out_grad[0])

    spread = (model // HD) % (shard_count * parts) == 0
    pieces = shard_count if spread else 1
    head_span = model // pieces
    head_width = head_span // parts
    head_starts = [
        s * model + p * head_span + ctx_at * head_width for s in range(3) for p in range(pieces)
    ]
    unit_span = hidden // shard_count
    unit_width = unit_span // parts
    unit_starts = [p * unit_span + ctx_at * unit_width for p in range(shard_count)]

    units = shard_count * unit_width
    spare = -units % 128
    empty = jnp.zeros((shard_rows, spare), BF)
    vectors = jnp.concatenate([ln_gain, ln_bias, b_qkv])
    vector_rows = -(-vectors.shape[0] // (3 * width)) + 15
    vector_rows = vector_rows // 16 * 16
    vectors = jnp.pad(vectors, (0, vector_rows * 3 * width - vectors.shape[0])).reshape(vector_rows, 3 * width)
    w_attn_own = jnp.concatenate(take_columns(w_qkv, head_starts, head_width), axis=1)
    w_attn_own = jnp.concatenate([w_attn_own, vectors], axis=0)
    attn_near = gather_first(w_attn_own)
    w_gate_own = jnp.concatenate(take_columns(w_gate, unit_starts, unit_width) + [empty], axis=1)
    gate_near = gather_first(w_gate_own)
    w_up_own = jnp.concatenate(take_columns(w_up, unit_starts, unit_width) + [empty], axis=1)
    attn_near, w_up_own = stage(attn_near, w_up_own)
    attn_far = gather_second(w_attn_own, attn_near)
    up_near = gather_first(w_up_own)
    gate_near, attn_far = stage(gate_near, attn_far)
    gate_far = gather_second(w_gate_own, gate_near)
    w_down_own = lax.dynamic_slice_in_dim(w_down, ctx_at * unit_width, unit_width, 0)
    if spread:
        w_out_own = lax.dynamic_slice_in_dim(w_out, ctx_at * head_width, head_width, 0)
        w_rest_own = jnp.concatenate([w_down_own, w_out_own], axis=0)
    else:
        w_rest_own = w_down_own
    attn_pieces = gathered_pieces(w_attn_own, attn_near, attn_far, shard_rows)
    vectors = gathered_rest(w_attn_own, attn_near, attn_far, shard_rows).reshape(shard_count, -1)
    gain_full = vectors[:, :shard_rows].reshape(-1).astype(F32)
    bias_full = vectors[:, shard_rows : 2 * shard_rows].reshape(-1).astype(F32)
    b_attn = vectors[:, 2 * shard_rows : 2 * shard_rows + b_qkv.shape[0]].reshape(-1).astype(F32)
    b_attn_own = jnp.concatenate([lax.dynamic_slice_in_dim(b_attn, s, head_width, 0) for s in head_starts])

    order_row = block_order[0]
    blocks = order_row.shape[0]
    places, begins = stream_places(order_row, lengths[0])
    tables = rotary_tables(places, begins)
    slots = jnp.sum(
        jnp.where(
            order_row[None, :] == jnp.arange(blocks, dtype=jnp.int32)[:, None],
            jnp.arange(blocks, dtype=jnp.int32)[None, :],
            0,
        ),
        axis=1,
    ).astype(jnp.int32)
    stream_starts = stream_begins(jnp.arange(tokens, dtype=jnp.int32), lengths[0]).astype(jnp.int32)
    lows = stream_starts[::CHUNK] // CHUNK
    stream_starts = stream_starts.reshape(tokens // CHUNK, 1, CHUNK)

    up_near, gate_far, w_rest_own = stage(up_near, gate_far, w_rest_own)
    up_far = gather_second(w_up_own, up_near)
    rest_near = gather_first(w_rest_own)
    normed, merged = attn_side(hidden_all, gain_full[None], bias_full[None], b_attn_own[None], attn_pieces)
    mixed, *kept = attention_forward(heads, slots, lows, merged, tables, stream_starts)
    mixed, up_far, rest_near = stage(mixed, up_far, rest_near)
    rest_far = gather_second(w_rest_own, rest_near)
    gate_pieces = gathered_pieces(w_gate_own, gate_near, gate_far, shard_rows)
    up_pieces = gathered_pieces(w_up_own, up_near, up_far, shard_rows)
    act, slope, silu = pair_side(normed, gate_pieces, up_pieces)
    if spread and shard_count == 4:
        me = lax.axis_index("fsdp")
        corner = jnp.concatenate(rest_far, axis=0)
        held = list(zip([w_rest_own, rest_near[0], rest_near[1], corner], [me, me ^ 1, me ^ 2, me ^ 3]))
        lower_pieces = [(array, 0, unit_width, at * unit_width) for array, at in held]
        proj_pieces = [(array, unit_width, head_width, at * head_width) for array, at in held]
    else:
        w_rest = rest_near[0].reshape(shard_count, -1, model)
        w_lower = jnp.pad(w_rest[:, :unit_width].reshape(units, model), ((0, spare), (0, 0)))
        if spread:
            w_proj = w_rest[:, unit_width:].reshape(width, model)
        else:
            w_proj = lax.dynamic_slice_in_dim(
                lax.all_gather(w_out, "fsdp", axis=0, tiled=True), ctx_at * width, width, 0
            )
        lower_pieces = [(w_lower, 0, units + spare, 0)]
        proj_pieces = [(w_proj, 0, width, 0)]
    out_part = out_side(mixed, act, model, lower_pieces, proj_pieces)
    out_rows = scatter_ctx(out_part)

    (grad_all,) = tie([grad_all], [out_part])
    down_part = matmul_tn(act, grad_all).astype(BF)
    proj_part = matmul_tn(mixed, grad_all).astype(BF)
    if spread:
        rest_part = jnp.concatenate(
            [p.reshape(shard_count, -1, model) for p in (down_part[:units], proj_part)], axis=1
        ).reshape(-1, model)
    else:
        rest_part = down_part[:units]
    rest_part, grad_all = stage(rest_part, grad_all)
    rest_first = scatter_first(halves(rest_part))
    grad_gate, grad_up, grad_mixed = grad_side(grad_all, slope, silu, width, lower_pieces, proj_pieces)
    grad_gate, grad_up, grad_mixed, rest_first = stage(grad_gate, grad_up, grad_mixed, rest_first)

    rest_second = scatter_second(halves(rest_part), rest_first)
    gate_part = matmul_tn(normed, grad_gate).astype(BF)
    up_part = matmul_tn(normed, grad_up).astype(BF)
    rest_sum = jnp.concatenate(scatter_last(halves(rest_part), rest_first, rest_second), axis=1)
    gate_part, up_part, rest_sum, grad_mixed = stage(gate_part, up_part, rest_sum, grad_mixed)
    rest_all = gather_ctx(rest_sum)

    pair_first = scatter_first((gate_part, up_part))
    grad_merged = attention_backward(heads, slots, lows, kept, grad_mixed, tables, stream_starts)
    grad_merged, pair_first = stage(grad_merged, pair_first)

    pair_second = scatter_second((gate_part, up_part), pair_first)
    attn_part = matmul_tn(normed, grad_merged).astype(BF)
    pair_sum = jnp.concatenate(
        [p[:, :units] for p in scatter_last((gate_part, up_part), pair_first, pair_second)], axis=1
    )
    attn_part, pair_sum, grad_merged = stage(attn_part, pair_sum, grad_merged)
    pair_all = gather_ctx(pair_sum[None])

    attn_first = scatter_first(halves(attn_part))
    grad_part, terms = input_side(
        grad_gate, grad_up, grad_merged, hidden_all, gate_pieces, up_pieces, attn_pieces
    )
    merged_term = jnp.sum(grad_merged, axis=0, dtype=F32).reshape(3, pieces, 1, head_width)
    merged_term = jnp.where(
        lax.broadcasted_iota(jnp.int32, (3, pieces, parts, head_width), 2) == ctx_at, merged_term, 0.0
    )
    terms = jnp.concatenate([terms.reshape(-1), merged_term.reshape(-1)]).reshape(-1, 128)
    grad_part, terms, attn_first = stage(grad_part, terms, attn_first)

    attn_second = scatter_second(halves(attn_part), attn_first)
    attn_sum = jnp.concatenate(scatter_last(halves(attn_part), attn_first, attn_second), axis=1)
    attn_sum, grad_part, terms = stage(attn_sum, grad_part, terms)

    pair_plan = [
        [
            (c, side * units + p * unit_width, unit_width)
            for p in range(shard_count)
            for c in range(parts)
        ]
        for side in range(2)
    ]
    attn_plan = [
        [
            (c, (s * pieces + p) * head_width, head_width)
            for s in range(3)
            for p in range(pieces)
            for c in range(parts)
        ]
    ]
    places = parts // 2
    attn_got = gather_step(1, [attn_sum, attn_sum])
    attn_held, attn_other = [attn_sum[None]], []
    other_terms = others_of(terms, "fsdp", 1, shard_count)
    part_own, part_other = split_cores(grad_part)
    part_other = flip(part_other, "ctx", 0)
    part_places = (part_own.astype(F32) + part_other.astype(F32)).astype(BF)
    part_ends = [line_block(part_places, 1).astype(BF), line_block(part_places, places - 1).astype(BF)]
    float_in = hidden_in[0].astype(F32)
    output = (float_in + out_rows.astype(F32)).astype(BF)[None]
    (rest_all,) = tie([rest_all], [output])
    rest_blocks = rest_all.reshape(parts, -1, model)
    grad_down_w = rest_blocks[:, :unit_width].reshape(-1, model).astype(F32)
    if spread:
        grad_proj_w = rest_blocks[:, unit_width:].reshape(-1, model).astype(F32)
    else:
        grad_proj_w = lax.dynamic_slice_in_dim(
            gather_ctx(lax.psum(proj_part.astype(F32), "fsdp")), fsdp_at * shard_rows, shard_rows, 0
        )
    terms, others, part_places, part_ends, attn_got, output, grad_down_w, grad_proj_w = stage(
        terms, other_terms[0], part_places, part_ends, attn_got, output, grad_down_w, grad_proj_w
    )
    terms = sum_of(terms, others, other_terms[1])

    waiting = None
    grad_step = None
    for step in range(2, places):
        attn_held += [block[None] for block in attn_got]
        attn_before = attn_got
        attn_got = gather_step(step, attn_got)
        grad_step = line_step(part_places, step - 1, grad_step) if grad_step else line_start(part_ends)
        if waiting is not None:
            attn_other.append(flip(waiting, "ctx", 0))
        waiting = jnp.stack([attn_sum, *attn_before] if step == 2 else attn_before)
        other_terms = flip(terms, "ctx", 0) if step == 2 else terms
        late = []
        if step == 3:
            (pair_all,) = tie([pair_all], [grad_down_w])
            late = list(assemble(pair_all, pair_plan))
        grad_step, attn_got, attn_other, late, part_places, waiting, terms, other_terms = stage(
            grad_step, attn_got, attn_other, late, part_places, waiting, terms, other_terms
        )
        if step == 2:
            terms = terms + other_terms
        if step == 3:
            grad_gate_w, grad_up_w = late
    attn_held += [block[None] for block in attn_got]
    grad_step = line_step(part_places, places - 1, grad_step) if grad_step else line_start(part_ends)
    attn_other.append(flip(waiting, "ctx", 0))
    attn_last = [flip(block[None], "ctx", 0) for block in attn_got]
    sources = [(attn_held[0], 0), (attn_other[0], 0)]
    for step in range(1, places):
        sources += [(attn_held[2 * step - 1], 0), (attn_held[2 * step], 0)]
        first = 1 if step == 1 else 0
        if step < places - 1:
            sources += [(attn_other[step - 1], first), (attn_other[step - 1], first + 1)]
        else:
            sources += [(block, 0) for block in attn_last]
    grad_attn_w = assemble_line(sources, line_origins(), attn_plan[0])
    other_terms = others_of(terms, "ctx", 2, places)
    grad_attn_w, others, grad_step, part_places = stage(grad_attn_w, other_terms[0], grad_step, part_places)
    terms = sum_of(terms, others, other_terms[1])
    terms = terms.reshape(-1)
    grad_normed = line_block(part_places, 0) + grad_step[0].astype(F32) + grad_step[1].astype(F32)

    normal_hat, inverse_std = normalise(float_in)
    b_rows = b_qkv.shape[0]
    grad_b_attn = lax.dynamic_slice_in_dim(terms, 2 * model + fsdp_at * b_rows, b_rows, 0)
    grad_gain = lax.dynamic_slice_in_dim(terms, fsdp_at * shard_rows, shard_rows, 0)
    grad_bias = lax.dynamic_slice_in_dim(terms, model + fsdp_at * shard_rows, shard_rows, 0)

    grad_hat = grad_normed * gain_full
    grad_in = out_grad[0].astype(F32) + inverse_std * (
        grad_hat
        - jnp.mean(grad_hat, axis=1, keepdims=True)
        - normal_hat * jnp.mean(grad_hat * normal_hat, axis=1, keepdims=True)
    )
    grad_in = grad_in.astype(BF)[None]
    return (
        output,
        grad_in,
        grad_gain,
        grad_bias,
        grad_attn_w,
        grad_b_attn,
        grad_proj_w,
        grad_gate_w,
        grad_up_w,
        grad_down_w,
    )


def solution(mesh):
    return jax.shard_map(
        shards,
        mesh=mesh,
        in_specs=(
            P("fsdp", "ctx", None),
            P("fsdp", "ctx", None),
            P("fsdp", None),
            P("fsdp", None),
            P("fsdp"),
            P("fsdp"),
            P("fsdp", None),
            P("fsdp"),
            P("fsdp", None),
            P("fsdp", None),
            P("fsdp", None),
            P("fsdp", None),
        ),
        out_specs=(
            P("fsdp", "ctx", None),
            P("fsdp", "ctx", None),
            P("fsdp"),
            P("fsdp"),
            P("fsdp", None),
            P("fsdp"),
            P("fsdp", None),
            P("fsdp", None),
            P("fsdp", None),
            P("fsdp", None),
        ),
        check_vma=False,
    )
```
